256 devices in a mesh: ctx: 64 (over x, z, core), lat: 4 (over y).
Axes of the slice: x: 4, y: 4, z: 8, core: 2. Of those that a mesh axis runs over, the one named last changes fastest.
Arguments:
- token_ids: int32 [32768], P('ctx'), may hold values from 0 to 255
- latent_offset: int32 [1], replicated, may hold values from 31616 to 31744
- embed_table: bfloat16 [256, 2048], replicated, may hold values from -6 to 6
- cross_q: bfloat16 [2048, 2048], P('ctx', 'lat')
- cross_kv: bfloat16 [2, 2048, 2048], P(None, 'ctx', 'lat')
- cross_out: bfloat16 [2048, 2048], P('lat'), may hold values from -0.375 to 0.375
- self_qkv: bfloat16 [3, 2048, 2048], P(None, None, 'lat')
- self_out: bfloat16 [2048, 2048], P('lat'), may hold values from -0.25 to 0.25
- mlp_in: bfloat16 [2048, 8192], P(None, 'ctx'), may hold values from -0.125 to 0.125
- mlp_out: bfloat16 [8192, 2048], P('ctx'), may hold values from -0.0625 to 0.0625
Outputs:
- latent_out: bfloat16 [4, 256, 2048], P('lat', 'ctx')
The draws below stay inside these ranges and needn't reach their ends.
Inputs may be any that keep to these rules, and one draw needn't show every extreme that they name: `latent_offset`: the latent rows lie inside the context.
All inputs are finite; a program needn't handle non-finite values.
Results may differ from the reference program's by a relative error of at most 0.014.
Values may be sent and summed in bfloat16 or wider, within the bound.
A program may use at most 128 MiB of HBM per device.

```python
import math
import jax
import jax.numpy as jnp
import numpy as np
from jax import lax

D = 2048
H = 16
HD = 128
FF = 8192
VOCAB = 256
LATENTS = 1024
CTX_DEV = 512
CONTEXT = 32768
N_CTX = 64
N_LAT = 4


def query_key_pair(key, salt):
    own_query = jax.random.normal(jax.random.fold_in(key, salt + 2), (D, D), jnp.float32) / math.sqrt(D)
    own_key = jax.random.normal(jax.random.fold_in(key, salt + 3), (D, D), jnp.float32) / math.sqrt(D)
    return (own_query, own_key)


def draw_cross_q(key, part):
    return query_key_pair(key, 100)[0].astype(jnp.bfloat16)


def draw_cross_kv(key, part):
    key_part = query_key_pair(key, 100)[1]
    value_part = jax.random.normal(jax.random.fold_in(key, 150), (D, D), jnp.float32) / math.sqrt(D)
    return jnp.stack([key_part, value_part]).astype(jnp.bfloat16)


def draw_self_qkv(key, part):
    query_part, key_part = query_key_pair(key, 200)
    value_part = jax.random.normal(jax.random.fold_in(key, 250), (D, D), jnp.float32) / math.sqrt(D)
    return jnp.stack([query_part, key_part, value_part]).astype(jnp.bfloat16)


def set_ends(entries, rng, least, top_value):
    shape = entries.shape
    index_at = [jax.random.randint(jax.random.fold_in(rng, axis), (), 0, shape[axis]) for axis in range(len(shape))]
    entries = entries.at[tuple(index_at)].set(least)
    longest = shape.index(max(shape))
    index_at[longest] = (index_at[longest] + 1) % shape[longest]
    return entries.at[tuple(index_at)].set(top_value)


def block_levels(stream_key, shape, split, low, top_value):
    factor_of, own = 1.0, jax.random.fold_in(stream_key, 6)
    for position, blocks in split:
        steps = jnp.exp(jax.random.uniform(jax.random.fold_in(own, position), (blocks,), jnp.float32, low / len(split), top_value / len(split)))
        factor_of = factor_of * jnp.repeat(steps, shape[position] // blocks).reshape([-1 if axis == position else 1 for axis in range(len(shape))])
    return factor_of


def cumulative_ranks(number_of, lean):
    weights = [(1 << 20) // math.isqrt(rank ** lean) + 1 for rank in range(1, number_of + 1)]
    scale = 1 + sum(weights) // (1 << 30)
    return np.cumsum(np.array([max(1, weight // scale) for weight in weights]))


def ranked_ids(stream_key, extent, count, slope):
    table = cumulative_ranks(count, slope)
    ticket = jax.random.randint(jax.random.fold_in(stream_key, 1), extent, 0, int(table[count - 1]))
    standing = jnp.searchsorted(jnp.asarray(table, jnp.int32), ticket, side="right")
    return jax.random.permutation(jax.random.fold_in(stream_key, 2), count)[standing].astype(jnp.int32)


def normal_values(key, dims, deviation, limit, shards=(), held_as=jnp.bfloat16):
    factor_of = block_levels(key, dims, shards, -0.22, 0.18) if shards else 1.0
    values = jax.random.normal(key, dims, jnp.float32) * deviation * factor_of
    return jnp.minimum(jnp.maximum(values, -limit), limit).astype(held_as)


def setup_inputs(seed: int = 0) -> dict:
    splits = jax.random.split(jax.random.key(seed), 11)
    return {
        "token_ids": set_ends(ranked_ids(splits[0], (CONTEXT,), VOCAB, 2), jax.random.fold_in(splits[0], 3), 0, VOCAB - 1).astype(jnp.int32),
        "latent_offset": jax.random.randint(splits[1], (1,), CONTEXT - LATENTS - CTX_DEV // 4, CONTEXT - LATENTS + 1).astype(jnp.int32),
        "embed_table": normal_values(splits[2], (VOCAB, D), 1.0, 6.0),
        "cross_q": draw_cross_q(jax.random.fold_in(splits[10], 71), 0),
        "cross_kv": draw_cross_kv(jax.random.fold_in(splits[10], 71), 0),
        "cross_out": normal_values(splits[5], (D, D), (3.0 * D ** -0.5), 0.375, ((0, 4),)),
        "self_qkv": draw_self_qkv(jax.random.fold_in(splits[10], 71), 0),
        "self_out": normal_values(splits[7], (D, D), (2.0 * D ** -0.5), 0.25, ((0, 4),)),
        "mlp_in": normal_values(splits[8], (D, FF), D ** -0.5, 0.125, ((1, 64),)),
        "mlp_out": normal_values(splits[9], (FF, D), FF ** -0.5, 0.0625, ((0, 64),)),
    }


EPSILON = 1e-06
MASKED = -1e+30

def rms_normalize(values):
    return values * lax.rsqrt(lax.optimization_barrier(jnp.mean(values * values, axis=-1, keepdims=True)) + EPSILON)

def sinusoid(places, width):
    index = jnp.arange(width // 2).astype(jnp.float32)
    rates = jnp.exp(index * (-2.0 * math.log(10000.0) / width))
    angles = places.astype(jnp.float32)[:, None] * rates[None, :]
    return jnp.stack([jnp.sin(angles), jnp.cos(angles)], axis=-1).reshape(places.shape[0], width)

def reference(token_ids, latent_offset, embed_table, cross_q, cross_kv, cross_out, self_qkv, self_out, mlp_in, mlp_out):
    offset = latent_offset[0]
    scale = 1.0 / math.sqrt(HD)
    places = jnp.arange(CONTEXT, dtype=jnp.int32)
    looked = embed_table[token_ids].astype(jnp.float32)
    context = rms_normalize(looked + sinusoid(places, D)).astype(jnp.bfloat16)
    keys = jnp.dot(context, cross_kv[0], preferred_element_type=jnp.float32).astype(jnp.bfloat16)
    values = jnp.dot(context, cross_kv[1], preferred_element_type=jnp.float32).astype(jnp.bfloat16)
    latent = lax.dynamic_slice_in_dim(context, offset, LATENTS, 0)
    queries = jnp.dot(latent, cross_q, preferred_element_type=jnp.float32).astype(jnp.bfloat16)
    query_places = offset + jnp.arange(LATENTS, dtype=jnp.int32)
    blocked = places.reshape(N_CTX, CTX_DEV)[None, :, :] > query_places[:, None, None]

    def cross_head(head_index):
        query = lax.dynamic_slice_in_dim(queries, head_index * HD, HD, 1).astype(jnp.float32)
        key = lax.dynamic_slice_in_dim(keys, head_index * HD, HD, 1).astype(jnp.float32).reshape(N_CTX, CTX_DEV, HD)
        value = lax.dynamic_slice_in_dim(values, head_index * HD, HD, 1).astype(jnp.float32).reshape(N_CTX, CTX_DEV, HD)
        scores = jnp.einsum('ld,ncd->lnc', query, key) * scale
        scores = jnp.where(blocked, MASKED, scores)
        block_max = lax.optimization_barrier(jnp.max(scores, axis=2))
        weights = jnp.exp(scores - block_max[:, :, None]).astype(jnp.bfloat16)
        block_total = lax.optimization_barrier(jnp.sum(weights.astype(jnp.float32), axis=2))
        block_output = jnp.einsum('lnc,ncd->lnd', weights.astype(jnp.float32), value)
        row_max = lax.optimization_barrier(jnp.max(block_max, axis=1))
        factor = jnp.exp(block_max - row_max[:, None])
        total = lax.optimization_barrier(jnp.sum(block_total * factor, axis=1))
        merged = lax.optimization_barrier(jnp.sum(block_output * factor[:, :, None], axis=1))
        return merged / total[:, None]
    heads_out = lax.map(cross_head, jnp.arange(H, dtype=jnp.int32))
    cross_attended = jnp.transpose(heads_out, (1, 0, 2)).reshape(LATENTS, D).astype(jnp.bfloat16)
    first_stream = latent.astype(jnp.float32) + jnp.dot(cross_attended, cross_out, preferred_element_type=jnp.float32)
    self_normed = rms_normalize(first_stream).astype(jnp.bfloat16)
    self_queries = jnp.dot(self_normed, self_qkv[0], preferred_element_type=jnp.float32).astype(jnp.bfloat16)
    self_keys = jnp.dot(self_normed, self_qkv[1], preferred_element_type=jnp.float32).astype(jnp.bfloat16)
    self_values = jnp.dot(self_normed, self_qkv[2], preferred_element_type=jnp.float32).astype(jnp.bfloat16)
    rows = jnp.arange(LATENTS, dtype=jnp.int32)
    later = rows[None, :] > rows[:, None]

    def self_head(head_index):
        query = lax.dynamic_slice_in_dim(self_queries, head_index * HD, HD, 1).astype(jnp.float32)
        key = lax.dynamic_slice_in_dim(self_keys, head_index * HD, HD, 1).astype(jnp.float32)
        value = lax.dynamic_slice_in_dim(self_values, head_index * HD, HD, 1).astype(jnp.float32)
        scores = jnp.einsum('id,jd->ij', query, key) * scale
        scores = jnp.where(later, MASKED, scores)
        peak = lax.optimization_barrier(jnp.max(scores, axis=1))
        weights = jnp.exp(scores - peak[:, None]).astype(jnp.bfloat16)
        total = lax.optimization_barrier(jnp.sum(weights.astype(jnp.float32), axis=1))
        return jnp.einsum('ij,jd->id', weights.astype(jnp.float32), value) / total[:, None]
    self_out_heads = lax.map(self_head, jnp.arange(H, dtype=jnp.int32))
    self_attended = jnp.transpose(self_out_heads, (1, 0, 2)).reshape(LATENTS, D).astype(jnp.bfloat16)
    second_stream = first_stream + jnp.dot(self_attended, self_out, preferred_element_type=jnp.float32)
    mlp_normed = rms_normalize(second_stream).astype(jnp.bfloat16)
    pre_hidden = jnp.dot(mlp_normed, mlp_in, preferred_element_type=jnp.float32)
    mlp_hidden = jax.nn.gelu(pre_hidden, approximate=True).astype(jnp.bfloat16)
    final = second_stream + jnp.dot(mlp_hidden, mlp_out, preferred_element_type=jnp.float32)
    return final.astype(jnp.bfloat16).reshape(N_LAT, LATENTS // N_LAT, D)
```

```python
import math

import jax
import jax.numpy as jnp
from jax import lax
from jax.experimental import pallas as pl
from jax.experimental.pallas import tpu as pltpu
from jax.sharding import PartitionSpec as P

MESH = pl.DeviceIdType.MESH
HD = 128
D = 2048
LATENTS = 1024
EPSILON = 1e-06
MASKED = -1e30
SCALE = 1.0 / math.sqrt(HD)
BF = jnp.bfloat16
F32 = jnp.float32
VLIMIT = 56 * 1024 * 1024


def place():
    g = lax.axis_index("ctx")
    y = lax.axis_index("lat")
    return g // 16, (g // 4) % 4, (g // 2) % 2, g % 2, y


def at(x, a, b, c, y):
    return (16 * x + 4 * a + 2 * b + c, y)


def push(src, dst, send_sem, recv_sem, device):
    copy = pltpu.make_async_remote_copy(
        src_ref=src,
        dst_ref=dst,
        send_sem=send_sem,
        recv_sem=recv_sem,
        device_id=device,
        device_id_type=MESH,
    )
    return copy


def arrive(dst, recv_sem, device):
    push(dst, dst, recv_sem, recv_sem, device).wait_recv()


def greet(devices):
    barrier = pltpu.get_barrier_semaphore()
    for device in devices:
        pl.semaphore_signal(barrier, inc=1, device_id=device, device_id_type=MESH)
    pl.semaphore_wait(barrier, len(devices))


def each(first, last, body):
    def step(k, carry):
        body(k)
        return carry

    lax.fori_loop(first, last, step, 0)


class Exchange:
    def __init__(self, src, dst, send, recv, me, device_of, n, whole=False):
        self.src, self.dst, self.send, self.recv = src, dst, send, recv
        self.me, self.device_of, self.n, self.whole = me, device_of, n, whole

    def copy(self, j):
        src = self.src if self.whole else self.src.at[j]
        return push(src, self.dst.at[self.me], self.send.at[j], self.recv.at[self.me], self.device_of(j))

    def start(self):
        def one(k):
            self.copy((self.me + k) % self.n).start()

        each(1, self.n, one)
        self.dst[self.me] = self.src[...] if self.whole else self.src[self.me]

    def wait_all(self):
        def one(k):
            j = (self.me + self.n - k) % self.n
            arrive(self.dst.at[j], self.recv.at[j], self.device_of(j))

        each(1, self.n, one)

    def wait_sent(self):
        def one(k):
            self.copy((self.me + k) % self.n).wait_send()

        each(1, self.n, one)


def rms_rows(values):
    return values * lax.rsqrt(jnp.mean(values * values, axis=-1, keepdims=True) + EPSILON)


def gather_kernel(q_ref, kv_ref, tok_ref, w_ref, t_ref, stage, s1, r1, s2, r2, s3, r3):
    x, a, b, c, y = place()
    k = 2 * b + c
    j_me = 2 * x + b
    partner = at(x, a, b, 1 - c, y)
    heads = [((a + d) % 4) for d in range(1, 4)]
    rows = [((x + dx) % 4, (b + db) % 2) for dx in (0, 1, 3, 2) for db in (0, 1) if dx or db]
    greet([at(x, h, b, c, y) for h in heads] + [at(rx, a, rb, c, y) for rx, rb in rows] + [partner])
    for h in range(4):
        stage[h, 0] = q_ref[:, 128 * h : 128 * h + 128]
        stage[h, 1] = kv_ref[0, :, 128 * h : 128 * h + 128]
        stage[h, 2] = kv_ref[1, :, 128 * h : 128 * h + 128]
    first = []
    for h in heads:
        there = at(x, h, b, c, y)
        first.append(push(tok_ref, t_ref.at[x, a, k], s1.at[1, h], r1.at[1, a], there))
        first.append(push(stage.at[h], w_ref.at[:, x, a, k], s1.at[0, h], r1.at[0, a], there))
    for copy in first:
        copy.start()
    t_ref[x, a, k] = tok_ref[...]
    w_ref[0, x, a, k] = stage[a, 0]
    w_ref[1, x, a, k] = stage[a, 1]
    w_ref[2, x, a, k] = stage[a, 2]
    for h in heads:
        arrive(t_ref.at[x, h, k], r1.at[1, h], partner)
        arrive(w_ref.at[:, x, h, k], r1.at[0, h], partner)
    second = []
    for rx, rb in rows:
        there = at(rx, a, rb, c, y)
        j = 2 * rx + rb
        second.append(push(t_ref.at[x, :, k], t_ref.at[x, :, k], s2.at[1, j], r2.at[1, j_me], there))
        second.append(push(w_ref.at[:, x, :, k], w_ref.at[:, x, :, k], s2.at[0, j], r2.at[0, j_me], there))
    for copy in second:
        copy.start()

    def onward(rx, rb):
        j = 2 * rx + rb
        k2 = 2 * rb + c
        return [
            push(t_ref.at[rx, :, k2], t_ref.at[rx, :, k2], s3.at[1, j], r3.at[1, j], partner),
            push(w_ref.at[:, rx, :, k2], w_ref.at[:, rx, :, k2], s3.at[0, j], r3.at[0, j], partner),
        ]

    third = onward(x, b)
    for copy in third:
        copy.start()
    for rx, rb in rows:
        sx, sb = (2 * x + 4 - rx) % 4, rb
        j = 2 * sx + sb
        k2 = 2 * sb + c
        arrive(t_ref.at[sx, :, k2], r2.at[1, j], partner)
        arrive(w_ref.at[:, sx, :, k2], r2.at[0, j], partner)
        more = onward(sx, sb)
        for copy in more:
            copy.start()
        third += more
    for rx, rb in [(x, b)] + rows:
        j = 2 * rx + rb
        k3 = 2 * rb + 1 - c
        arrive(t_ref.at[rx, :, k3], r3.at[1, j], partner)
        arrive(w_ref.at[:, rx, :, k3], r3.at[0, j], partner)
    for copy in first + second + third:
        copy.wait_send()


def gathered(cross_q, cross_kv, token_rows):
    dma = pltpu.SemaphoreType.DMA
    return pl.pallas_call(
        gather_kernel,
        out_shape=(
            jax.ShapeDtypeStruct((3, 4, 4, 4, 32, HD), BF),
            jax.ShapeDtypeStruct((4, 4, 4, 8, 128), jnp.int32),
        ),
        in_specs=[pl.BlockSpec(memory_space=pltpu.VMEM)] * 3,
        out_specs=(pl.BlockSpec(memory_space=pltpu.VMEM),) * 2,
        scratch_shapes=[
            pltpu.VMEM((4, 3, 32, HD), BF),
            dma((2, 4)),
            dma((2, 4)),
            dma((2, 8)),
            dma((2, 8)),
            dma((2, 8)),
            dma((2, 8)),
        ],
        compiler_params=pltpu.CompilerParams(
            collective_id=0, has_side_effects=True, vmem_limit_bytes=VLIMIT
        ),
    )(cross_q, cross_kv, token_rows)


def cross_kernel(
    offset_ref, tok_ref, kpos_ref, table_ref, base_ref, mid_ref, low_ref, w_ref,
    o_ref, st_ref, lat_ref,
    wkv, rows_sin, rows_cos, looked, block, keys, values, queries,
):
    wkv[:, :HD] = w_ref[1]
    wkv[:, HD:] = w_ref[2]
    vocab = lax.broadcasted_iota(jnp.int32, (128, 256), 1)

    def embed(n):
        s, c = base_ref[0, pl.ds(n, 1)], base_ref[1, pl.ds(n, 1)]
        rows_sin[...] = s * mid_ref[1] + c * mid_ref[0]
        rows_cos[...] = c * mid_ref[1] - s * mid_ref[0]

        def quarter(part):
            at_row = pl.multiple_of(n * 512 + part * 128, 128)
            one_hot = (tok_ref[pl.ds(at_row, 128), :] == vocab).astype(BF)
            looked[...] = jnp.dot(one_hot, table_ref[...], preferred_element_type=F32)

            def sixteen(g):
                m = part * 8 + g
                row = pl.multiple_of(g * 16, 16)
                values_here = (
                    looked[pl.ds(row, 16), :]
                    + rows_sin[pl.ds(m, 1), :] * low_ref[1]
                    + rows_cos[pl.ds(m, 1), :] * low_ref[0]
                )
                out_row = pl.multiple_of(part * 128 + g * 16, 16)
                block[pl.ds(out_row, 16), :] = rms_rows(values_here).astype(BF)

            each(0, 8, sixteen)

        each(0, 4, quarter)

    def context_run(n):
        embed(n)
        both = jnp.dot(block[...], wkv[...], preferred_element_type=F32).astype(BF)
        row = pl.multiple_of(n * 512, 512)
        keys[pl.ds(row, 512), :] = both[:, :HD]
        values[pl.ds(row, 512), :] = both[:, HD:]

    each(0, 4, context_run)

    def latent_run(n):
        embed(4 + n)
        row = pl.multiple_of(n * 512, 512)
        lat_ref[pl.ds(row, 512), :] = block[...]
        queries[pl.ds(row, 512), :] = jnp.dot(block[...], w_ref[0], preferred_element_type=F32).astype(BF)

    each(0, 2, latent_run)

    def attend(t, carry):
        maxima, totals = carry
        row = pl.multiple_of(t * 256, 256)
        scores = lax.dot_general(
            queries[pl.ds(row, 256), :], keys[...], (((1,), (1,)), ((), ())), preferred_element_type=F32
        )
        scores = scores * SCALE
        qpos = offset_ref[0] + t * 256 + lax.broadcasted_iota(jnp.int32, (256, 1), 0)
        scores = jnp.where(kpos_ref[...] > qpos, MASKED, scores)
        peak = jnp.max(scores, axis=1, keepdims=True)
        weights = jnp.exp(scores - peak).astype(BF)
        total = jnp.sum(weights.astype(F32), axis=1, keepdims=True)
        out = jnp.dot(weights, values[...], preferred_element_type=F32).astype(BF)
        o_ref[:, t] = out.reshape(16, 16, HD)
        lane = lax.broadcasted_iota(jnp.int32, (16, 16, 128), 2)
        sub = lax.broadcasted_iota(jnp.int32, (16, 16, 128), 1)
        mine = lane == sub + 16 * t
        maxima = maxima + jnp.sum(jnp.where(mine, peak.reshape(16, 16, 1), 0.0), axis=1)
        totals = totals + jnp.sum(jnp.where(mine, total.reshape(16, 16, 1), 0.0), axis=1)
        return maxima, totals

    zero = jnp.zeros((16, 128), F32)
    maxima, totals = lax.fori_loop(0, 4, attend, (zero, zero))
    for r in range(16):
        st_ref[r, 0:1, :] = maxima[r : r + 1]
        st_ref[r, 1:2, :] = totals[r : r + 1]


def crossed(offset, tokens, kpos, table, base, mid, low, weights):
    vmem = pl.BlockSpec(memory_space=pltpu.VMEM)
    return pl.pallas_call(
        cross_kernel,
        out_shape=(
            jax.ShapeDtypeStruct((16, 4, 16, HD), BF),
            jax.ShapeDtypeStruct((16, 8, 128), F32),
            jax.ShapeDtypeStruct((LATENTS, D), BF),
        ),
        in_specs=[pl.BlockSpec(memory_space=pltpu.SMEM)] + [vmem] * 7,
        out_specs=(vmem,) * 3,
        scratch_shapes=[
            pltpu.VMEM((D, 2 * HD), BF),
            pltpu.VMEM((32, D), F32),
            pltpu.VMEM((32, D), F32),
            pltpu.VMEM((128, D), F32),
            pltpu.VMEM((512, D), BF),
            pltpu.VMEM((2048, HD), BF),
            pltpu.VMEM((2048, HD), BF),
            pltpu.VMEM((LATENTS, HD), BF),
        ],
        compiler_params=pltpu.CompilerParams(vmem_limit_bytes=VLIMIT),
    )(offset, tokens, kpos, table, base, mid, low, weights)


def middle_kernel(
    o_ref, st_ref, lat_ref, cout_ref, sqkv_ref, sout_ref,
    second_ref,
    ro, rst, w_co, w_qkv, w_so, msg, came, own, all_rows, normed, kv, kv_all, msg2, came2,
    load, s_o, r_o, s_st, r_st, s_m, r_m, s_a, r_a, s_kv, r_kv, s_m2, r_m2,
):
    x, a, b, c, y = place()
    r = 4 * x + 2 * b + c
    p = 4 * y + a
    row_of = lambda j: at(j // 4, a, (j // 2) % 2, j % 2, y)
    head_of = lambda j: at(x, j % 4, b, c, j // 4)
    row_at = pl.multiple_of(a * HD, HD)
    loads = [
        pltpu.make_async_copy(cout_ref.at[pl.ds(row_at, HD), :], w_co, load.at[0]),
        pltpu.make_async_copy(sqkv_ref.at[:, :, pl.ds(row_at, HD)], w_qkv, load.at[1]),
        pltpu.make_async_copy(sout_ref.at[pl.ds(row_at, HD), :], w_so, load.at[2]),
    ]
    for copy in loads:
        copy.start()
    greet([row_of((r + k) % 16) for k in range(1, 16)] + [head_of((p + k) % 16) for k in range(1, 16)])
    outs = Exchange(o_ref, ro, s_o, r_o, r, row_of, 16)
    stats = Exchange(st_ref, rst, s_st, r_st, r, row_of, 16)
    stats.start()
    outs.start()
    stats.wait_all()
    outs.wait_all()
    maxima, totals = rst[:, 0, :], rst[:, 1, :]
    factor = jnp.exp(maxima - jnp.max(maxima, axis=0, keepdims=True))
    factor = factor / jnp.sum(factor * totals, axis=0, keepdims=True)
    diagonal = lax.broadcasted_iota(jnp.int32, (64, 128), 0) == lax.broadcasted_iota(jnp.int32, (64, 128), 1)
    attended = jnp.zeros((64, HD), F32)
    for j in range(16):
        column = jnp.sum(jnp.where(diagonal, factor[j : j + 1, :], 0.0), axis=1, keepdims=True)
        attended = attended + column * ro[j].astype(F32)
    loads[0].wait()
    loads[1].wait()
    loads[2].wait()

    def shares(rows, weight, out):
        for q in range(4):
            part = jnp.dot(rows, weight[:, 512 * q : 512 * q + 512], preferred_element_type=F32).astype(BF)
            for t in range(4):
                out[4 * t + q] = part[16 * t : 16 * t + 16]

    shares(attended.astype(BF), w_co, msg)
    summed = Exchange(msg, came, s_m, r_m, p, head_of, 16)
    summed.start()
    summed.wait_all()
    first = jnp.sum(came[...].astype(F32), axis=0) + lat_ref[...].astype(F32)
    own[...] = first.astype(BF)
    spread = Exchange(own, all_rows, s_a, r_a, p, head_of, 16, whole=True)
    spread.start()
    spread.wait_all()
    for t in range(4):
        rows = jnp.concatenate([all_rows[4 * t + q] for q in range(4)], axis=1).astype(F32)
        normed[16 * t : 16 * t + 16, :] = rms_rows(rows).astype(BF)
    query = jnp.dot(normed[...], w_qkv[0], preferred_element_type=F32).astype(BF)
    kv[:, :HD] = jnp.dot(normed[...], w_qkv[1], preferred_element_type=F32).astype(BF)
    kv[:, HD:] = jnp.dot(normed[...], w_qkv[2], preferred_element_type=F32).astype(BF)
    both = Exchange(kv, kv_all, s_kv, r_kv, r, row_of, 16, whole=True)
    both.start()
    both.wait_all()
    keys = kv_all[:, :, :HD].reshape(LATENTS, HD)
    values = kv_all[:, :, HD:].reshape(LATENTS, HD)
    scores = lax.dot_general(query, keys, (((1,), (1,)), ((), ())), preferred_element_type=F32) * SCALE
    row = lax.broadcasted_iota(jnp.int32, (64, 1), 0)
    col = lax.broadcasted_iota(jnp.int32, (1, LATENTS), 1)
    row_place = (row // 16) * 256 + 16 * r + row % 16
    col_place = ((col // 16) % 4) * 256 + 16 * (col // 64) + col % 16
    scores = jnp.where(col_place > row_place, MASKED, scores)
    weights = jnp.exp(scores - jnp.max(scores, axis=1, keepdims=True)).astype(BF)
    total = jnp.sum(weights.astype(F32), axis=1, keepdims=True)
    attended = jnp.dot(weights, values, preferred_element_type=F32) / total
    shares(attended.astype(BF), w_so, msg2)
    summed2 = Exchange(msg2, came2, s_m2, r_m2, p, head_of, 16)
    summed2.start()
    summed2.wait_all()
    second_ref[...] = first + jnp.sum(came2[...].astype(F32), axis=0)
    for exchange in (outs, stats, summed, spread, both, summed2):
        exchange.wait_sent()


def middle(outs, stats, latent, cross_out, self_qkv, self_out):
    vmem = pl.BlockSpec(memory_space=pltpu.VMEM)
    hbm = pl.BlockSpec(memory_space=pl.ANY)
    dma = pltpu.SemaphoreType.DMA
    return pl.pallas_call(
        middle_kernel,
        out_shape=jax.ShapeDtypeStruct((16, 512), F32),
        in_specs=[vmem] * 3 + [hbm] * 3,
        out_specs=vmem,
        scratch_shapes=[
            pltpu.VMEM((16, 64, HD), BF),
            pltpu.VMEM((16, 8, 128), F32),
            pltpu.VMEM((HD, D), BF),
            pltpu.VMEM((3, D, HD), BF),
            pltpu.VMEM((HD, D), BF),
            pltpu.VMEM((16, 16, 512), BF),
            pltpu.VMEM((16, 16, 512), BF),
            pltpu.VMEM((16, 512), BF),
            pltpu.VMEM((16, 16, 512), BF),
            pltpu.VMEM((64, D), BF),
            pltpu.VMEM((64, 2 * HD), BF),
            pltpu.VMEM((16, 64, 2 * HD), BF),
            pltpu.VMEM((16, 16, 512), BF),
            pltpu.VMEM((16, 16, 512), BF),
            dma((3,)),
        ]
        + [dma((16,))] * 12,
        compiler_params=pltpu.CompilerParams(
            collective_id=1, has_side_effects=True, vmem_limit_bytes=VLIMIT
        ),
    )(outs, stats, latent, cross_out, self_qkv, self_out)


def mlp_kernel(
    second_ref, in_ref, mout_ref,
    out_ref,
    own, group, all_rows, normed, partial, halves, half_in, msg, came, last, came_last,
    s_h, r_h, s_r, r_r, s_p, r_p, s_x, r_x, s_m, r_m, s_l, r_l,
):
    x, a, b, c, y = place()
    r = 4 * x + 2 * b + c
    partner = at(x, a, b, 1 - c, y)
    j_me = 2 * x + b
    f = 4 * x + a
    k_me = 2 * b + c
    head_of = lambda j: at(x, j, b, c, y)
    rows = [((x + dx) % 4, (b + db) % 2) for dx in (0, 1, 3, 2) for db in (0, 1) if dx or db]
    final_of = lambda j: at(j // 4, j % 4, b, c, y)
    quad_of = lambda j: at(x, a, j // 2, j % 2, y)
    greet(
        [head_of((a + d) % 4) for d in range(1, 4)]
        + [at(rx, a, rb, c, y) for rx, rb in rows]
        + [final_of((f + k) % 16) for k in range(1, 16)]
        + [quad_of((k_me + k) % 4) for k in range(1, 4)]
    )
    own[...] = second_ref[...].astype(BF)
    heads = Exchange(own, group, s_h, r_h, a, head_of, 4, whole=True)
    heads.start()
    heads.wait_all()
    second = []
    for rx, rb in rows:
        second.append(push(group, all_rows.at[r], s_r.at[2 * rx + rb], r_r.at[j_me], at(rx, a, rb, c, y)))
    for copy in second:
        copy.start()
    all_rows[r] = group[...]
    onward = [push(group, all_rows.at[r], s_p.at[j_me], r_p.at[j_me], partner)]
    onward[0].start()
    for rx, rb in rows:
        sx, sb = (2 * x + 4 - rx) % 4, rb
        j = 2 * sx + sb
        slot = all_rows.at[4 * sx + 2 * sb + c]
        arrive(slot, r_r.at[j], partner)
        copy = push(slot, slot, s_p.at[j], r_p.at[j], partner)
        copy.start()
        onward.append(copy)
    for rx, rb in [(x, b)] + rows:
        arrive(all_rows.at[4 * rx + 2 * rb + 1 - c], r_p.at[2 * rx + rb], partner)
    def norm_one(t):
        wide = jnp.concatenate([all_rows[t, q] for q in range(4)], axis=1).astype(F32)
        normed[pl.ds(pl.multiple_of(t * 16, 16), 16), :] = rms_rows(wide).astype(BF)

    each(0, 16, norm_one)
    pre = jnp.dot(normed[...], in_ref[...], preferred_element_type=F32)
    hidden = jax.nn.gelu(pre, approximate=True).astype(BF)
    for q in range(4):
        partial[:, 512 * q : 512 * q + 512] = jnp.dot(
            hidden, mout_ref[:, 512 * q : 512 * q + 512], preferred_element_type=F32
        )
    here = (pl.ds(pl.multiple_of(r * 16, 16), 16), pl.ds(pl.multiple_of(a * 512, 512), 512))
    partial[here] = partial[here] + second_ref[...]
    other_cols = pl.ds(pl.multiple_of((1 - c) * 1024, 1024), 1024)
    own_cols = pl.ds(pl.multiple_of(c * 1024, 1024), 1024)
    halves[...] = partial[:, other_cols].astype(BF)
    swap = push(halves, half_in, s_x.at[0], r_x.at[0], partner)
    swap.start()
    swap.wait_recv()
    msg[...] = (partial[:, own_cols] + half_in[...].astype(F32)).astype(BF).reshape(16, 16, 1024)
    summed = Exchange(msg, came, s_m, r_m, f, final_of, 16)
    summed.start()
    summed.wait_all()
    last[...] = jnp.sum(came[...].astype(F32), axis=0).astype(BF)
    ends = Exchange(last, came_last, s_l, r_l, k_me, quad_of, 4, whole=True)
    ends.start()
    ends.wait_all()
    for h in range(2):
        both = came_last[h].astype(F32) + came_last[2 + h].astype(F32)
        chosen = jnp.zeros((4, 1024), F32)
        for k in range(4):
            chosen = chosen + jnp.where(k_me == k, both[4 * k : 4 * k + 4], 0.0)
        out_ref[:, 1024 * h : 1024 * h + 1024] = chosen
    for copy in second + onward + [swap]:
        copy.wait_send()
    for exchange in (heads, summed, ends):
        exchange.wait_sent()


def fed_forward(second, mlp_in, mlp_out):
    vmem = pl.BlockSpec(memory_space=pltpu.VMEM)
    dma = pltpu.SemaphoreType.DMA
    return pl.pallas_call(
        mlp_kernel,
        out_shape=jax.ShapeDtypeStruct((4, D), F32),
        in_specs=[vmem] * 3,
        out_specs=vmem,
        scratch_shapes=[
            pltpu.VMEM((16, 512), BF),
            pltpu.VMEM((4, 16, 512), BF),
            pltpu.VMEM((16, 4, 16, 512), BF),
            pltpu.VMEM((256, D), BF),
            pltpu.VMEM((256, D), F32),
            pltpu.VMEM((256, 1024), BF),
            pltpu.VMEM((256, 1024), BF),
            pltpu.VMEM((16, 16, 1024), BF),
            pltpu.VMEM((16, 16, 1024), BF),
            pltpu.VMEM((16, 1024), BF),
            pltpu.VMEM((4, 16, 1024), BF),
            dma((4,)),
            dma((4,)),
            dma((8,)),
            dma((8,)),
            dma((8,)),
            dma((8,)),
            dma((1,)),
            dma((1,)),
            dma((16,)),
            dma((16,)),
            dma((4,)),
            dma((4,)),
        ],
        compiler_params=pltpu.CompilerParams(
            collective_id=2, has_side_effects=True, vmem_limit_bytes=VLIMIT
        ),
    )(second, mlp_in, mlp_out)


def per_device(
    token_ids,
    latent_offset,
    embed_table,
    cross_q,
    cross_kv,
    cross_out,
    self_qkv,
    self_out,
    mlp_in,
    mlp_out,
):
    x, a, b, c, y = place()
    r = 4 * x + 2 * b + c
    offset = latent_offset[0]
    feature = jnp.arange(D, dtype=jnp.int32)
    rates = jnp.exp((feature // 2).astype(F32) * (-2.0 * math.log(10000.0) / D))
    block_starts = 512 * (16 * x + 4 * jnp.arange(4, dtype=jnp.int32) + 2 * b + c)
    starts = jnp.concatenate([block_starts, jnp.stack([offset, offset + 512, offset, offset])])
    places = jnp.concatenate([starts, 16 * jnp.arange(32, dtype=jnp.int32), jnp.arange(16, dtype=jnp.int32)])
    angles = places.astype(F32)[:, None] * rates[None, :]
    sines, cosines = jnp.sin(angles), jnp.cos(angles)
    odd = (feature % 2 == 1)[None, :]
    base = jnp.stack([jnp.where(odd, cosines[:8], sines[:8]), jnp.where(odd, -sines[:8], cosines[:8])])
    mid = jnp.stack([sines[8:40], cosines[8:40]])
    low = jnp.stack([sines[40:], cosines[40:]])

    token_rows = jnp.pad(token_ids.reshape(4, 128), ((0, 4), (0, 0)))
    weights, tokens = gathered(cross_q, cross_kv, token_rows)
    tokens = tokens[:, :, :, :4].reshape(64, 512)
    mine = lax.dynamic_index_in_dim(tokens.reshape(4, 4, 4, 512), x, 0, keepdims=False)
    mine = lax.dynamic_index_in_dim(mine, 2 * b + c, 1, keepdims=False).reshape(2048)
    latent_tokens = lax.dynamic_slice_in_dim(tokens.reshape(-1), offset, LATENTS, 0)
    column = jnp.concatenate([mine, latent_tokens])[:, None]
    kpos = (block_starts[:, None] + jnp.arange(512, dtype=jnp.int32)[None, :]).reshape(1, 2048)
    outs, stats, latent = crossed(
        latent_offset, column, kpos, embed_table, base, mid, low, weights.reshape(3, D, HD)
    )
    own_latent = lax.dynamic_slice(latent, (y * 256 + r * 16, a * 512), (16, 512))
    second = middle(outs.reshape(16, 64, HD), stats, own_latent, cross_out, self_qkv, self_out)
    return fed_forward(second, mlp_in, mlp_out).astype(BF)[None]


def solution(mesh):
    placed = (
        P("ctx"),
        P(),
        P(),
        P("ctx", "lat"),
        P(None, "ctx", "lat"),
        P("lat", None),
        P(None, None, "lat"),
        P("lat", None),
        P(None, "ctx"),
        P("ctx", None),
    )
    return jax.shard_map(
        per_device, mesh=mesh, in_specs=placed, out_specs=P("lat", "ctx", None), check_vma=False
    )
```

```python
import math

import jax
import jax.numpy as jnp
from jax import lax
from jax.experimental import pallas as pl
from jax.experimental.pallas import tpu as pltpu
from jax.sharding import PartitionSpec as P

MESH = pl.DeviceIdType.MESH
HD = 128
D = 2048
LATENTS = 1024
EPSILON = 1e-06
MASKED = -1e30
SCALE = 1.0 / math.sqrt(HD)
BF = jnp.bfloat16
F32 = jnp.float32
VLIMIT = 58 * 1024 * 1024


def place():
    g = lax.axis_index("ctx")
    y = lax.axis_index("lat")
    return g // 16, (g // 4) % 4, (g // 2) % 2, g % 2, y


def at(x, a, b, c, y):
    return (16 * x + 4 * a + 2 * b + c, y)


def push(src, dst, send_sem, recv_sem, device):
    copy = pltpu.make_async_remote_copy(
        src_ref=src,
        dst_ref=dst,
        send_sem=send_sem,
        recv_sem=recv_sem,
        device_id=device,
        device_id_type=MESH,
    )
    return copy


def arrive(dst, recv_sem, device):
    push(dst, dst, recv_sem, recv_sem, device).wait_recv()


def each(first, last, body):
    def step(k, carry):
        body(k)
        return carry

    lax.fori_loop(first, last, step, 0)


class Exchange:
    def __init__(self, src, dst, send, recv, me, device_of, n, whole=False):
        self.src, self.dst, self.send, self.recv = src, dst, send, recv
        self.me, self.device_of, self.n, self.whole = me, device_of, n, whole

    def copy(self, j):
        src = self.src if self.whole else self.src.at[j]
        return push(src, self.dst.at[self.me], self.send.at[j], self.recv.at[self.me], self.device_of(j))

    def start(self):
        def one(k):
            self.copy((self.me + k) % self.n).start()

        each(1, self.n, one)
        self.dst[self.me] = self.src[...] if self.whole else self.src[self.me]

    def wait_all(self):
        def one(k):
            j = (self.me + self.n - k) % self.n
            arrive(self.dst.at[j], self.recv.at[j], self.device_of(j))

        each(1, self.n, one)

    def wait_sent(self):
        def one(k):
            self.copy((self.me + k) % self.n).wait_send()

        each(1, self.n, one)


def rms_rows(values):
    return values * lax.rsqrt(jnp.mean(values * values, axis=-1, keepdims=True) + EPSILON)


def whole_kernel(
    offset_ref, sin_ref, cos_ref, tok_ref, table_ref, q_ref, kv_ref,
    cout_ref, sqkv_ref, sout_ref, in_ref, mout_ref,
    out_ref,
    stage, w_all, tokens, wkv, tw, rows_sin, rows_cos, waves, one_hot, inverse, latent, keys, values, q_own, q_all,
    o_msg, o_came, st_msg, st_came, w_co, w_qkv, w_so, msg, came, own, all_rows, normed, kv, kv_all, msg2, came2,
    own2, all_rows2, w_in, w_out, partial, msg3, came3,
    load, s1, r1, s2, r2, s3, r3, s_q, r_q, s_o, r_o, s_st, r_st, s_m, r_m, s_a, r_a, s_kv, r_kv, s_m2, r_m2,
    s_a2, r_a2, s_m3, r_m3, own_w, sw1, rw1, sw2, rw2, sw3, rw3,
):
    x, a, b, c, y = place()
    k = 2 * b + c
    r = 4 * x + k
    p = 4 * y + a
    j_me = 2 * x + b
    partner = at(x, a, b, 1 - c, y)

    def row_of(j):
        return at(j // 4, a, (j // 2) % 2, j % 2, y)

    def head_of(j):
        return at(x, j % 4, b, c, j // 4)

    def final_of(j):
        return at(x, k, (j // 2) % 2, j % 2, j // 4)

    def sender_of(j):
        return at(x, j % 4, a // 2, a % 2, j // 4)

    final_self = jnp.where(a == k, 4 * y + k, 16)
    sender_self = jnp.where(a == k, p, 16)

    row_at = pl.multiple_of(a * HD, HD)
    loads = [
        pltpu.make_async_copy(cout_ref.at[pl.ds(row_at, HD), :], w_co, load.at[0]),
        pltpu.make_async_copy(sqkv_ref.at[:, :, pl.ds(row_at, HD)], w_qkv, load.at[1]),
        pltpu.make_async_copy(sout_ref.at[pl.ds(row_at, HD), :], w_so, load.at[2]),
    ]
    for copy in loads:
        copy.start()
    barrier = pltpu.get_barrier_semaphore()

    def hello(device):
        pl.semaphore_signal(barrier, inc=1, device_id=device, device_id_type=MESH)

    each(1, 16, lambda i: hello(row_of((r + i) % 16)))
    each(1, 16, lambda i: hello(head_of((p + i) % 16)))

    def hello_sender(j):
        @pl.when(j != sender_self)
        def _():
            hello(sender_of(j))

    each(0, 16, hello_sender)
    for h in range(4):
        stage[h, 0] = q_ref[:, 128 * h : 128 * h + 128]
        stage[h, 1] = kv_ref[0, :, 128 * h : 128 * h + 128]
        stage[h, 2] = kv_ref[1, :, 128 * h : 128 * h + 128]
    pl.semaphore_wait(barrier, jnp.where(a == k, 45, 46))

    heads = [(a + d) % 4 for d in range(1, 4)]
    rows = [((x + dx) % 4, (b + db) % 2) for dx in (0, 1, 3, 2) for db in (0, 1) if dx or db]
    first_copies = []
    for h in heads:
        there = at(x, h, b, c, y)
        first_copies.append(push(tok_ref, tokens.at[x, a, k], s1.at[1, h], r1.at[1, a], there))
        first_copies.append(push(stage.at[h], w_all.at[:, x, a, k], s1.at[0, h], r1.at[0, a], there))
    for copy in first_copies:
        copy.start()
    tokens[x, a, k] = tok_ref[...]
    for part in range(3):
        w_all[part, x, a, k] = stage[a, part]

    odd = lax.broadcasted_iota(jnp.int32, (1, D), 1) % 2 == 1
    mid_sin, mid_cos = sin_ref[8:40], cos_ref[8:40]

    def start_of(n):
        s, co = sin_ref[pl.ds(n, 1)], cos_ref[pl.ds(n, 1)]
        return jnp.where(odd, co, s), jnp.where(odd, -s, co)

    def waves_of(n):
        s, co = start_of(n)
        rows_sin[...] = s * mid_cos + co * mid_sin
        rows_cos[...] = co * mid_cos - s * mid_sin

        def columns(j):
            lanes = pl.ds(pl.multiple_of(j * 128, 128), 128)
            low_sin, low_cos = sin_ref[40:56, lanes], cos_ref[40:56, lanes]
            for m in range(32):
                wave = rows_sin[m : m + 1, lanes] * low_cos + rows_cos[m : m + 1, lanes] * low_sin
                waves[pl.ds(pl.multiple_of(n * 512 + 16 * m, 16), 16), lanes] = wave.astype(BF)

        each(0, 16, columns)

    each(0, 4, waves_of)

    for h in heads:
        arrive(tokens.at[x, h, k], r1.at[1, h], partner)
        arrive(w_all.at[:, x, h, k], r1.at[0, h], partner)
    second_copies = []
    for rx, rb in rows:
        there = at(rx, a, rb, c, y)
        j = 2 * rx + rb
        second_copies.append(push(tokens.at[x, :, k], tokens.at[x, :, k], s2.at[1, j], r2.at[1, j_me], there))
        second_copies.append(push(w_all.at[:, x, :, k], w_all.at[:, x, :, k], s2.at[0, j], r2.at[0, j_me], there))
    for copy in second_copies:
        copy.start()

    def onward(rx, rb):
        j = 2 * rx + rb
        k2 = 2 * rb + c
        return [
            push(tokens.at[rx, :, k2], tokens.at[rx, :, k2], s3.at[1, j], r3.at[1, j], partner),
            push(w_all.at[:, rx, :, k2], w_all.at[:, rx, :, k2], s3.at[0, j], r3.at[0, j], partner),
        ]

    third_copies = onward(x, b)
    for copy in third_copies:
        copy.start()

    square = table_ref[...].astype(F32)
    square = square * square
    high = square.astype(BF)
    lower = (square - high.astype(F32)).astype(BF)
    ones = jnp.ones((8, D), BF)
    across = (((1,), (1,)), ((), ()))
    norms = lax.dot_general(ones, high, across, preferred_element_type=F32) + lax.dot_general(
        ones, lower, across, preferred_element_type=F32
    )
    norms = norms[0:1]
    vocab = lax.broadcasted_iota(jnp.int32, (128, 256), 1).astype(F32)
    diagonal = lax.broadcasted_iota(jnp.int32, (128, 128), 0) == lax.broadcasted_iota(jnp.int32, (128, 128), 1)

    def scales_of(n):
        here = tokens[x, n, k].astype(F32)
        row = pl.multiple_of(n * 512, 512)
        products = lax.dot_general(waves[pl.ds(row, 512), :], table_ref[...], across, preferred_element_type=F32)
        for q in range(4):
            column = jnp.sum(jnp.where(diagonal, here[q : q + 1, :], 0.0), axis=1, keepdims=True)
            chosen = column == vocab
            quarter = pl.ds(pl.multiple_of(n * 512 + 128 * q, 128), 128)
            one_hot[quarter, :] = chosen.astype(BF)
            total = jnp.sum(
                jnp.where(chosen, 2.0 * products[128 * q : 128 * q + 128] + norms, 0.0), axis=1, keepdims=True
            )
            total = jnp.maximum(total + D / 2, 0.0)
            inverse[quarter, :] = lax.rsqrt(total * (1.0 / D) + EPSILON)

    each(0, 4, scales_of)

    for rx, rb in rows:
        sx, sb = (2 * x + 4 - rx) % 4, rb
        j = 2 * sx + sb
        k2 = 2 * sb + c
        arrive(tokens.at[sx, :, k2], r2.at[1, j], partner)
        arrive(w_all.at[:, sx, :, k2], r2.at[0, j], partner)
        more = onward(sx, sb)
        for copy in more:
            copy.start()
        third_copies += more
    for rx, rb in [(x, b)] + rows:
        j = 2 * rx + rb
        k3 = 2 * rb + 1 - c
        arrive(tokens.at[rx, :, k3], r3.at[1, j], partner)
        arrive(w_all.at[:, rx, :, k3], r3.at[0, j], partner)

    main = c == y // 2
    source = jnp.logical_and(main, b == y % 2)
    beside = at(x, a, 1 - b, c, y)
    mine = [
        pltpu.make_async_copy(in_ref, w_in.at[x], own_w.at[0]),
        pltpu.make_async_copy(mout_ref, w_out.at[x], own_w.at[1]),
    ]
    step1 = [
        push(in_ref, w_in.at[x], sw1.at[0], rw1.at[0], beside),
        push(mout_ref, w_out.at[x], sw1.at[1], rw1.at[1], beside),
    ]

    @pl.when(source)
    def _():
        for copy in step1 + mine:
            copy.start()

    offset = offset_ref[0]
    slot = lax.broadcasted_iota(jnp.int32, (64, 1), 0)
    target = offset + (slot // 16) * 256 + 16 * r + slot % 16
    lane = lax.broadcasted_iota(jnp.int32, (1, 128), 1)
    found = jnp.zeros((64, 128), F32)
    for q in range(3):
        bytes_here = tokens[3, 3, 1 + q].astype(F32)
        for t in range(4):
            hit = target == lane + (31232 + 512 * q + 128 * t)
            found = found + jnp.where(hit, bytes_here[t : t + 1, :], 0.0)
    column = jnp.sum(found, axis=1, keepdims=True)
    looked = jnp.dot((column == vocab[:64]).astype(BF), table_ref[...], preferred_element_type=F32)
    for t in range(4):
        s, co = start_of(4 + t)
        wave = s * cos_ref[40:56] + co * sin_ref[40:56]
        latent[16 * t : 16 * t + 16, :] = rms_rows(looked[16 * t : 16 * t + 16] + wave).astype(BF)
    weights_of = w_all.reshape(3, D, HD)
    q_own[...] = jnp.dot(latent[...], weights_of[0], preferred_element_type=F32).astype(BF)
    asked = Exchange(q_own, q_all, s_q, r_q, r, row_of, 16, whole=True)
    asked.start()

    wkv[:, :HD] = weights_of[1]
    wkv[:, HD:] = weights_of[2]
    table_w = jnp.dot(table_ref[...], wkv[...], preferred_element_type=F32)
    tw[0] = table_w.astype(BF)
    tw[1] = (table_w - table_w.astype(BF).astype(F32)).astype(BF)

    def keys_of(n):
        run = pl.ds(pl.multiple_of(n * 512, 512), 512)
        both = jnp.dot(waves[run, :], wkv[...], preferred_element_type=F32)
        both = both + jnp.dot(one_hot[run, :], tw[0], preferred_element_type=F32)
        both = both + jnp.dot(one_hot[run, :], tw[1], preferred_element_type=F32)
        both = (both * inverse[run, :]).astype(BF)
        keys[run, :] = both[:, :HD]
        values[run, :] = both[:, HD:]

    each(0, 4, keys_of)
    asked.wait_all()

    key_col = lax.broadcasted_iota(jnp.int32, (1, 2048), 1)
    key_place = 512 * (16 * x + 4 * (key_col // 512) + k) + key_col % 512
    outs = Exchange(o_msg, o_came, s_o, r_o, r, row_of, 16)
    stats = Exchange(st_msg, st_came, s_st, r_st, r, row_of, 16)
    diagonal64 = lax.broadcasted_iota(jnp.int32, (64, 128), 0) == lax.broadcasted_iota(jnp.int32, (64, 128), 1)

    def attend(step):
        t = (x + 1 + step) % 4
        query = q_all[pl.ds(4 * t, 4)].reshape(256, HD)
        scores = lax.dot_general(query, keys[...], across, preferred_element_type=F32) * SCALE
        row = lax.broadcasted_iota(jnp.int32, (256, 1), 0)
        row_place = offset + ((row // 16) % 4) * 256 + 16 * (4 * t + row // 64) + row % 16
        scores = jnp.where(key_place > row_place, MASKED, scores)
        peak = jnp.max(scores, axis=1, keepdims=True)
        weights = jnp.exp(scores - peak).astype(BF)
        total = jnp.sum(weights.astype(F32), axis=1, keepdims=True)
        out = jnp.dot(weights, values[...], preferred_element_type=F32).astype(BF)
        for g in range(4):
            some = slice(64 * g, 64 * g + 64)
            j = 4 * t + g
            o_msg[j] = out[some]
            st_msg[j, 0:1, :] = jnp.sum(jnp.where(diagonal64, peak[some], 0.0), axis=0, keepdims=True)
            st_msg[j, 1:2, :] = jnp.sum(jnp.where(diagonal64, total[some], 0.0), axis=0, keepdims=True)

            @pl.when(j != r)
            def _():
                stats.copy(j).start()
                outs.copy(j).start()

    each(0, 4, attend)
    o_came[r] = o_msg[r]
    st_came[r] = st_msg[r]
    stats.wait_all()
    outs.wait_all()

    def forward(i):
        return [
            push(w_in.at[i], w_in.at[i], sw3.at[0, i], rw3.at[0, i], partner),
            push(w_out.at[i], w_out.at[i], sw3.at[1, i], rw3.at[1, i], partner),
        ]

    step2 = []
    for d in (1, 3, 2):
        there = at((x + d) % 4, a, b, c, y)
        step2.append(push(w_in.at[x], w_in.at[x], sw2.at[0, d], rw2.at[0, x], there))
        step2.append(push(w_out.at[x], w_out.at[x], sw2.at[1, d], rw2.at[1, x], there))

    @pl.when(source)
    def _():
        for copy in mine:
            copy.wait()

    @pl.when(jnp.logical_and(main, jnp.logical_not(source)))
    def _():
        arrive(w_in.at[x], rw1.at[0], partner)
        arrive(w_out.at[x], rw1.at[1], partner)

    @pl.when(main)
    def _():
        for copy in step2 + forward(x):
            copy.start()

    maxima, totals = st_came[:, 0, :], st_came[:, 1, :]
    factor = jnp.exp(maxima - jnp.max(maxima, axis=0, keepdims=True))
    factor = factor / jnp.sum(factor * totals, axis=0, keepdims=True)
    attended = jnp.zeros((64, HD), F32)
    for j in range(16):
        column = jnp.sum(jnp.where(diagonal64, factor[j : j + 1, :], 0.0), axis=1, keepdims=True)
        attended = attended + column * o_came[j].astype(F32)
    for copy in loads:
        copy.wait()

    def shares(rows, weight, out):
        for q in range(4):
            part = jnp.dot(rows, weight[:, 512 * q : 512 * q + 512], preferred_element_type=F32).astype(BF)
            for t in range(4):
                out[4 * t + q] = part[16 * t : 16 * t + 16]

    def rows_normed(blocks):
        for t in range(4):
            wide = jnp.concatenate([blocks[4 * t + q] for q in range(4)], axis=1).astype(F32)
            normed[16 * t : 16 * t + 16, :] = rms_rows(wide).astype(BF)

    shares(attended.astype(BF), w_co, msg)
    summed = Exchange(msg, came, s_m, r_m, p, head_of, 16)
    summed.start()
    own_block = (pl.ds(pl.multiple_of(16 * y, 16), 16), pl.ds(pl.multiple_of(512 * a, 512), 512))
    own_latent = latent[own_block].astype(F32)
    summed.wait_all()
    first = jnp.sum(came[...].astype(F32), axis=0) + own_latent
    own[...] = first.astype(BF)
    spread = Exchange(own, all_rows, s_a, r_a, p, head_of, 16, whole=True)
    spread.start()
    spread.wait_all()

    rows_normed(all_rows)
    kv[:, :HD] = jnp.dot(normed[...], w_qkv[1], preferred_element_type=F32).astype(BF)
    kv[:, HD:] = jnp.dot(normed[...], w_qkv[2], preferred_element_type=F32).astype(BF)
    both = Exchange(kv, kv_all, s_kv, r_kv, r, row_of, 16, whole=True)
    both.start()
    query = jnp.dot(normed[...], w_qkv[0], preferred_element_type=F32).astype(BF)
    both.wait_all()

    @pl.when(main)
    def _():
        for d in (1, 3, 2):
            i = (x + d) % 4
            arrive(w_in.at[i], rw2.at[0, i], partner)
            arrive(w_out.at[i], rw2.at[1, i], partner)
            for copy in forward(i):
                copy.start()

    all_keys = kv_all[:, :, :HD].reshape(LATENTS, HD)
    all_values = kv_all[:, :, HD:].reshape(LATENTS, HD)
    scores = lax.dot_general(query, all_keys, across, preferred_element_type=F32) * SCALE
    row = lax.broadcasted_iota(jnp.int32, (64, 1), 0)
    col = lax.broadcasted_iota(jnp.int32, (1, LATENTS), 1)
    row_place = (row // 16) * 256 + 16 * r + row % 16
    col_place = ((col // 16) % 4) * 256 + 16 * (col // 64) + col % 16
    scores = jnp.where(col_place > row_place, MASKED, scores)
    weights = jnp.exp(scores - jnp.max(scores, axis=1, keepdims=True)).astype(BF)
    total = jnp.sum(weights.astype(F32), axis=1, keepdims=True)
    attended = jnp.dot(weights, all_values, preferred_element_type=F32) / total
    shares(attended.astype(BF), w_so, msg2)
    summed2 = Exchange(msg2, came2, s_m2, r_m2, p, head_of, 16)
    summed2.start()
    summed2.wait_all()
    second = first + jnp.sum(came2[...].astype(F32), axis=0)
    own2[...] = second.astype(BF)
    spread2 = Exchange(own2, all_rows2, s_a2, r_a2, p, head_of, 16, whole=True)
    spread2.start()

    @pl.when(jnp.logical_not(main))
    def _():
        for i in range(4):
            arrive(w_in.at[i], rw3.at[0, i], partner)
            arrive(w_out.at[i], rw3.at[1, i], partner)

    spread2.wait_all()

    rows_normed(all_rows2)
    hidden = []
    for i in range(4):
        pre = jnp.dot(normed[...], w_in[i], preferred_element_type=F32)
        hidden.append(jax.nn.gelu(pre, approximate=True).astype(BF))
    hidden = jnp.concatenate(hidden, axis=1)
    for q in range(4):
        columns = slice(512 * q, 512 * q + 512)
        partial[q] = jnp.dot(hidden, w_out[:, :, columns].reshape(512, 512), preferred_element_type=F32)
    here = pl.ds(pl.multiple_of(16 * y, 16), 16)
    partial[a, here, :] = partial[a, here, :] + second
    for j in range(16):
        some = slice(4 * j, 4 * j + 4)
        msg3[j] = jnp.concatenate([partial[q, some, :] for q in range(4)], axis=0).astype(BF)

    def last_copy(j):
        return push(msg3.at[j], came3.at[p], s_m3.at[j], r_m3.at[p], final_of(j))

    def last_start(i):
        j = (p + i) % 16

        @pl.when(j != final_self)
        def _():
            last_copy(j).start()

    each(0, 16, last_start)

    @pl.when(a == k)
    def _():
        came3[p] = msg3[4 * y + k]

    def last_wait(i):
        j = (p + i) % 16

        @pl.when(j != sender_self)
        def _():
            arrive(came3.at[j], r_m3.at[j], partner)

    each(0, 16, last_wait)
    ended = jnp.sum(came3[...].astype(F32), axis=0)
    for q in range(4):
        out_ref[:, 512 * q : 512 * q + 512] = ended[4 * q : 4 * q + 4]

    for copy in first_copies + second_copies + third_copies:
        copy.wait_send()
    for exchange in (asked, outs, stats, summed, spread, both, summed2, spread2):
        exchange.wait_sent()

    def last_sent(i):
        j = (p + i) % 16

        @pl.when(j != final_self)
        def _():
            last_copy(j).wait_send()

    each(0, 16, last_sent)

    @pl.when(source)
    def _():
        for copy in step1:
            copy.wait_send()

    @pl.when(main)
    def _():
        for copy in step2:
            copy.wait_send()
        for i in range(4):
            for copy in forward(i):
                copy.wait_send()


def per_device(
    token_ids,
    latent_offset,
    embed_table,
    cross_q,
    cross_kv,
    cross_out,
    self_qkv,
    self_out,
    mlp_in,
    mlp_out,
):
    x, a, b, c, y = place()
    r = 4 * x + 2 * b + c
    feature = jnp.arange(D, dtype=jnp.int32)
    rates = jnp.exp((feature // 2).astype(F32) * (-2.0 * math.log(10000.0) / D))
    four = jnp.arange(4, dtype=jnp.int32)
    places = jnp.concatenate(
        [
            512 * (16 * x + 4 * four + 2 * b + c),
            latent_offset[0] + 256 * four + 16 * r,
            16 * jnp.arange(32, dtype=jnp.int32),
            jnp.arange(16, dtype=jnp.int32),
        ]
    )
    angles = places.astype(F32)[:, None] * rates[None, :]
    vmem = pl.BlockSpec(memory_space=pltpu.VMEM)
    hbm = pl.BlockSpec(memory_space=pl.ANY)
    dma = pltpu.SemaphoreType.DMA
    rows = pl.pallas_call(
        whole_kernel,
        out_shape=jax.ShapeDtypeStruct((4, D), F32),
        in_specs=[pl.BlockSpec(memory_space=pltpu.SMEM)] + [vmem] * 6 + [hbm] * 5,
        out_specs=vmem,
        scratch_shapes=[
            pltpu.VMEM((4, 3, 32, HD), BF),
            pltpu.VMEM((3, 4, 4, 4, 32, HD), BF),
            pltpu.VMEM((4, 4, 4, 4, 128), jnp.int32),
            pltpu.VMEM((D, 2 * HD), BF),
            pltpu.VMEM((2, 256, 2 * HD), BF),
            pltpu.VMEM((32, D), F32),
            pltpu.VMEM((32, D), F32),
            pltpu.VMEM((2048, D), BF),
            pltpu.VMEM((2048, 256), BF),
            pltpu.VMEM((2048, 1), F32),
            pltpu.VMEM((64, D), BF),
            pltpu.VMEM((2048, HD), BF),
            pltpu.VMEM((2048, HD), BF),
            pltpu.VMEM((64, HD), BF),
            pltpu.VMEM((16, 64, HD), BF),
            pltpu.VMEM((16, 64, HD), BF),
            pltpu.VMEM((16, 64, HD), BF),
            pltpu.VMEM((16, 8, 128), F32),
            pltpu.VMEM((16, 8, 128), F32),
            pltpu.VMEM((HD, D), BF),
            pltpu.VMEM((3, D, HD), BF),
            pltpu.VMEM((HD, D), BF),
            pltpu.VMEM((16, 16, 512), BF),
            pltpu.VMEM((16, 16, 512), BF),
            pltpu.VMEM((16, 512), BF),
            pltpu.VMEM((16, 16, 512), BF),
            pltpu.VMEM((64, D), BF),
            pltpu.VMEM((64, 2 * HD), BF),
            pltpu.VMEM((16, 64, 2 * HD), BF),
            pltpu.VMEM((16, 16, 512), BF),
            pltpu.VMEM((16, 16, 512), BF),
            pltpu.VMEM((16, 512), BF),
            pltpu.VMEM((16, 16, 512), BF),
            pltpu.VMEM((4, D, HD), BF),
            pltpu.VMEM((4, HD, D), BF),
            pltpu.VMEM((4, 64, 512), F32),
            pltpu.VMEM((16, 16, 512), BF),
            pltpu.VMEM((16, 16, 512), BF),
            dma((3,)),
            dma((2, 4)),
            dma((2, 4)),
            dma((2, 8)),
            dma((2, 8)),
            dma((2, 8)),
            dma((2, 8)),
        ]
        + [dma((16,))] * 18
        + [dma((2,)), dma((2,)), dma((2,)), dma((2, 4)), dma((2, 4)), dma((2, 4)), dma((2, 4))],
        compiler_params=pltpu.CompilerParams(
            collective_id=0, has_side_effects=True, vmem_limit_bytes=VLIMIT
        ),
    )(
        latent_offset, jnp.sin(angles), jnp.cos(angles), token_ids.reshape(4, 128), embed_table,
        cross_q, cross_kv, cross_out, self_qkv, self_out, mlp_in, mlp_out,
    )
    return rows.astype(BF)[None]


def solution(mesh):
    placed = (
        P("ctx"),
        P(),
        P(),
        P("ctx", "lat"),
        P(None, "ctx", "lat"),
        P("lat", None),
        P(None, None, "lat"),
        P("lat", None),
        P(None, "ctx"),
        P("ctx", None),
    )
    return jax.shard_map(
        per_device, mesh=mesh, in_specs=placed, out_specs=P("lat", "ctx", None), check_vma=False
    )
```

```python
import math

import jax
import jax.numpy as jnp
from jax import lax
from jax.experimental import pallas as pl
from jax.experimental.pallas import tpu as pltpu
from jax.sharding import PartitionSpec as P

MESH = pl.DeviceIdType.MESH
HD = 128
D = 2048
LATENTS = 1024
EPSILON = 1e-06
MASKED = -1e30
SCALE = 1.0 / math.sqrt(HD)
BF = jnp.bfloat16
F32 = jnp.float32
VLIMIT = 58 * 1024 * 1024


def place():
    g = lax.axis_index("ctx")
    y = lax.axis_index("lat")
    return g // 16, (g // 4) % 4, (g // 2) % 2, g % 2, y


def at(x, a, b, c, y):
    return (16 * x + 4 * a + 2 * b + c, y)


def push(src, dst, send_sem, recv_sem, device):
    copy = pltpu.make_async_remote_copy(
        src_ref=src,
        dst_ref=dst,
        send_sem=send_sem,
        recv_sem=recv_sem,
        device_id=device,
        device_id_type=MESH,
    )
    return copy


def arrive(dst, recv_sem, device):
    push(dst, dst, recv_sem, recv_sem, device).wait_recv()


def each(first, last, body):
    def step(k, carry):
        body(k)
        return carry

    lax.fori_loop(first, last, step, 0)


class Exchange:
    def __init__(self, src, dst, send, recv, me, device_of, n, whole=False):
        self.src, self.dst, self.send, self.recv = src, dst, send, recv
        self.me, self.device_of, self.n, self.whole = me, device_of, n, whole

    def copy(self, j):
        src = self.src if self.whole else self.src.at[j]
        return push(src, self.dst.at[self.me], self.send.at[j], self.recv.at[self.me], self.device_of(j))

    def start(self):
        def one(k):
            self.copy((self.me + k) % self.n).start()

        each(1, self.n, one)
        self.dst[self.me] = self.src[...] if self.whole else self.src[self.me]

    def wait_all(self):
        def one(k):
            j = (self.me + self.n - k) % self.n
            arrive(self.dst.at[j], self.recv.at[j], self.device_of(j))

        each(1, self.n, one)

    def wait_sent(self):
        def one(k):
            self.copy((self.me + k) % self.n).wait_send()

        each(1, self.n, one)


def rms_rows(values):
    return values * lax.rsqrt(jnp.mean(values * values, axis=-1, keepdims=True) + EPSILON)


def whole_kernel(
    offset_ref, tok_ref, table_ref, q_ref, kv_ref,
    cout_ref, sqkv_ref, sout_ref, in_ref, mout_ref,
    out_ref,
    stage, w_all, tokens, wkv, tw, sin_ref, cos_ref, rows_sin, rows_cos, waves, products, one_hot, inverse, latent, keys, values, q_own, q_all,
    o_msg, o_came, st_msg, st_came, w_co, w_qkv, w_so, msg, came, own, all_rows, normed, kv, kv_all, msg2, came2,
    own2, all_rows2, w_in, w_out, partial, msg3, came3,
    load, s1, r1, s2, r2, s3, r3, s_q, r_q, s_o, r_o, s_st, r_st, s_m, r_m, s_a, r_a, s_kv, r_kv, s_m2, r_m2,
    s_a2, r_a2, s_m3, r_m3, own_w, sw1, rw1, sw2, rw2, sw3, rw3,
):
    x, a, b, c, y = place()
    k = 2 * b + c
    r = 4 * x + k
    p = 4 * y + a
    j_me = 2 * x + b
    partner = at(x, a, b, 1 - c, y)

    def row_of(j):
        return at(j // 4, a, (j // 2) % 2, j % 2, y)

    def head_of(j):
        return at(x, j % 4, b, c, j // 4)

    def final_of(j):
        return at(x, k, (j // 2) % 2, j % 2, j // 4)

    def sender_of(j):
        return at(x, j % 4, a // 2, a % 2, j // 4)

    final_self = jnp.where(a == k, 4 * y + k, 16)
    sender_self = jnp.where(a == k, p, 16)

    row_at = pl.multiple_of(a * HD, HD)
    loads = [
        pltpu.make_async_copy(cout_ref.at[pl.ds(row_at, HD), :], w_co, load.at[0]),
        pltpu.make_async_copy(sqkv_ref.at[:, :, pl.ds(row_at, HD)], w_qkv, load.at[1]),
        pltpu.make_async_copy(sout_ref.at[pl.ds(row_at, HD), :], w_so, load.at[2]),
    ]
    for copy in loads:
        copy.start()
    barrier = pltpu.get_barrier_semaphore()

    def hello(device):
        pl.semaphore_signal(barrier, inc=1, device_id=device, device_id_type=MESH)

    each(1, 16, lambda i: hello(row_of((r + i) % 16)))
    each(1, 16, lambda i: hello(head_of((p + i) % 16)))

    def hello_sender(j):
        @pl.when(j != sender_self)
        def _():
            hello(sender_of(j))

    each(0, 16, hello_sender)
    for h in range(4):
        stage[h, 0] = q_ref[:, 128 * h : 128 * h + 128]
        stage[h, 1] = kv_ref[0, :, 128 * h : 128 * h + 128]
        stage[h, 2] = kv_ref[1, :, 128 * h : 128 * h + 128]
    offset = offset_ref[0]
    index = lax.broadcasted_iota(jnp.int32, (56, 1), 0)
    places = jnp.where(index < 4, 512 * (16 * x + 4 * index + k), offset + 256 * (index - 4) + 16 * r)
    places = jnp.where(index < 8, places, jnp.where(index < 40, 16 * (index - 8), index - 40)).astype(F32)

    def table_columns(j):
        lanes = pl.ds(pl.multiple_of(j * 256, 256), 256)
        pair = ((j * 256 + lax.broadcasted_iota(jnp.int32, (1, 256), 1)) // 2).astype(F32)
        angles = places * jnp.exp(pair * (-2.0 * math.log(10000.0) / D))
        sin_ref[:, lanes] = jnp.sin(angles)
        cos_ref[:, lanes] = jnp.cos(angles)

    each(0, 8, table_columns)
    odd = lax.broadcasted_iota(jnp.int32, (1, D), 1) % 2 == 1
    mid_sin, mid_cos = sin_ref[8:40], cos_ref[8:40]

    def start_of(n):
        s, co = sin_ref[pl.ds(n, 1)], cos_ref[pl.ds(n, 1)]
        return jnp.where(odd, co, s), jnp.where(odd, -s, co)

    def waves_of(n):
        s, co = start_of(n)
        rows_sin[...] = s * mid_cos + co * mid_sin
        rows_cos[...] = co * mid_cos - s * mid_sin

        def columns(j):
            lanes = pl.ds(pl.multiple_of(j * 128, 128), 128)
            low_sin, low_cos = sin_ref[40:56, lanes], cos_ref[40:56, lanes]
            for m in range(32):
                wave = rows_sin[m : m + 1, lanes] * low_cos + rows_cos[m : m + 1, lanes] * low_sin
                waves[pl.ds(pl.multiple_of(n * 512 + 16 * m, 16), 16), lanes] = wave.astype(BF)

        each(0, 16, columns)

    each(0, 4, waves_of)
    pl.semaphore_wait(barrier, jnp.where(a == k, 45, 46))
    ends = []

    heads = [(a + d) % 4 for d in range(1, 4)]
    rows = [((x + dx) % 4, (b + db) % 2) for dx in (0, 1, 3, 2) for db in (0, 1) if dx or db]
    first_copies = []
    for h in heads:
        there = at(x, h, b, c, y)
        first_copies.append(push(tok_ref, tokens.at[x, a, k], s1.at[1, h], r1.at[1, a], there))
        first_copies.append(push(stage.at[h], w_all.at[:, x, a, k], s1.at[0, h], r1.at[0, a], there))
    for copy in first_copies:
        copy.start()
        ends.append(copy.wait_send)
    tokens[x, a, k] = tok_ref[...]
    for part in range(3):
        w_all[part, x, a, k] = stage[a, part]

    square = table_ref[...].astype(F32)
    square = square * square
    high = square.astype(BF)
    lower = (square - high.astype(F32)).astype(BF)
    ones = jnp.ones((8, D), BF)
    across = (((1,), (1,)), ((), ()))
    norms = lax.dot_general(ones, high, across, preferred_element_type=F32) + lax.dot_general(
        ones, lower, across, preferred_element_type=F32
    )
    norms = norms[0:1]

    def products_of(n):
        run = pl.ds(pl.multiple_of(n * 512, 512), 512)
        products[run, :] = lax.dot_general(waves[run, :], table_ref[...], across, preferred_element_type=F32)

    each(0, 4, products_of)

    for h in heads:
        arrive(tokens.at[x, h, k], r1.at[1, h], partner)
        arrive(w_all.at[:, x, h, k], r1.at[0, h], partner)
    second_copies = []
    for rx, rb in rows:
        there = at(rx, a, rb, c, y)
        j = 2 * rx + rb
        second_copies.append(push(tokens.at[x, :, k], tokens.at[x, :, k], s2.at[1, j], r2.at[1, j_me], there))
        second_copies.append(push(w_all.at[:, x, :, k], w_all.at[:, x, :, k], s2.at[0, j], r2.at[0, j_me], there))
    for copy in second_copies:
        copy.start()
        ends.append(copy.wait_send)

    def onward(rx, rb):
        j = 2 * rx + rb
        k2 = 2 * rb + c
        return [
            push(tokens.at[rx, :, k2], tokens.at[rx, :, k2], s3.at[1, j], r3.at[1, j], partner),
            push(w_all.at[:, rx, :, k2], w_all.at[:, rx, :, k2], s3.at[0, j], r3.at[0, j], partner),
        ]

    third_copies = onward(x, b)
    for copy in third_copies:
        copy.start()
        ends.append(copy.wait_send)

    main = c == y // 2
    source = jnp.logical_and(main, b == y % 2)
    beside = at(x, a, 1 - b, c, y)
    mine = [
        pltpu.make_async_copy(in_ref, w_in.at[x], own_w.at[0]),
        pltpu.make_async_copy(mout_ref, w_out.at[x], own_w.at[1]),
    ]
    step1 = [
        push(in_ref, w_in.at[x], sw1.at[0], rw1.at[0], beside),
        push(mout_ref, w_out.at[x], sw1.at[1], rw1.at[1], beside),
    ]

    @pl.when(source)
    def _():
        for copy in step1 + mine:
            copy.start()

    vocab = lax.broadcasted_iota(jnp.int32, (128, 256), 1).astype(F32)
    diagonal = lax.broadcasted_iota(jnp.int32, (128, 128), 0) == lax.broadcasted_iota(jnp.int32, (128, 128), 1)

    def scales_of(n):
        here = tokens[x, n, k].astype(F32)
        for q in range(4):
            column = jnp.sum(jnp.where(diagonal, here[q : q + 1, :], 0.0), axis=1, keepdims=True)
            chosen = column == vocab
            quarter = pl.ds(pl.multiple_of(n * 512 + 128 * q, 128), 128)
            one_hot[quarter, :] = chosen.astype(BF)
            total = jnp.sum(
                jnp.where(chosen, 2.0 * products[quarter, :] + norms, 0.0), axis=1, keepdims=True
            )
            total = jnp.maximum(total + D / 2, 0.0)
            inverse[quarter, :] = lax.rsqrt(total * (1.0 / D) + EPSILON)

    each(0, 4, scales_of)

    for rx, rb in rows:
        sx, sb = (2 * x + 4 - rx) % 4, rb
        j = 2 * sx + sb
        k2 = 2 * sb + c
        arrive(tokens.at[sx, :, k2], r2.at[1, j], partner)
        arrive(w_all.at[:, sx, :, k2], r2.at[0, j], partner)
        more = onward(sx, sb)
        for copy in more:
            copy.start()
            ends.append(copy.wait_send)
    for rx, rb in [(x, b)] + rows:
        j = 2 * rx + rb
        k3 = 2 * rb + 1 - c
        arrive(tokens.at[rx, :, k3], r3.at[1, j], partner)
        arrive(w_all.at[:, rx, :, k3], r3.at[0, j], partner)

    slot = lax.broadcasted_iota(jnp.int32, (64, 1), 0)
    target = offset + (slot // 16) * 256 + 16 * r + slot % 16
    lane = lax.broadcasted_iota(jnp.int32, (1, 128), 1)
    found = jnp.zeros((64, 128), F32)
    for q in range(3):
        bytes_here = tokens[3, 3, 1 + q].astype(F32)
        for t in range(4):
            hit = target == lane + (31232 + 512 * q + 128 * t)
            found = found + jnp.where(hit, bytes_here[t : t + 1, :], 0.0)
    column = jnp.sum(found, axis=1, keepdims=True)
    looked = jnp.dot((column == vocab[:64]).astype(BF), table_ref[...], preferred_element_type=F32)
    for t in range(4):
        s, co = start_of(4 + t)
        wave = s * cos_ref[40:56] + co * sin_ref[40:56]
        latent[16 * t : 16 * t + 16, :] = rms_rows(looked[16 * t : 16 * t + 16] + wave).astype(BF)
    weights_of = w_all.reshape(3, D, HD)
    q_own[...] = jnp.dot(latent[...], weights_of[0], preferred_element_type=F32).astype(BF)
    asked = Exchange(q_own, q_all, s_q, r_q, r, row_of, 16, whole=True)
    asked.start()
    ends.append(asked.wait_sent)

    wkv[:, :HD] = weights_of[1]
    wkv[:, HD:] = weights_of[2]
    table_w = jnp.dot(table_ref[...], wkv[...], preferred_element_type=F32)
    tw[0] = table_w.astype(BF)
    tw[1] = (table_w - table_w.astype(BF).astype(F32)).astype(BF)

    def keys_of(n):
        run = pl.ds(pl.multiple_of(n * 512, 512), 512)
        both = jnp.dot(waves[run, :], wkv[...], preferred_element_type=F32)
        both = both + jnp.dot(one_hot[run, :], tw[0], preferred_element_type=F32)
        both = both + jnp.dot(one_hot[run, :], tw[1], preferred_element_type=F32)
        both = (both * inverse[run, :]).astype(BF)
        keys[run, :] = both[:, :HD]
        values[run, :] = both[:, HD:]

    each(0, 4, keys_of)
    asked.wait_all()

    key_col = lax.broadcasted_iota(jnp.int32, (1, 2048), 1)
    key_place = 512 * (16 * x + 4 * (key_col // 512) + k) + key_col % 512
    outs = Exchange(o_msg, o_came, s_o, r_o, r, row_of, 16)
    stats = Exchange(st_msg, st_came, s_st, r_st, r, row_of, 16)
    diagonal64 = lax.broadcasted_iota(jnp.int32, (64, 128), 0) == lax.broadcasted_iota(jnp.int32, (64, 128), 1)

    def attend(step):
        t = (x + 1 + step) % 4
        query = q_all[pl.ds(4 * t, 4)].reshape(256, HD)
        scores = lax.dot_general(query, keys[...], across, preferred_element_type=F32) * SCALE
        row = lax.broadcasted_iota(jnp.int32, (256, 1), 0)
        row_place = offset + ((row // 16) % 4) * 256 + 16 * (4 * t + row // 64) + row % 16
        scores = jnp.where(key_place > row_place, MASKED, scores)
        peak = jnp.max(scores, axis=1, keepdims=True)
        weights = jnp.exp(scores - peak).astype(BF)
        total = jnp.sum(weights.astype(F32), axis=1, keepdims=True)
        out = jnp.dot(weights, values[...], preferred_element_type=F32).astype(BF)
        for g in range(4):
            some = slice(64 * g, 64 * g + 64)
            j = 4 * t + g
            o_msg[j] = out[some]
            st_msg[j, 0:1, :] = jnp.sum(jnp.where(diagonal64, peak[some], 0.0), axis=0, keepdims=True)
            st_msg[j, 1:2, :] = jnp.sum(jnp.where(diagonal64, total[some], 0.0), axis=0, keepdims=True)

            @pl.when(j != r)
            def _():
                stats.copy(j).start()
                outs.copy(j).start()

    each(0, 4, attend)
    o_came[r] = o_msg[r]
    st_came[r] = st_msg[r]
    stats.wait_all()
    outs.wait_all()
    ends += [stats.wait_sent, outs.wait_sent]

    halves = (w_in, w_out)
    others = [(x + d) % 4 for d in (1, 3, 2)]

    def along(h):
        copies = [push(halves[h].at[x], halves[h].at[x], sw2.at[h, i], rw2.at[h, x], at(i, a, b, c, y)) for i in others]
        return copies + [forward(h, x)]

    def forward(h, i):
        return push(halves[h].at[i], halves[h].at[i], sw3.at[h, i], rw3.at[h, i], partner)

    def set_out(h):
        @pl.when(source)
        def _():
            mine[h].wait()

        @pl.when(jnp.logical_and(main, jnp.logical_not(source)))
        def _():
            arrive(halves[h].at[x], rw1.at[h], partner)

        @pl.when(main)
        def _():
            for copy in along(h):
                copy.start()

    def hand_over(h):
        @pl.when(main)
        def _():
            for i in others:
                arrive(halves[h].at[i], rw2.at[h, i], partner)
                forward(h, i).start()

    def receive(h):
        @pl.when(jnp.logical_not(main))
        def _():
            for i in range(4):
                arrive(halves[h].at[i], rw3.at[h, i], partner)

    set_out(0)

    maxima, totals = st_came[:, 0, :], st_came[:, 1, :]
    factor = jnp.exp(maxima - jnp.max(maxima, axis=0, keepdims=True))
    factor = factor / jnp.sum(factor * totals, axis=0, keepdims=True)
    attended = jnp.zeros((64, HD), F32)
    for j in range(16):
        column = jnp.sum(jnp.where(diagonal64, factor[j : j + 1, :], 0.0), axis=1, keepdims=True)
        attended = attended + column * o_came[j].astype(F32)
    for copy in loads:
        copy.wait()

    def shares(rows, weight, out):
        for q in range(4):
            part = jnp.dot(rows, weight[:, 512 * q : 512 * q + 512], preferred_element_type=F32).astype(BF)
            for t in range(4):
                out[4 * t + q] = part[16 * t : 16 * t + 16]

    def rows_normed(blocks):
        for t in range(4):
            wide = jnp.concatenate([blocks[4 * t + q] for q in range(4)], axis=1).astype(F32)
            normed[16 * t : 16 * t + 16, :] = rms_rows(wide).astype(BF)

    shares(attended.astype(BF), w_co, msg)
    summed = Exchange(msg, came, s_m, r_m, p, head_of, 16)
    summed.start()
    own_block = (pl.ds(pl.multiple_of(16 * y, 16), 16), pl.ds(pl.multiple_of(512 * a, 512), 512))
    own_latent = latent[own_block].astype(F32)
    summed.wait_all()
    ends.append(summed.wait_sent)
    first = jnp.sum(came[...].astype(F32), axis=0) + own_latent
    own[...] = first.astype(BF)
    spread = Exchange(own, all_rows, s_a, r_a, p, head_of, 16, whole=True)
    spread.start()
    spread.wait_all()
    ends.append(spread.wait_sent)

    rows_normed(all_rows)
    kv[:, :HD] = jnp.dot(normed[...], w_qkv[1], preferred_element_type=F32).astype(BF)
    kv[:, HD:] = jnp.dot(normed[...], w_qkv[2], preferred_element_type=F32).astype(BF)
    both = Exchange(kv, kv_all, s_kv, r_kv, r, row_of, 16, whole=True)
    both.start()
    query = jnp.dot(normed[...], w_qkv[0], preferred_element_type=F32).astype(BF)
    both.wait_all()
    ends.append(both.wait_sent)

    set_out(1)
    hand_over(0)
    all_keys = kv_all[:, :, :HD].reshape(LATENTS, HD)
    all_values = kv_all[:, :, HD:].reshape(LATENTS, HD)
    scores = lax.dot_general(query, all_keys, across, preferred_element_type=F32) * SCALE
    row = lax.broadcasted_iota(jnp.int32, (64, 1), 0)
    col = lax.broadcasted_iota(jnp.int32, (1, LATENTS), 1)
    row_place = (row // 16) * 256 + 16 * r + row % 16
    col_place = ((col // 16) % 4) * 256 + 16 * (col // 64) + col % 16
    scores = jnp.where(col_place > row_place, MASKED, scores)
    weights = jnp.exp(scores - jnp.max(scores, axis=1, keepdims=True)).astype(BF)
    total = jnp.sum(weights.astype(F32), axis=1, keepdims=True)
    attended = jnp.dot(weights, all_values, preferred_element_type=F32) / total
    shares(attended.astype(BF), w_so, msg2)
    summed2 = Exchange(msg2, came2, s_m2, r_m2, p, head_of, 16)
    summed2.start()
    summed2.wait_all()
    ends.append(summed2.wait_sent)
    second = first + jnp.sum(came2[...].astype(F32), axis=0)
    own2[...] = second.astype(BF)
    spread2 = Exchange(own2, all_rows2, s_a2, r_a2, p, head_of, 16, whole=True)
    spread2.start()

    spread2.wait_all()
    ends.append(spread2.wait_sent)

    rows_normed(all_rows2)
    hand_over(1)
    receive(0)
    hidden = []
    for i in range(4):
        pre = jnp.dot(normed[...], w_in[i], preferred_element_type=F32)
        hidden.append(jax.nn.gelu(pre, approximate=True).astype(BF))
    hidden = jnp.concatenate(hidden, axis=1)
    receive(1)
    for q in range(4):
        columns = slice(512 * q, 512 * q + 512)
        partial[q] = jnp.dot(hidden, w_out[:, :, columns].reshape(512, 512), preferred_element_type=F32)
    here = pl.ds(pl.multiple_of(16 * y, 16), 16)
    partial[a, here, :] = partial[a, here, :] + second
    for j in range(16):
        some = slice(4 * j, 4 * j + 4)
        msg3[j] = jnp.concatenate([partial[q, some, :] for q in range(4)], axis=0).astype(BF)

    def last_copy(j):
        return push(msg3.at[j], came3.at[p], s_m3.at[j], r_m3.at[p], final_of(j))

    def last_start(i):
        j = (p + i) % 16

        @pl.when(j != final_self)
        def _():
            last_copy(j).start()

    each(0, 16, last_start)

    @pl.when(a == k)
    def _():
        came3[p] = msg3[4 * y + k]

    def last_wait(i):
        j = (p + i) % 16

        @pl.when(j != sender_self)
        def _():
            arrive(came3.at[j], r_m3.at[j], partner)

    each(0, 16, last_wait)
    ended = jnp.sum(came3[...].astype(F32), axis=0)
    for q in range(4):
        out_ref[:, 512 * q : 512 * q + 512] = ended[4 * q : 4 * q + 4]

    for end in ends:
        end()

    def last_sent(i):
        j = (p + i) % 16

        @pl.when(j != final_self)
        def _():
            last_copy(j).wait_send()

    each(0, 16, last_sent)

    @pl.when(source)
    def _():
        for copy in step1:
            copy.wait_send()

    @pl.when(main)
    def _():
        for h in range(2):
            for copy in along(h):
                copy.wait_send()
            for i in others:
                forward(h, i).wait_send()


def per_device(
    token_ids,
    latent_offset,
    embed_table,
    cross_q,
    cross_kv,
    cross_out,
    self_qkv,
    self_out,
    mlp_in,
    mlp_out,
):
    vmem = pl.BlockSpec(memory_space=pltpu.VMEM)
    hbm = pl.BlockSpec(memory_space=pl.ANY)
    dma = pltpu.SemaphoreType.DMA
    rows = pl.pallas_call(
        whole_kernel,
        out_shape=jax.ShapeDtypeStruct((4, D), F32),
        in_specs=[pl.BlockSpec(memory_space=pltpu.SMEM)] + [vmem] * 4 + [hbm] * 5,
        out_specs=vmem,
        scratch_shapes=[
            pltpu.VMEM((4, 3, 32, HD), BF),
            pltpu.VMEM((3, 4, 4, 4, 32, HD), BF),
            pltpu.VMEM((4, 4, 4, 4, 128), jnp.int32),
            pltpu.VMEM((D, 2 * HD), BF),
            pltpu.VMEM((2, 256, 2 * HD), BF),
            pltpu.VMEM((56, D), F32),
            pltpu.VMEM((56, D), F32),
            pltpu.VMEM((32, D), F32),
            pltpu.VMEM((32, D), F32),
            pltpu.VMEM((2048, D), BF),
            pltpu.VMEM((2048, 256), F32),
            pltpu.VMEM((2048, 256), BF),
            pltpu.VMEM((2048, 1), F32),
            pltpu.VMEM((64, D), BF),
            pltpu.VMEM((2048, HD), BF),
            pltpu.VMEM((2048, HD), BF),
            pltpu.VMEM((64, HD), BF),
            pltpu.VMEM((16, 64, HD), BF),
            pltpu.VMEM((16, 64, HD), BF),
            pltpu.VMEM((16, 64, HD), BF),
            pltpu.VMEM((16, 8, 128), F32),
            pltpu.VMEM((16, 8, 128), F32),
            pltpu.VMEM((HD, D), BF),
            pltpu.VMEM((3, D, HD), BF),
            pltpu.VMEM((HD, D), BF),
            pltpu.VMEM((16, 16, 512), BF),
            pltpu.VMEM((16, 16, 512), BF),
            pltpu.VMEM((16, 512), BF),
            pltpu.VMEM((16, 16, 512), BF),
            pltpu.VMEM((64, D), BF),
            pltpu.VMEM((64, 2 * HD), BF),
            pltpu.VMEM((16, 64, 2 * HD), BF),
            pltpu.VMEM((16, 16, 512), BF),
            pltpu.VMEM((16, 16, 512), BF),
            pltpu.VMEM((16, 512), BF),
            pltpu.VMEM((16, 16, 512), BF),
            pltpu.VMEM((4, D, HD), BF),
            pltpu.VMEM((4, HD, D), BF),
            pltpu.VMEM((4, 64, 512), F32),
            pltpu.VMEM((16, 16, 512), BF),
            pltpu.VMEM((16, 16, 512), BF),
            dma((3,)),
            dma((2, 4)),
            dma((2, 4)),
            dma((2, 8)),
            dma((2, 8)),
            dma((2, 8)),
            dma((2, 8)),
        ]
        + [dma((16,))] * 18
        + [dma((2,)), dma((2,)), dma((2,)), dma((2, 4)), dma((2, 4)), dma((2, 4)), dma((2, 4))],
        compiler_params=pltpu.CompilerParams(
            collective_id=0, has_side_effects=True, vmem_limit_bytes=VLIMIT
        ),
    )(
        latent_offset, token_ids.reshape(4, 128), embed_table,
        cross_q, cross_kv, cross_out, self_qkv, self_out, mlp_in, mlp_out,
    )
    return rows.astype(BF)[None]


def solution(mesh):
    placed = (
        P("ctx"),
        P(),
        P(),
        P("ctx", "lat"),
        P(None, "ctx", "lat"),
        P("lat", None),
        P(None, None, "lat"),
        P("lat", None),
        P(None, "ctx"),
        P("ctx", None),
    )
    return jax.shard_map(
        per_device, mesh=mesh, in_specs=placed, out_specs=P("lat", "ctx", None), check_vma=False
    )
```

```python
import math

import jax
import jax.numpy as jnp
from jax import lax
from jax.experimental import pallas as pl
from jax.experimental.pallas import tpu as pltpu
from jax.sharding import PartitionSpec as P

MESH = pl.DeviceIdType.MESH
HD = 128
D = 2048
LATENTS = 1024
EPSILON = 1e-06
MASKED = -1e30
SCALE = 1.0 / math.sqrt(HD)
BF = jnp.bfloat16
F32 = jnp.float32
VLIMIT = 58 * 1024 * 1024


def place():
    g = lax.axis_index("ctx")
    y = lax.axis_index("lat")
    return g // 16, (g // 4) % 4, (g // 2) % 2, g % 2, y


def at(x, a, b, c, y):
    return (16 * x + 4 * a + 2 * b + c, y)


def push(src, dst, send_sem, recv_sem, device):
    copy = pltpu.make_async_remote_copy(
        src_ref=src,
        dst_ref=dst,
        send_sem=send_sem,
        recv_sem=recv_sem,
        device_id=device,
        device_id_type=MESH,
    )
    return copy


def arrive(dst, recv_sem, device):
    push(dst, dst, recv_sem, recv_sem, device).wait_recv()


def each(first, last, body):
    def step(k, carry):
        body(k)
        return carry

    lax.fori_loop(first, last, step, 0)


class Exchange:
    def __init__(self, src, dst, send, recv, me, device_of, n, whole=False):
        self.src, self.dst, self.send, self.recv = src, dst, send, recv
        self.me, self.device_of, self.n, self.whole = me, device_of, n, whole

    def copy(self, j):
        src = self.src if self.whole else self.src.at[j]
        return push(src, self.dst.at[self.me], self.send.at[j], self.recv.at[self.me], self.device_of(j))

    def start(self):
        def one(k):
            self.copy((self.me + k) % self.n).start()

        each(1, self.n, one)
        self.dst[self.me] = self.src[...] if self.whole else self.src[self.me]

    def wait_all(self):
        def one(k):
            j = (self.me + self.n - k) % self.n
            arrive(self.dst.at[j], self.recv.at[j], self.device_of(j))

        each(1, self.n, one)

    def wait_sent(self):
        def one(k):
            self.copy((self.me + k) % self.n).wait_send()

        each(1, self.n, one)


def rms_rows(values):
    return values * lax.rsqrt(jnp.mean(values * values, axis=-1, keepdims=True) + EPSILON)


def whole_kernel(
    offset_ref, tok_ref, table_ref, q_ref, kv_ref,
    cout_ref, sqkv_ref, sout_ref, in_ref, mout_ref,
    out_ref,
    stage, w_all, tokens, wkv, table_w, tw, sin_ref, cos_ref, rows_sin, rows_cos, waves, products, one_hot, inverse, latent, keys, values, q_own, q_all,
    o_msg, o_came, st_msg, st_came, w_co, w_qkv, w_so, msg, came, own, all_rows, normed, kv, kv_all, msg2, came2,
    own2, all_rows2, w_in, w_out, partial, msg3, came3,
    load, s1, r1, s2, r2, s3, r3, s_q, r_q, s_o, r_o, s_st, r_st, s_m, r_m, s_a, r_a, s_kv, r_kv, s_m2, r_m2,
    s_a2, r_a2, s_m3, r_m3, own_w, sw1, rw1, sw2, rw2, sw3, rw3,
):
    x, a, b, c, y = place()
    k = 2 * b + c
    r = 4 * x + k
    p = 4 * y + a
    j_me = 2 * x + b
    partner = at(x, a, b, 1 - c, y)

    def row_of(j):
        return at(j // 4, a, (j // 2) % 2, j % 2, y)

    def head_of(j):
        return at(x, j % 4, b, c, j // 4)

    def final_of(j):
        return at(x, k, (j // 2) % 2, j % 2, j // 4)

    def sender_of(j):
        return at(x, j % 4, a // 2, a % 2, j // 4)

    final_self = jnp.where(a == k, 4 * y + k, 16)
    sender_self = jnp.where(a == k, p, 16)

    row_at = pl.multiple_of(a * HD, HD)
    loads = [
        pltpu.make_async_copy(cout_ref.at[pl.ds(row_at, HD), :], w_co, load.at[0]),
        pltpu.make_async_copy(sqkv_ref.at[:, :, pl.ds(row_at, HD)], w_qkv, load.at[1]),
        pltpu.make_async_copy(sout_ref.at[pl.ds(row_at, HD), :], w_so, load.at[2]),
    ]
    for copy in loads:
        copy.start()
    barrier = pltpu.get_barrier_semaphore()

    def hello(device):
        pl.semaphore_signal(barrier, inc=1, device_id=device, device_id_type=MESH)

    each(1, 16, lambda i: hello(head_of((p + i) % 16)))

    def hello_sender(j):
        @pl.when(j != sender_self)
        def _():
            hello(sender_of(j))

    each(0, 16, hello_sender)
    each(1, 16, lambda i: hello(row_of((r + i) % 16)))
    for h in range(4):
        stage[h, 0] = q_ref[:, 128 * h : 128 * h + 128]
        stage[h, 1] = kv_ref[0, :, 128 * h : 128 * h + 128]
        stage[h, 2] = kv_ref[1, :, 128 * h : 128 * h + 128]
    offset = offset_ref[0]
    index = lax.broadcasted_iota(jnp.int32, (56, 1), 0)
    places = jnp.where(index < 4, 512 * (16 * x + 4 * index + k), offset + 256 * (index - 4) + 16 * r)
    places = jnp.where(index < 8, places, jnp.where(index < 40, 16 * (index - 8), index - 40)).astype(F32)

    def table_columns(j):
        lanes = pl.ds(pl.multiple_of(j * 256, 256), 256)
        pair = ((j * 256 + lax.broadcasted_iota(jnp.int32, (1, 256), 1)) // 2).astype(F32)
        angles = places * jnp.exp(pair * (-2.0 * math.log(10000.0) / D))
        sin_ref[:, lanes] = jnp.sin(angles)
        cos_ref[:, lanes] = jnp.cos(angles)

    each(0, 8, table_columns)
    odd = lax.broadcasted_iota(jnp.int32, (1, D), 1) % 2 == 1
    mid_sin, mid_cos = sin_ref[8:40], cos_ref[8:40]

    def start_of(n):
        s, co = sin_ref[pl.ds(n, 1)], cos_ref[pl.ds(n, 1)]
        return jnp.where(odd, co, s), jnp.where(odd, -s, co)

    def waves_of(n):
        s, co = start_of(n)
        rows_sin[...] = s * mid_cos + co * mid_sin
        rows_cos[...] = co * mid_cos - s * mid_sin

        def columns(j):
            lanes = pl.ds(pl.multiple_of(j * 128, 128), 128)
            low_sin, low_cos = sin_ref[40:56, lanes], cos_ref[40:56, lanes]
            for m in range(32):
                wave = rows_sin[m : m + 1, lanes] * low_cos + rows_cos[m : m + 1, lanes] * low_sin
                waves[pl.ds(pl.multiple_of(n * 512 + 16 * m, 16), 16), lanes] = wave.astype(BF)

        each(0, 16, columns)

    each(0, 4, waves_of)
    square = table_ref[...].astype(F32)
    square = square * square
    high = square.astype(BF)
    lower = (square - high.astype(F32)).astype(BF)
    ones = jnp.ones((8, D), BF)
    across = (((1,), (1,)), ((), ()))
    norms = lax.dot_general(ones, high, across, preferred_element_type=F32) + lax.dot_general(
        ones, lower, across, preferred_element_type=F32
    )
    norms = norms[0:1]

    def products_of(n):
        run = pl.ds(pl.multiple_of(n * 512, 512), 512)
        products[run, :] = lax.dot_general(waves[run, :], table_ref[...], across, preferred_element_type=F32)

    each(0, 4, products_of)
    pl.semaphore_wait(barrier, jnp.where(a == k, 45, 46))
    ends = []

    heads = [(a + d) % 4 for d in range(1, 4)]
    rows = [((x + dx) % 4, (b + db) % 2) for dx in (0, 1, 3, 2) for db in (0, 1) if dx or db]
    early, late = pl.ds(0, 1), pl.ds(1, 2)

    def begin(copies):
        for copy in copies:
            copy.start()
            ends.append(copy.wait_send)

    begin([push(tok_ref, tokens.at[x, a, k], s1.at[2, h], r1.at[2, a], at(x, h, b, c, y)) for h in heads])
    for n, part in enumerate((early, late)):
        begin(
            [
                push(stage.at[h, part], w_all.at[part, x, a, k], s1.at[n, h], r1.at[n, a], at(x, h, b, c, y))
                for h in heads
            ]
        )
    tokens[x, a, k] = tok_ref[...]
    for part in range(3):
        w_all[part, x, a, k] = stage[a, part]

    for h in heads:
        arrive(tokens.at[x, h, k], r1.at[2, h], partner)
        arrive(w_all.at[early, x, h, k], r1.at[0, h], partner)
        arrive(w_all.at[late, x, h, k], r1.at[1, h], partner)

    def piece(n, rx, rb, core):
        k2 = 2 * rb + core
        if n == 2:
            return tokens.at[rx, :, k2]
        return w_all.at[(early, late)[n], rx, :, k2]

    def along_rows(n):
        return [
            push(piece(n, x, b, c), piece(n, x, b, c), s2.at[n, 2 * rx + rb], r2.at[n, j_me], at(rx, a, rb, c, y))
            for rx, rb in rows
        ]

    def onward(n, rx, rb):
        j = 2 * rx + rb
        return push(piece(n, rx, rb, c), piece(n, rx, rb, c), s3.at[n, j], r3.at[n, j], partner)

    for n in (2, 0, 1):
        begin(along_rows(n) + [onward(n, x, b)])

    vocab = lax.broadcasted_iota(jnp.int32, (128, 256), 1).astype(F32)
    diagonal = lax.broadcasted_iota(jnp.int32, (128, 128), 0) == lax.broadcasted_iota(jnp.int32, (128, 128), 1)

    def scales_of(n):
        here = tokens[x, n, k].astype(F32)
        for q in range(4):
            column = jnp.sum(jnp.where(diagonal, here[q : q + 1, :], 0.0), axis=1, keepdims=True)
            chosen = column == vocab
            quarter = pl.ds(pl.multiple_of(n * 512 + 128 * q, 128), 128)
            one_hot[quarter, :] = chosen.astype(BF)
            total = jnp.sum(
                jnp.where(chosen, 2.0 * products[quarter, :] + norms, 0.0), axis=1, keepdims=True
            )
            total = jnp.maximum(total + D / 2, 0.0)
            inverse[quarter, :] = lax.rsqrt(total * (1.0 / D) + EPSILON)

    each(0, 4, scales_of)

    def hand_on(n, rx, rb):
        arrive(piece(n, rx, rb, c), r2.at[n, 2 * rx + rb], partner)
        begin([onward(n, rx, rb)])

    def handed(n, rx, rb):
        arrive(piece(n, rx, rb, 1 - c), r3.at[n, 2 * rx + rb], partner)

    for rx, rb in rows:
        hand_on(2, (2 * x + 4 - rx) % 4, rb)
        hand_on(0, (2 * x + 4 - rx) % 4, rb)
    for rx, rb in [(x, b)] + rows:
        handed(2, rx, rb)
        handed(0, rx, rb)

    slot = lax.broadcasted_iota(jnp.int32, (64, 1), 0)
    target = offset + (slot // 16) * 256 + 16 * r + slot % 16
    lane = lax.broadcasted_iota(jnp.int32, (1, 128), 1)
    found = jnp.zeros((64, 128), F32)
    for q in range(3):
        bytes_here = tokens[3, 3, 1 + q].astype(F32)
        for t in range(4):
            hit = target == lane + (31232 + 512 * q + 128 * t)
            found = found + jnp.where(hit, bytes_here[t : t + 1, :], 0.0)
    column = jnp.sum(found, axis=1, keepdims=True)
    looked = jnp.dot((column == vocab[:64]).astype(BF), table_ref[...], preferred_element_type=F32)
    for t in range(4):
        s, co = start_of(4 + t)
        wave = s * cos_ref[40:56] + co * sin_ref[40:56]
        latent[16 * t : 16 * t + 16, :] = rms_rows(looked[16 * t : 16 * t + 16] + wave).astype(BF)
    q_own[...] = jnp.dot(latent[...], w_all[0].reshape(D, HD), preferred_element_type=F32).astype(BF)
    asked = Exchange(q_own, q_all, s_q, r_q, r, row_of, 16, whole=True)
    asked.start()

    main = c == y // 2
    source = jnp.logical_and(main, b == y % 2)
    beside = at(x, a, 1 - b, c, y)
    mine = [
        pltpu.make_async_copy(in_ref, w_in.at[x], own_w.at[0]),
        pltpu.make_async_copy(mout_ref, w_out.at[x], own_w.at[1]),
    ]
    step1 = [
        push(in_ref, w_in.at[x], sw1.at[0], rw1.at[0], beside),
        push(mout_ref, w_out.at[x], sw1.at[1], rw1.at[1], beside),
    ]

    def set_first():
        @pl.when(source)
        def _():
            for copy in step1 + mine:
                copy.start()

    for d in (0, 1, 3, 2):
        sx = (x + d) % 4
        if d == 0:
            hand_on(1, x, 1 - b)
            handed(1, x, b)
            handed(1, x, 1 - b)
        else:
            for rb in (0, 1):
                hand_on(1, sx, rb)
            for rb in (0, 1):
                handed(1, sx, rb)
        if d == 2:
            ends.append(asked.wait_sent)
        if d == 2:
            set_first()
        wkv[:, :HD] = w_all[1, sx].reshape(512, HD)
        wkv[:, HD:] = w_all[2, sx].reshape(512, HD)
        features = pl.ds(pl.multiple_of(512 * sx, 512), 512)

        def add_to(n):
            run = pl.ds(pl.multiple_of(n * 512, 512), 512)
            part = jnp.dot(waves[run, features], wkv[...], preferred_element_type=F32)
            products[run, :] = part if d == 0 else products[run, :] + part

        each(0, 4, add_to)
        part = jnp.dot(table_ref[:, features], wkv[...], preferred_element_type=F32)
        table_w[...] = part if d == 0 else table_w[...] + part
    high = table_w[...].astype(BF)
    tw[0] = high
    tw[1] = (table_w[...] - high.astype(F32)).astype(BF)

    def keys_of(n):
        run = pl.ds(pl.multiple_of(n * 512, 512), 512)
        both = products[run, :] + jnp.dot(one_hot[run, :], tw[0], preferred_element_type=F32)
        both = both + jnp.dot(one_hot[run, :], tw[1], preferred_element_type=F32)
        both = (both * inverse[run, :]).astype(BF)
        keys[run, :] = both[:, :HD]
        values[run, :] = both[:, HD:]

    each(0, 4, keys_of)
    asked.wait_all()

    key_col = lax.broadcasted_iota(jnp.int32, (1, 2048), 1)
    key_place = 512 * (16 * x + 4 * (key_col // 512) + k) + key_col % 512
    outs = Exchange(o_msg, o_came, s_o, r_o, r, row_of, 16)
    stats = Exchange(st_msg, st_came, s_st, r_st, r, row_of, 16)
    diagonal64 = lax.broadcasted_iota(jnp.int32, (64, 128), 0) == lax.broadcasted_iota(jnp.int32, (64, 128), 1)

    def attend(step):
        t = (x + 1 + step) % 4
        query = q_all[pl.ds(4 * t, 4)].reshape(256, HD)
        scores = lax.dot_general(query, keys[...], across, preferred_element_type=F32) * SCALE
        row = lax.broadcasted_iota(jnp.int32, (256, 1), 0)
        row_place = offset + ((row // 16) % 4) * 256 + 16 * (4 * t + row // 64) + row % 16
        scores = jnp.where(key_place > row_place, MASKED, scores)
        peak = jnp.max(scores, axis=1, keepdims=True)
        weights = jnp.exp(scores - peak).astype(BF)
        total = jnp.sum(weights.astype(F32), axis=1, keepdims=True)
        out = jnp.dot(weights, values[...], preferred_element_type=F32).astype(BF)
        for g in range(4):
            some = slice(64 * g, 64 * g + 64)
            j = 4 * t + g
            o_msg[j] = out[some]
            st_msg[j, 0:1, :] = jnp.sum(jnp.where(diagonal64, peak[some], 0.0), axis=0, keepdims=True)
            st_msg[j, 1:2, :] = jnp.sum(jnp.where(diagonal64, total[some], 0.0), axis=0, keepdims=True)

            @pl.when(j != r)
            def _():
                stats.copy(j).start()
                outs.copy(j).start()

    each(0, 4, attend)
    o_came[r] = o_msg[r]
    st_came[r] = st_msg[r]
    stats.wait_all()
    outs.wait_all()
    ends += [stats.wait_sent, outs.wait_sent]

    halves = (w_in, w_out)
    others = [(x + d) % 4 for d in (1, 3, 2)]

    def along(h):
        copies = [push(halves[h].at[x], halves[h].at[x], sw2.at[h, i], rw2.at[h, x], at(i, a, b, c, y)) for i in others]
        return copies + [forward(h, x)]

    def forward(h, i):
        return push(halves[h].at[i], halves[h].at[i], sw3.at[h, i], rw3.at[h, i], partner)

    def set_out(h):
        @pl.when(source)
        def _():
            mine[h].wait()

        @pl.when(jnp.logical_and(main, jnp.logical_not(source)))
        def _():
            arrive(halves[h].at[x], rw1.at[h], partner)

        @pl.when(main)
        def _():
            for copy in along(h):
                copy.start()

    def hand_over(h):
        @pl.when(main)
        def _():
            for i in others:
                arrive(halves[h].at[i], rw2.at[h, i], partner)
                forward(h, i).start()

    def receive(h):
        @pl.when(jnp.logical_not(main))
        def _():
            for i in range(4):
                arrive(halves[h].at[i], rw3.at[h, i], partner)

    set_out(0)

    maxima, totals = st_came[:, 0, :], st_came[:, 1, :]
    factor = jnp.exp(maxima - jnp.max(maxima, axis=0, keepdims=True))
    factor = factor / jnp.sum(factor * totals, axis=0, keepdims=True)
    attended = jnp.zeros((64, HD), F32)
    for j in range(16):
        column = jnp.sum(jnp.where(diagonal64, factor[j : j + 1, :], 0.0), axis=1, keepdims=True)
        attended = attended + column * o_came[j].astype(F32)
    for copy in loads:
        copy.wait()

    def shares(rows, weight, out):
        for q in range(4):
            part = jnp.dot(rows, weight[:, 512 * q : 512 * q + 512], preferred_element_type=F32).astype(BF)
            for t in range(4):
                out[4 * t + q] = part[16 * t : 16 * t + 16]

    def rows_normed(blocks):
        for t in range(4):
            wide = jnp.concatenate([blocks[4 * t + q] for q in range(4)], axis=1).astype(F32)
            normed[16 * t : 16 * t + 16, :] = rms_rows(wide).astype(BF)

    shares(attended.astype(BF), w_co, msg)
    summed = Exchange(msg, came, s_m, r_m, p, head_of, 16)
    summed.start()
    own_block = (pl.ds(pl.multiple_of(16 * y, 16), 16), pl.ds(pl.multiple_of(512 * a, 512), 512))
    own_latent = latent[own_block].astype(F32)
    summed.wait_all()
    ends.append(summed.wait_sent)
    first = jnp.sum(came[...].astype(F32), axis=0) + own_latent
    own[...] = first.astype(BF)
    spread = Exchange(own, all_rows, s_a, r_a, p, head_of, 16, whole=True)
    spread.start()
    spread.wait_all()
    ends.append(spread.wait_sent)

    rows_normed(all_rows)
    kv[:, :HD] = jnp.dot(normed[...], w_qkv[1], preferred_element_type=F32).astype(BF)
    kv[:, HD:] = jnp.dot(normed[...], w_qkv[2], preferred_element_type=F32).astype(BF)
    both = Exchange(kv, kv_all, s_kv, r_kv, r, row_of, 16, whole=True)
    both.start()
    query = jnp.dot(normed[...], w_qkv[0], preferred_element_type=F32).astype(BF)
    both.wait_all()
    ends.append(both.wait_sent)

    set_out(1)
    hand_over(0)
    all_keys = kv_all[:, :, :HD].reshape(LATENTS, HD)
    all_values = kv_all[:, :, HD:].reshape(LATENTS, HD)
    scores = lax.dot_general(query, all_keys, across, preferred_element_type=F32) * SCALE
    row = lax.broadcasted_iota(jnp.int32, (64, 1), 0)
    col = lax.broadcasted_iota(jnp.int32, (1, LATENTS), 1)
    row_place = (row // 16) * 256 + 16 * r + row % 16
    col_place = ((col // 16) % 4) * 256 + 16 * (col // 64) + col % 16
    scores = jnp.where(col_place > row_place, MASKED, scores)
    weights = jnp.exp(scores - jnp.max(scores, axis=1, keepdims=True)).astype(BF)
    total = jnp.sum(weights.astype(F32), axis=1, keepdims=True)
    attended = jnp.dot(weights, all_values, preferred_element_type=F32) / total
    shares(attended.astype(BF), w_so, msg2)
    summed2 = Exchange(msg2, came2, s_m2, r_m2, p, head_of, 16)
    summed2.start()
    summed2.wait_all()
    ends.append(summed2.wait_sent)
    second = first + jnp.sum(came2[...].astype(F32), axis=0)
    own2[...] = second.astype(BF)
    spread2 = Exchange(own2, all_rows2, s_a2, r_a2, p, head_of, 16, whole=True)
    spread2.start()
    hand_over(1)

    spread2.wait_all()
    ends.append(spread2.wait_sent)

    rows_normed(all_rows2)
    receive(0)
    hidden = []
    for i in range(4):
        pre = jnp.dot(normed[...], w_in[i], preferred_element_type=F32)
        hidden.append(jax.nn.gelu(pre, approximate=True).astype(BF))
    hidden = jnp.concatenate(hidden, axis=1)
    receive(1)
    for q in range(4):
        columns = slice(512 * q, 512 * q + 512)
        partial[q] = jnp.dot(hidden, w_out[:, :, columns].reshape(512, 512), preferred_element_type=F32)
    here = pl.ds(pl.multiple_of(16 * y, 16), 16)
    partial[a, here, :] = partial[a, here, :] + second
    for j in range(16):
        some = slice(4 * j, 4 * j + 4)
        msg3[j] = jnp.concatenate([partial[q, some, :] for q in range(4)], axis=0).astype(BF)

    def last_copy(j):
        return push(msg3.at[j], came3.at[p], s_m3.at[j], r_m3.at[p], final_of(j))

    def last_start(i):
        j = (p + i) % 16

        @pl.when(j != final_self)
        def _():
            last_copy(j).start()

    each(0, 16, last_start)

    @pl.when(a == k)
    def _():
        came3[p] = msg3[4 * y + k]

    def last_wait(i):
        j = (p + i) % 16

        @pl.when(j != sender_self)
        def _():
            arrive(came3.at[j], r_m3.at[j], partner)

    each(0, 16, last_wait)
    ended = jnp.sum(came3[...].astype(F32), axis=0)
    for q in range(4):
        out_ref[:, 512 * q : 512 * q + 512] = ended[4 * q : 4 * q + 4]

    for end in ends:
        end()

    def last_sent(i):
        j = (p + i) % 16

        @pl.when(j != final_self)
        def _():
            last_copy(j).wait_send()

    each(0, 16, last_sent)

    @pl.when(source)
    def _():
        for copy in step1:
            copy.wait_send()

    @pl.when(main)
    def _():
        for h in range(2):
            for copy in along(h):
                copy.wait_send()
            for i in others:
                forward(h, i).wait_send()


def per_device(
    token_ids,
    latent_offset,
    embed_table,
    cross_q,
    cross_kv,
    cross_out,
    self_qkv,
    self_out,
    mlp_in,
    mlp_out,
):
    vmem = pl.BlockSpec(memory_space=pltpu.VMEM)
    hbm = pl.BlockSpec(memory_space=pl.ANY)
    dma = pltpu.SemaphoreType.DMA
    rows = pl.pallas_call(
        whole_kernel,
        out_shape=jax.ShapeDtypeStruct((4, D), F32),
        in_specs=[pl.BlockSpec(memory_space=pltpu.SMEM)] + [vmem] * 4 + [hbm] * 5,
        out_specs=vmem,
        scratch_shapes=[
            pltpu.VMEM((4, 3, 32, HD), BF),
            pltpu.VMEM((3, 4, 4, 4, 32, HD), BF),
            pltpu.VMEM((4, 4, 4, 4, 128), jnp.int32),
            pltpu.VMEM((512, 2 * HD), BF),
            pltpu.VMEM((256, 2 * HD), F32),
            pltpu.VMEM((2, 256, 2 * HD), BF),
            pltpu.VMEM((56, D), F32),
            pltpu.VMEM((56, D), F32),
            pltpu.VMEM((32, D), F32),
            pltpu.VMEM((32, D), F32),
            pltpu.VMEM((2048, D), BF),
            pltpu.VMEM((2048, 256), F32),
            pltpu.VMEM((2048, 256), BF),
            pltpu.VMEM((2048, 1), F32),
            pltpu.VMEM((64, D), BF),
            pltpu.VMEM((2048, HD), BF),
            pltpu.VMEM((2048, HD), BF),
            pltpu.VMEM((64, HD), BF),
            pltpu.VMEM((16, 64, HD), BF),
            pltpu.VMEM((16, 64, HD), BF),
            pltpu.VMEM((16, 64, HD), BF),
            pltpu.VMEM((16, 8, 128), F32),
            pltpu.VMEM((16, 8, 128), F32),
            pltpu.VMEM((HD, D), BF),
            pltpu.VMEM((3, D, HD), BF),
            pltpu.VMEM((HD, D), BF),
            pltpu.VMEM((16, 16, 512), BF),
            pltpu.VMEM((16, 16, 512), BF),
            pltpu.VMEM((16, 512), BF),
            pltpu.VMEM((16, 16, 512), BF),
            pltpu.VMEM((64, D), BF),
            pltpu.VMEM((64, 2 * HD), BF),
            pltpu.VMEM((16, 64, 2 * HD), BF),
            pltpu.VMEM((16, 16, 512), BF),
            pltpu.VMEM((16, 16, 512), BF),
            pltpu.VMEM((16, 512), BF),
            pltpu.VMEM((16, 16, 512), BF),
            pltpu.VMEM((4, D, HD), BF),
            pltpu.VMEM((4, HD, D), BF),
            pltpu.VMEM((4, 64, 512), F32),
            pltpu.VMEM((16, 16, 512), BF),
            pltpu.VMEM((16, 16, 512), BF),
            dma((3,)),
            dma((3, 4)),
            dma((3, 4)),
            dma((3, 8)),
            dma((3, 8)),
            dma((3, 8)),
            dma((3, 8)),
        ]
        + [dma((16,))] * 18
        + [dma((2,)), dma((2,)), dma((2,)), dma((2, 4)), dma((2, 4)), dma((2, 4)), dma((2, 4))],
        compiler_params=pltpu.CompilerParams(
            collective_id=0, has_side_effects=True, vmem_limit_bytes=VLIMIT
        ),
    )(
        latent_offset, token_ids.reshape(4, 128), embed_table,
        cross_q, cross_kv, cross_out, self_qkv, self_out, mlp_in, mlp_out,
    )
    return rows.astype(BF)[None]


def solution(mesh):
    placed = (
        P("ctx"),
        P(),
        P(),
        P("ctx", "lat"),
        P(None, "ctx", "lat"),
        P("lat", None),
        P(None, None, "lat"),
        P("lat", None),
        P(None, "ctx"),
        P("ctx", None),
    )
    return jax.shard_map(
        per_device, mesh=mesh, in_specs=placed, out_specs=P("lat", "ctx", None), check_vma=False
    )
```

```python
import math

import jax
import jax.numpy as jnp
from jax import lax
from jax.experimental import pallas as pl
from jax.experimental.pallas import tpu as pltpu
from jax.sharding import PartitionSpec as P

MESH = pl.DeviceIdType.MESH
HD = 128
D = 2048
LATENTS = 1024
EPSILON = 1e-06
MASKED = -1e30
SCALE = 1.0 / math.sqrt(HD)
BF = jnp.bfloat16
F32 = jnp.float32
VLIMIT = 58 * 1024 * 1024


def place():
    g = lax.axis_index("ctx")
    y = lax.axis_index("lat")
    return g // 16, (g // 4) % 4, (g // 2) % 2, g % 2, y


def at(x, a, b, c, y):
    return (16 * x + 4 * a + 2 * b + c, y)


def push(src, dst, send_sem, recv_sem, device):
    copy = pltpu.make_async_remote_copy(
        src_ref=src,
        dst_ref=dst,
        send_sem=send_sem,
        recv_sem=recv_sem,
        device_id=device,
        device_id_type=MESH,
    )
    return copy


def arrive(dst, recv_sem, device):
    push(dst, dst, recv_sem, recv_sem, device).wait_recv()


def each(first, last, body):
    def step(k, carry):
        body(k)
        return carry

    lax.fori_loop(first, last, step, 0)


class Exchange:
    def __init__(self, src, dst, send, recv, me, device_of, n, whole=False):
        self.src, self.dst, self.send, self.recv = src, dst, send, recv
        self.me, self.device_of, self.n, self.whole = me, device_of, n, whole

    def copy(self, j):
        src = self.src if self.whole else self.src.at[j]
        return push(src, self.dst.at[self.me], self.send.at[j], self.recv.at[self.me], self.device_of(j))

    def start(self):
        def one(k):
            self.copy((self.me + k) % self.n).start()

        each(1, self.n, one)
        self.dst[self.me] = self.src[...] if self.whole else self.src[self.me]

    def wait_all(self):
        def one(k):
            j = (self.me + self.n - k) % self.n
            arrive(self.dst.at[j], self.recv.at[j], self.device_of(j))

        each(1, self.n, one)

    def wait_sent(self):
        def one(k):
            self.copy((self.me + k) % self.n).wait_send()

        each(1, self.n, one)


def rms_rows(values):
    return values * lax.rsqrt(jnp.mean(values * values, axis=-1, keepdims=True) + EPSILON)


def whole_kernel(
    offset_ref, tok_ref, q_ref, kv_ref,
    table_hbm, cout_ref, sqkv_ref, sout_ref, in_ref, mout_ref,
    out_ref,
    table_ref, stage, w_all, tokens, wkv, tw, sin_ref, cos_ref, rows_sin, rows_cos, waves, products, one_hot, inverse, latent, keys, values, q_own, q_all,
    o_msg, o_came, st_msg, st_came, w_co, w_qkv, w_so, msg, came, own, all_rows, normed, kv, kv_all, msg2, came2,
    own2, all_rows2, w_in, w_out, partial, msg3, came3,
    load, s1, r1, s2, r2, s3, r3, s_q, r_q, s_o, r_o, s_st, r_st, s_m, r_m, s_a, r_a, s_kv, r_kv, s_m2, r_m2,
    s_a2, r_a2, s_m3, r_m3, own_w, sw1, rw1, sw2, rw2, sw3, rw3,
):
    x, a, b, c, y = place()
    k = 2 * b + c
    r = 4 * x + k
    p = 4 * y + a
    j_me = 2 * x + b
    partner = at(x, a, b, 1 - c, y)

    def row_of(j):
        return at(j // 4, a, (j // 2) % 2, j % 2, y)

    def head_of(j):
        return at(x, j % 4, b, c, j // 4)

    def final_of(j):
        return at(x, k, (j // 2) % 2, j % 2, j // 4)

    def sender_of(j):
        return at(x, j % 4, a // 2, a % 2, j // 4)

    final_self = jnp.where(a == k, 4 * y + k, 16)
    sender_self = jnp.where(a == k, p, 16)

    barrier = pltpu.get_barrier_semaphore()

    def hello(device):
        pl.semaphore_signal(barrier, inc=1, device_id=device, device_id_type=MESH)

    each(1, 16, lambda i: hello(row_of((r + i) % 16)))
    each(1, 16, lambda i: hello(head_of((p + i) % 16)))

    def hello_sender(j):
        @pl.when(j != sender_self)
        def _():
            hello(sender_of(j))

    each(0, 16, hello_sender)
    row_at = pl.multiple_of(a * HD, HD)
    table_load = pltpu.make_async_copy(table_hbm, table_ref, load.at[3])
    table_load.start()
    loads = [
        pltpu.make_async_copy(cout_ref.at[pl.ds(row_at, HD), :], w_co, load.at[0]),
        pltpu.make_async_copy(sqkv_ref.at[:, :, pl.ds(row_at, HD)], w_qkv, load.at[1]),
        pltpu.make_async_copy(sout_ref.at[pl.ds(row_at, HD), :], w_so, load.at[2]),
    ]
    for copy in loads:
        copy.start()
    for h in range(4):
        stage[h, 0] = q_ref[:, 128 * h : 128 * h + 128]
        stage[h, 1] = kv_ref[0, :, 128 * h : 128 * h + 128]
        stage[h, 2] = kv_ref[1, :, 128 * h : 128 * h + 128]
    pl.semaphore_wait(barrier, jnp.where(a == k, 45, 46))
    ends = []

    heads = [(a + d) % 4 for d in range(1, 4)]
    rows = [((x + dx) % 4, (b + db) % 2) for dx in (0, 1, 3, 2) for db in (0, 1) if dx or db]
    first_copies = []
    for h in heads:
        there = at(x, h, b, c, y)
        first_copies.append(push(tok_ref, tokens.at[x, a, k], s1.at[1, h], r1.at[1, a], there))
        first_copies.append(push(stage.at[h], w_all.at[:, x, a, k], s1.at[0, h], r1.at[0, a], there))
    for copy in first_copies:
        copy.start()
        ends.append(copy.wait_send)
    tokens[x, a, k] = tok_ref[...]
    for part in range(3):
        w_all[part, x, a, k] = stage[a, part]

    offset = offset_ref[0]
    index = lax.broadcasted_iota(jnp.int32, (56, 1), 0)
    places = jnp.where(index < 4, 512 * (16 * x + 4 * index + k), offset + 256 * (index - 4) + 16 * r)
    places = jnp.where(index < 8, places, jnp.where(index < 40, 16 * (index - 8), index - 40)).astype(F32)

    def table_columns(j):
        lanes = pl.ds(pl.multiple_of(j * 256, 256), 256)
        pair = ((j * 256 + lax.broadcasted_iota(jnp.int32, (1, 256), 1)) // 2).astype(F32)
        angles = places * jnp.exp(pair * (-2.0 * math.log(10000.0) / D))
        sin_ref[:, lanes] = jnp.sin(angles)
        cos_ref[:, lanes] = jnp.cos(angles)

    each(0, 8, table_columns)

    for h in heads:
        arrive(tokens.at[x, h, k], r1.at[1, h], partner)
        arrive(w_all.at[:, x, h, k], r1.at[0, h], partner)
    second_copies = []
    for rx, rb in rows:
        there = at(rx, a, rb, c, y)
        j = 2 * rx + rb
        second_copies.append(push(tokens.at[x, :, k], tokens.at[x, :, k], s2.at[1, j], r2.at[1, j_me], there))
        second_copies.append(push(w_all.at[:, x, :, k], w_all.at[:, x, :, k], s2.at[0, j], r2.at[0, j_me], there))
    for copy in second_copies:
        copy.start()
        ends.append(copy.wait_send)

    def onward(rx, rb):
        j = 2 * rx + rb
        k2 = 2 * rb + c
        return [
            push(tokens.at[rx, :, k2], tokens.at[rx, :, k2], s3.at[1, j], r3.at[1, j], partner),
            push(w_all.at[:, rx, :, k2], w_all.at[:, rx, :, k2], s3.at[0, j], r3.at[0, j], partner),
        ]

    third_copies = onward(x, b)
    for copy in third_copies:
        copy.start()
        ends.append(copy.wait_send)

    odd = lax.broadcasted_iota(jnp.int32, (1, D), 1) % 2 == 1
    mid_sin, mid_cos = sin_ref[8:40], cos_ref[8:40]

    def start_of(n):
        s, co = sin_ref[pl.ds(n, 1)], cos_ref[pl.ds(n, 1)]
        return jnp.where(odd, co, s), jnp.where(odd, -s, co)

    def waves_of(n):
        s, co = start_of(n)
        rows_sin[...] = s * mid_cos + co * mid_sin
        rows_cos[...] = co * mid_cos - s * mid_sin

        def columns(j):
            lanes = pl.ds(pl.multiple_of(j * 128, 128), 128)
            low_sin, low_cos = sin_ref[40:56, lanes], cos_ref[40:56, lanes]
            for m in range(32):
                wave = rows_sin[m : m + 1, lanes] * low_cos + rows_cos[m : m + 1, lanes] * low_sin
                waves[pl.ds(pl.multiple_of(n * 512 + 16 * m, 16), 16), lanes] = wave.astype(BF)

        each(0, 16, columns)

    each(0, 4, waves_of)

    table_load.wait()
    square = table_ref[...].astype(F32)
    square = square * square
    high = square.astype(BF)
    lower = (square - high.astype(F32)).astype(BF)
    ones = jnp.ones((8, D), BF)
    across = (((1,), (1,)), ((), ()))
    norms = lax.dot_general(ones, high, across, preferred_element_type=F32) + lax.dot_general(
        ones, lower, across, preferred_element_type=F32
    )
    norms = norms[0:1]

    def products_of(n):
        run = pl.ds(pl.multiple_of(n * 512, 512), 512)
        products[run, :] = lax.dot_general(waves[run, :], table_ref[...], across, preferred_element_type=F32)

    each(0, 4, products_of)

    vocab = lax.broadcasted_iota(jnp.int32, (128, 256), 1).astype(F32)
    diagonal = lax.broadcasted_iota(jnp.int32, (128, 128), 0) == lax.broadcasted_iota(jnp.int32, (128, 128), 1)

    def scales_of(n):
        here = tokens[x, n, k].astype(F32)
        for q in range(4):
            column = jnp.sum(jnp.where(diagonal, here[q : q + 1, :], 0.0), axis=1, keepdims=True)
            chosen = column == vocab
            quarter = pl.ds(pl.multiple_of(n * 512 + 128 * q, 128), 128)
            one_hot[quarter, :] = chosen.astype(BF)
            total = jnp.sum(
                jnp.where(chosen, 2.0 * products[quarter, :] + norms, 0.0), axis=1, keepdims=True
            )
            total = jnp.maximum(total + D / 2, 0.0)
            inverse[quarter, :] = lax.rsqrt(total * (1.0 / D) + EPSILON)

    each(0, 4, scales_of)

    for rx, rb in rows:
        sx, sb = (2 * x + 4 - rx) % 4, rb
        j = 2 * sx + sb
        k2 = 2 * sb + c
        arrive(tokens.at[sx, :, k2], r2.at[1, j], partner)
        arrive(w_all.at[:, sx, :, k2], r2.at[0, j], partner)
        more = onward(sx, sb)
        for copy in more:
            copy.start()
            ends.append(copy.wait_send)
    for rx, rb in [(x, b)] + rows:
        j = 2 * rx + rb
        k3 = 2 * rb + 1 - c
        arrive(tokens.at[rx, :, k3], r3.at[1, j], partner)
        arrive(w_all.at[:, rx, :, k3], r3.at[0, j], partner)

    slot = lax.broadcasted_iota(jnp.int32, (64, 1), 0)
    target = offset + (slot // 16) * 256 + 16 * r + slot % 16
    lane = lax.broadcasted_iota(jnp.int32, (1, 128), 1)
    found = jnp.zeros((64, 128), F32)
    for q in range(3):
        bytes_here = tokens[3, 3, 1 + q].astype(F32)
        for t in range(4):
            hit = target == lane + (31232 + 512 * q + 128 * t)
            found = found + jnp.where(hit, bytes_here[t : t + 1, :], 0.0)
    column = jnp.sum(found, axis=1, keepdims=True)
    looked = jnp.dot((column == vocab[:64]).astype(BF), table_ref[...], preferred_element_type=F32)
    for t in range(4):
        s, co = start_of(4 + t)
        wave = s * cos_ref[40:56] + co * sin_ref[40:56]
        latent[16 * t : 16 * t + 16, :] = rms_rows(looked[16 * t : 16 * t + 16] + wave).astype(BF)
    weights_of = w_all.reshape(3, D, HD)
    q_own[...] = jnp.dot(latent[...], weights_of[0], preferred_element_type=F32).astype(BF)
    asked = Exchange(q_own, q_all, s_q, r_q, r, row_of, 16, whole=True)
    asked.start()
    ends.append(asked.wait_sent)

    main = c == y // 2
    source = jnp.logical_and(main, b == y % 2)
    beside = at(x, a, 1 - b, c, y)
    mine = [
        pltpu.make_async_copy(in_ref, w_in.at[x], own_w.at[0]),
        pltpu.make_async_copy(mout_ref, w_out.at[x], own_w.at[1]),
    ]
    step1 = [
        push(in_ref, w_in.at[x], sw1.at[0], rw1.at[0], beside),
        push(mout_ref, w_out.at[x], sw1.at[1], rw1.at[1], beside),
    ]

    @pl.when(source)
    def _():
        for copy in step1 + mine:
            copy.start()


    wkv[:, :HD] = weights_of[1]
    wkv[:, HD:] = weights_of[2]
    table_w = jnp.dot(table_ref[...], wkv[...], preferred_element_type=F32)
    tw[0] = table_w.astype(BF)
    tw[1] = (table_w - table_w.astype(BF).astype(F32)).astype(BF)

    def keys_of(n):
        run = pl.ds(pl.multiple_of(n * 512, 512), 512)
        both = jnp.dot(waves[run, :], wkv[...], preferred_element_type=F32)
        both = both + jnp.dot(one_hot[run, :], tw[0], preferred_element_type=F32)
        both = both + jnp.dot(one_hot[run, :], tw[1], preferred_element_type=F32)
        both = (both * inverse[run, :]).astype(BF)
        keys[run, :] = both[:, :HD]
        values[run, :] = both[:, HD:]

    each(0, 4, keys_of)
    asked.wait_all()

    key_col = lax.broadcasted_iota(jnp.int32, (1, 2048), 1)
    key_place = 512 * (16 * x + 4 * (key_col // 512) + k) + key_col % 512
    outs = Exchange(o_msg, o_came, s_o, r_o, r, row_of, 16)
    stats = Exchange(st_msg, st_came, s_st, r_st, r, row_of, 16)
    diagonal64 = lax.broadcasted_iota(jnp.int32, (64, 128), 0) == lax.broadcasted_iota(jnp.int32, (64, 128), 1)

    def attend(step):
        t = (x + 1 + step) % 4
        query = q_all[pl.ds(4 * t, 4)].reshape(256, HD)
        scores = lax.dot_general(query, keys[...], across, preferred_element_type=F32) * SCALE
        row = lax.broadcasted_iota(jnp.int32, (256, 1), 0)
        row_place = offset + ((row // 16) % 4) * 256 + 16 * (4 * t + row // 64) + row % 16
        scores = jnp.where(key_place > row_place, MASKED, scores)
        peak = jnp.max(scores, axis=1, keepdims=True)
        weights = jnp.exp(scores - peak).astype(BF)
        total = jnp.sum(weights.astype(F32), axis=1, keepdims=True)
        out = jnp.dot(weights, values[...], preferred_element_type=F32).astype(BF)
        for g in range(4):
            some = slice(64 * g, 64 * g + 64)
            j = 4 * t + g
            o_msg[j] = out[some]
            st_msg[j, 0:1, :] = jnp.sum(jnp.where(diagonal64, peak[some], 0.0), axis=0, keepdims=True)
            st_msg[j, 1:2, :] = jnp.sum(jnp.where(diagonal64, total[some], 0.0), axis=0, keepdims=True)

            @pl.when(j != r)
            def _():
                stats.copy(j).start()
                outs.copy(j).start()

    each(0, 4, attend)
    o_came[r] = o_msg[r]
    st_came[r] = st_msg[r]
    stats.wait_all()
    outs.wait_all()
    ends += [stats.wait_sent, outs.wait_sent]

    halves = (w_in, w_out)
    others = [(x + d) % 4 for d in (1, 3, 2)]

    def along(h):
        copies = [push(halves[h].at[x], halves[h].at[x], sw2.at[h, i], rw2.at[h, x], at(i, a, b, c, y)) for i in others]
        return copies + [forward(h, x)]

    def forward(h, i):
        return push(halves[h].at[i], halves[h].at[i], sw3.at[h, i], rw3.at[h, i], partner)

    def set_out(h):
        @pl.when(source)
        def _():
            mine[h].wait()

        @pl.when(jnp.logical_and(main, jnp.logical_not(source)))
        def _():
            arrive(halves[h].at[x], rw1.at[h], partner)

        @pl.when(main)
        def _():
            for copy in along(h):
                copy.start()

    def hand_over(h):
        @pl.when(main)
        def _():
            for i in others:
                arrive(halves[h].at[i], rw2.at[h, i], partner)
                forward(h, i).start()

    def receive(h):
        @pl.when(jnp.logical_not(main))
        def _():
            for i in range(4):
                arrive(halves[h].at[i], rw3.at[h, i], partner)

    maxima, totals = st_came[:, 0, :], st_came[:, 1, :]
    factor = jnp.exp(maxima - jnp.max(maxima, axis=0, keepdims=True))
    factor = factor / jnp.sum(factor * totals, axis=0, keepdims=True)
    attended = jnp.zeros((64, HD), F32)
    for j in range(16):
        column = jnp.sum(jnp.where(diagonal64, factor[j : j + 1, :], 0.0), axis=1, keepdims=True)
        attended = attended + column * o_came[j].astype(F32)
    for copy in loads:
        copy.wait()

    def shares(rows, weight, out):
        for q in range(4):
            part = jnp.dot(rows, weight[:, 512 * q : 512 * q + 512], preferred_element_type=F32).astype(BF)
            for t in range(4):
                out[4 * t + q] = part[16 * t : 16 * t + 16]

    def rows_normed(blocks):
        for t in range(4):
            wide = jnp.concatenate([blocks[4 * t + q] for q in range(4)], axis=1).astype(F32)
            normed[16 * t : 16 * t + 16, :] = rms_rows(wide).astype(BF)

    shares(attended.astype(BF), w_co, msg)
    summed = Exchange(msg, came, s_m, r_m, p, head_of, 16)
    summed.start()
    set_out(0)
    own_block = (pl.ds(pl.multiple_of(16 * y, 16), 16), pl.ds(pl.multiple_of(512 * a, 512), 512))
    own_latent = latent[own_block].astype(F32)
    summed.wait_all()
    ends.append(summed.wait_sent)
    first = jnp.sum(came[...].astype(F32), axis=0) + own_latent
    own[...] = first.astype(BF)
    spread = Exchange(own, all_rows, s_a, r_a, p, head_of, 16, whole=True)
    spread.start()
    set_out(1)
    spread.wait_all()
    ends.append(spread.wait_sent)

    rows_normed(all_rows)
    kv[:, :HD] = jnp.dot(normed[...], w_qkv[1], preferred_element_type=F32).astype(BF)
    kv[:, HD:] = jnp.dot(normed[...], w_qkv[2], preferred_element_type=F32).astype(BF)
    both = Exchange(kv, kv_all, s_kv, r_kv, r, row_of, 16, whole=True)
    both.start()
    hand_over(0)
    query = jnp.dot(normed[...], w_qkv[0], preferred_element_type=F32).astype(BF)
    both.wait_all()
    ends.append(both.wait_sent)

    all_keys = kv_all[:, :, :HD].reshape(LATENTS, HD)
    all_values = kv_all[:, :, HD:].reshape(LATENTS, HD)
    scores = lax.dot_general(query, all_keys, across, preferred_element_type=F32) * SCALE
    row = lax.broadcasted_iota(jnp.int32, (64, 1), 0)
    col = lax.broadcasted_iota(jnp.int32, (1, LATENTS), 1)
    row_place = (row // 16) * 256 + 16 * r + row % 16
    col_place = ((col // 16) % 4) * 256 + 16 * (col // 64) + col % 16
    scores = jnp.where(col_place > row_place, MASKED, scores)
    weights = jnp.exp(scores - jnp.max(scores, axis=1, keepdims=True)).astype(BF)
    total = jnp.sum(weights.astype(F32), axis=1, keepdims=True)
    attended = jnp.dot(weights, all_values, preferred_element_type=F32) / total
    shares(attended.astype(BF), w_so, msg2)
    summed2 = Exchange(msg2, came2, s_m2, r_m2, p, head_of, 16)
    summed2.start()
    hand_over(1)
    summed2.wait_all()
    ends.append(summed2.wait_sent)
    second = first + jnp.sum(came2[...].astype(F32), axis=0)
    own2[...] = second.astype(BF)
    spread2 = Exchange(own2, all_rows2, s_a2, r_a2, p, head_of, 16, whole=True)
    spread2.start()

    spread2.wait_all()
    ends.append(spread2.wait_sent)

    rows_normed(all_rows2)
    receive(0)
    hidden = []
    for i in range(4):
        pre = jnp.dot(normed[...], w_in[i], preferred_element_type=F32)
        hidden.append(jax.nn.gelu(pre, approximate=True).astype(BF))
    hidden = jnp.concatenate(hidden, axis=1)
    receive(1)
    for q in range(4):
        columns = slice(512 * q, 512 * q + 512)
        partial[q] = jnp.dot(hidden, w_out[:, :, columns].reshape(512, 512), preferred_element_type=F32)
    here = pl.ds(pl.multiple_of(16 * y, 16), 16)
    partial[a, here, :] = partial[a, here, :] + second
    for j in range(16):
        some = slice(4 * j, 4 * j + 4)
        msg3[j] = jnp.concatenate([partial[q, some, :] for q in range(4)], axis=0).astype(BF)

    def last_copy(j):
        return push(msg3.at[j], came3.at[p], s_m3.at[j], r_m3.at[p], final_of(j))

    def last_start(i):
        j = (p + i) % 16

        @pl.when(j != final_self)
        def _():
            last_copy(j).start()

    each(0, 16, last_start)

    @pl.when(a == k)
    def _():
        came3[p] = msg3[4 * y + k]

    def last_wait(i):
        j = (p + i) % 16

        @pl.when(j != sender_self)
        def _():
            arrive(came3.at[j], r_m3.at[j], partner)

    each(0, 16, last_wait)
    ended = jnp.sum(came3[...].astype(F32), axis=0)
    for q in range(4):
        out_ref[:, 512 * q : 512 * q + 512] = ended[4 * q : 4 * q + 4]

    for end in ends:
        end()

    def last_sent(i):
        j = (p + i) % 16

        @pl.when(j != final_self)
        def _():
            last_copy(j).wait_send()

    each(0, 16, last_sent)

    @pl.when(source)
    def _():
        for copy in step1:
            copy.wait_send()

    @pl.when(main)
    def _():
        for h in range(2):
            for copy in along(h):
                copy.wait_send()
            for i in others:
                forward(h, i).wait_send()


def per_device(
    token_ids,
    latent_offset,
    embed_table,
    cross_q,
    cross_kv,
    cross_out,
    self_qkv,
    self_out,
    mlp_in,
    mlp_out,
):
    vmem = pl.BlockSpec(memory_space=pltpu.VMEM)
    hbm = pl.BlockSpec(memory_space=pl.ANY)
    dma = pltpu.SemaphoreType.DMA
    rows = pl.pallas_call(
        whole_kernel,
        out_shape=jax.ShapeDtypeStruct((4, D), F32),
        in_specs=[pl.BlockSpec(memory_space=pltpu.SMEM)] + [vmem] * 3 + [hbm] * 6,
        out_specs=vmem,
        scratch_shapes=[
            pltpu.VMEM((256, D), BF),
            pltpu.VMEM((4, 3, 32, HD), BF),
            pltpu.VMEM((3, 4, 4, 4, 32, HD), BF),
            pltpu.VMEM((4, 4, 4, 4, 128), jnp.int32),
            pltpu.VMEM((D, 2 * HD), BF),
            pltpu.VMEM((2, 256, 2 * HD), BF),
            pltpu.VMEM((56, D), F32),
            pltpu.VMEM((56, D), F32),
            pltpu.VMEM((32, D), F32),
            pltpu.VMEM((32, D), F32),
            pltpu.VMEM((2048, D), BF),
            pltpu.VMEM((2048, 256), F32),
            pltpu.VMEM((2048, 256), BF),
            pltpu.VMEM((2048, 1), F32),
            pltpu.VMEM((64, D), BF),
            pltpu.VMEM((2048, HD), BF),
            pltpu.VMEM((2048, HD), BF),
            pltpu.VMEM((64, HD), BF),
            pltpu.VMEM((16, 64, HD), BF),
            pltpu.VMEM((16, 64, HD), BF),
            pltpu.VMEM((16, 64, HD), BF),
            pltpu.VMEM((16, 8, 128), F32),
            pltpu.VMEM((16, 8, 128), F32),
            pltpu.VMEM((HD, D), BF),
            pltpu.VMEM((3, D, HD), BF),
            pltpu.VMEM((HD, D), BF),
            pltpu.VMEM((16, 16, 512), BF),
            pltpu.VMEM((16, 16, 512), BF),
            pltpu.VMEM((16, 512), BF),
            pltpu.VMEM((16, 16, 512), BF),
            pltpu.VMEM((64, D), BF),
            pltpu.VMEM((64, 2 * HD), BF),
            pltpu.VMEM((16, 64, 2 * HD), BF),
            pltpu.VMEM((16, 16, 512), BF),
            pltpu.VMEM((16, 16, 512), BF),
            pltpu.VMEM((16, 512), BF),
            pltpu.VMEM((16, 16, 512), BF),
            pltpu.VMEM((4, D, HD), BF),
            pltpu.VMEM((4, HD, D), BF),
            pltpu.VMEM((4, 64, 512), F32),
            pltpu.VMEM((16, 16, 512), BF),
            pltpu.VMEM((16, 16, 512), BF),
            dma((4,)),
            dma((2, 4)),
            dma((2, 4)),
            dma((2, 8)),
            dma((2, 8)),
            dma((2, 8)),
            dma((2, 8)),
        ]
        + [dma((16,))] * 18
        + [dma((2,)), dma((2,)), dma((2,)), dma((2, 4)), dma((2, 4)), dma((2, 4)), dma((2, 4))],
        compiler_params=pltpu.CompilerParams(
            collective_id=0, has_side_effects=True, vmem_limit_bytes=VLIMIT
        ),
    )(
        latent_offset, token_ids.reshape(4, 128), cross_q, cross_kv, embed_table, cross_out, self_qkv, self_out, mlp_in, mlp_out,
    )
    return rows.astype(BF)[None]


def solution(mesh):
    placed = (
        P("ctx"),
        P(),
        P(),
        P("ctx", "lat"),
        P(None, "ctx", "lat"),
        P("lat", None),
        P(None, None, "lat"),
        P("lat", None),
        P(None, "ctx"),
        P("ctx", None),
    )
    return jax.shard_map(
        per_device, mesh=mesh, in_specs=placed, out_specs=P("lat", "ctx", None), check_vma=False
    )
```

```python
import math

import jax
import jax.numpy as jnp
from jax import lax
from jax.experimental import pallas as pl
from jax.experimental.pallas import tpu as pltpu
from jax.sharding import PartitionSpec as P

MESH = pl.DeviceIdType.MESH
HD = 128
D = 2048
LATENTS = 1024
EPSILON = 1e-06
MASKED = -1e30
SCALE = 1.0 / math.sqrt(HD)
BF = jnp.bfloat16
F32 = jnp.float32
VLIMIT = 58 * 1024 * 1024


def place():
    g = lax.axis_index("ctx")
    y = lax.axis_index("lat")
    return g // 16, (g // 4) % 4, (g // 2) % 2, g % 2, y


def at(x, a, b, c, y):
    return (16 * x + 4 * a + 2 * b + c, y)


def push(src, dst, send_sem, recv_sem, device):
    copy = pltpu.make_async_remote_copy(
        src_ref=src,
        dst_ref=dst,
        send_sem=send_sem,
        recv_sem=recv_sem,
        device_id=device,
        device_id_type=MESH,
    )
    return copy


def arrive(dst, recv_sem, device):
    push(dst, dst, recv_sem, recv_sem, device).wait_recv()


def each(first, last, body):
    def step(k, carry):
        body(k)
        return carry

    lax.fori_loop(first, last, step, 0)


class Exchange:
    def __init__(self, src, dst, send, recv, me, device_of, n, whole=False):
        self.src, self.dst, self.send, self.recv = src, dst, send, recv
        self.me, self.device_of, self.n, self.whole = me, device_of, n, whole

    def copy(self, j):
        src = self.src if self.whole else self.src.at[j]
        return push(src, self.dst.at[self.me], self.send.at[j], self.recv.at[self.me], self.device_of(j))

    def start(self):
        def one(k):
            self.copy((self.me + k) % self.n).start()

        each(1, self.n, one)
        self.dst[self.me] = self.src[...] if self.whole else self.src[self.me]

    def wait_all(self):
        def one(k):
            j = (self.me + self.n - k) % self.n
            arrive(self.dst.at[j], self.recv.at[j], self.device_of(j))

        each(1, self.n, one)

    def wait_sent(self):
        def one(k):
            self.copy((self.me + k) % self.n).wait_send()

        each(1, self.n, one)


def rms_rows(values):
    return values * lax.rsqrt(jnp.mean(values * values, axis=-1, keepdims=True) + EPSILON)


def whole_kernel(
    offset_ref, tok_ref, q_ref, kv_ref,
    table_hbm, cout_ref, sqkv_ref, sout_ref, in_ref, mout_ref,
    out_ref,
    table_ref, stage, w_all, tokens, wkv, tw, sin_ref, cos_ref, rows_sin, rows_cos, waves, products, one_hot, inverse, latent, keys, values, q_own, q_all,
    o_msg, o_came, st_msg, st_came, w_co, w_qkv, w_so, msg, came, own, all_rows, normed, kv, kv_all, msg2, came2,
    own2, all_rows2, w_in, w_out, partial, msg3, came3,
    load, s1, r1, s2, r2, s3, r3, s_q, r_q, s_o, r_o, s_st, r_st, s_m, r_m, s_a, r_a, s_kv, r_kv, s_m2, r_m2,
    s_a2, r_a2, s_m3, r_m3, own_w, sw1, rw1, sw2, rw2, sw3, rw3,
):
    x, a, b, c, y = place()
    k = 2 * b + c
    r = 4 * x + k
    p = 4 * y + a
    j_me = 2 * x + b
    partner = at(x, a, b, 1 - c, y)

    def row_of(j):
        return at(j // 4, a, (j // 2) % 2, j % 2, y)

    def head_of(j):
        return at(x, j % 4, b, c, j // 4)

    def final_of(j):
        return at(x, k, (j // 2) % 2, j % 2, j // 4)

    def sender_of(j):
        return at(x, j % 4, a // 2, a % 2, j // 4)

    final_self = jnp.where(a == k, 4 * y + k, 16)
    sender_self = jnp.where(a == k, p, 16)

    barrier = pltpu.get_barrier_semaphore()

    def hello(device):
        pl.semaphore_signal(barrier, inc=1, device_id=device, device_id_type=MESH)

    each(1, 16, lambda i: hello(row_of((r + i) % 16)))
    each(1, 16, lambda i: hello(head_of((p + i) % 16)))

    def hello_sender(j):
        @pl.when(j != sender_self)
        def _():
            hello(sender_of(j))

    each(0, 16, hello_sender)
    row_at = pl.multiple_of(a * HD, HD)
    table_load = pltpu.make_async_copy(table_hbm, table_ref, load.at[3])
    table_load.start()
    loads = [
        pltpu.make_async_copy(cout_ref.at[pl.ds(row_at, HD), :], w_co, load.at[0]),
        pltpu.make_async_copy(sqkv_ref.at[:, :, pl.ds(row_at, HD)], w_qkv, load.at[1]),
        pltpu.make_async_copy(sout_ref.at[pl.ds(row_at, HD), :], w_so, load.at[2]),
    ]
    for copy in loads:
        copy.start()
    for h in range(4):
        stage[h, 0] = q_ref[:, 128 * h : 128 * h + 128]
        stage[h, 1] = kv_ref[0, :, 128 * h : 128 * h + 128]
        stage[h, 2] = kv_ref[1, :, 128 * h : 128 * h + 128]
    pl.semaphore_wait(barrier, jnp.where(a == k, 45, 46))
    ends = []

    heads = [(a + d) % 4 for d in range(1, 4)]
    rows = [((x + dx) % 4, (b + db) % 2) for dx in (0, 1, 3, 2) for db in (0, 1) if dx or db]
    first_copies = []
    for h in heads:
        there = at(x, h, b, c, y)
        first_copies.append(push(tok_ref, tokens.at[x, a, k], s1.at[1, h], r1.at[1, a], there))
        first_copies.append(push(stage.at[h], w_all.at[:, x, a, k], s1.at[0, h], r1.at[0, a], there))
    for copy in first_copies:
        copy.start()
        ends.append(copy.wait_send)
    main = c == y // 2
    source = jnp.logical_and(main, b == y % 2)
    beside = at(x, a, 1 - b, c, y)
    mine = [
        pltpu.make_async_copy(in_ref, w_in.at[x], own_w.at[0]),
        pltpu.make_async_copy(mout_ref, w_out.at[x], own_w.at[1]),
    ]
    step1 = [
        push(in_ref, w_in.at[x], sw1.at[0], rw1.at[0], beside),
        push(mout_ref, w_out.at[x], sw1.at[1], rw1.at[1], beside),
    ]

    @pl.when(source)
    def _():
        for copy in step1 + mine:
            copy.start()

    tokens[x, a, k] = tok_ref[...]
    for part in range(3):
        w_all[part, x, a, k] = stage[a, part]

    offset = offset_ref[0]
    index = lax.broadcasted_iota(jnp.int32, (56, 1), 0)
    places = jnp.where(index < 4, 512 * (16 * x + 4 * index + k), offset + 256 * (index - 4) + 16 * r)
    places = jnp.where(index < 8, places, jnp.where(index < 40, 16 * (index - 8), index - 40)).astype(F32)

    def table_columns(j):
        lanes = pl.ds(pl.multiple_of(j * 256, 256), 256)
        pair = ((j * 256 + lax.broadcasted_iota(jnp.int32, (1, 256), 1)) // 2).astype(F32)
        angles = places * jnp.exp(pair * (-2.0 * math.log(10000.0) / D))
        sin_ref[:, lanes] = jnp.sin(angles)
        cos_ref[:, lanes] = jnp.cos(angles)

    each(0, 8, table_columns)

    for h in heads:
        arrive(tokens.at[x, h, k], r1.at[1, h], partner)
        arrive(w_all.at[:, x, h, k], r1.at[0, h], partner)
    second_copies = []
    for rx, rb in rows:
        there = at(rx, a, rb, c, y)
        j = 2 * rx + rb
        second_copies.append(push(tokens.at[x, :, k], tokens.at[x, :, k], s2.at[1, j], r2.at[1, j_me], there))
        second_copies.append(push(w_all.at[:, x, :, k], w_all.at[:, x, :, k], s2.at[0, j], r2.at[0, j_me], there))
    for copy in second_copies:
        copy.start()
        ends.append(copy.wait_send)

    def onward(rx, rb):
        j = 2 * rx + rb
        k2 = 2 * rb + c
        return [
            push(tokens.at[rx, :, k2], tokens.at[rx, :, k2], s3.at[1, j], r3.at[1, j], partner),
            push(w_all.at[:, rx, :, k2], w_all.at[:, rx, :, k2], s3.at[0, j], r3.at[0, j], partner),
        ]

    third_copies = onward(x, b)
    for copy in third_copies:
        copy.start()
        ends.append(copy.wait_send)

    odd = lax.broadcasted_iota(jnp.int32, (1, D), 1) % 2 == 1
    mid_sin, mid_cos = sin_ref[8:40], cos_ref[8:40]

    def start_of(n):
        s, co = sin_ref[pl.ds(n, 1)], cos_ref[pl.ds(n, 1)]
        return jnp.where(odd, co, s), jnp.where(odd, -s, co)

    def waves_of(n):
        s, co = start_of(n)
        rows_sin[...] = s * mid_cos + co * mid_sin
        rows_cos[...] = co * mid_cos - s * mid_sin

        def columns(j):
            lanes = pl.ds(pl.multiple_of(j * 128, 128), 128)
            low_sin, low_cos = sin_ref[40:56, lanes], cos_ref[40:56, lanes]
            for m in range(32):
                wave = rows_sin[m : m + 1, lanes] * low_cos + rows_cos[m : m + 1, lanes] * low_sin
                waves[pl.ds(pl.multiple_of(n * 512 + 16 * m, 16), 16), lanes] = wave.astype(BF)

        each(0, 16, columns)

    each(0, 4, waves_of)

    table_load.wait()
    square = table_ref[...].astype(F32)
    square = square * square
    high = square.astype(BF)
    lower = (square - high.astype(F32)).astype(BF)
    ones = jnp.ones((8, D), BF)
    across = (((1,), (1,)), ((), ()))
    norms = lax.dot_general(ones, high, across, preferred_element_type=F32) + lax.dot_general(
        ones, lower, across, preferred_element_type=F32
    )
    norms = norms[0:1]

    def products_of(n):
        run = pl.ds(pl.multiple_of(n * 512, 512), 512)
        products[run, :] = lax.dot_general(waves[run, :], table_ref[...], across, preferred_element_type=F32)

    each(0, 4, products_of)

    vocab = lax.broadcasted_iota(jnp.int32, (128, 256), 1).astype(F32)
    diagonal = lax.broadcasted_iota(jnp.int32, (128, 128), 0) == lax.broadcasted_iota(jnp.int32, (128, 128), 1)

    def scales_of(n):
        here = tokens[x, n, k].astype(F32)
        for q in range(4):
            column = jnp.sum(jnp.where(diagonal, here[q : q + 1, :], 0.0), axis=1, keepdims=True)
            chosen = column == vocab
            quarter = pl.ds(pl.multiple_of(n * 512 + 128 * q, 128), 128)
            one_hot[quarter, :] = chosen.astype(BF)
            total = jnp.sum(
                jnp.where(chosen, 2.0 * products[quarter, :] + norms, 0.0), axis=1, keepdims=True
            )
            total = jnp.maximum(total + D / 2, 0.0)
            inverse[quarter, :] = lax.rsqrt(total * (1.0 / D) + EPSILON)

    each(0, 4, scales_of)

    for rx, rb in rows:
        sx, sb = (2 * x + 4 - rx) % 4, rb
        j = 2 * sx + sb
        k2 = 2 * sb + c
        arrive(tokens.at[sx, :, k2], r2.at[1, j], partner)
        arrive(w_all.at[:, sx, :, k2], r2.at[0, j], partner)
        more = onward(sx, sb)
        for copy in more:
            copy.start()
            ends.append(copy.wait_send)
    for rx, rb in [(x, b)] + rows:
        j = 2 * rx + rb
        k3 = 2 * rb + 1 - c
        arrive(tokens.at[rx, :, k3], r3.at[1, j], partner)
        arrive(w_all.at[:, rx, :, k3], r3.at[0, j], partner)

    slot = lax.broadcasted_iota(jnp.int32, (64, 1), 0)
    target = offset + (slot // 16) * 256 + 16 * r + slot % 16
    lane = lax.broadcasted_iota(jnp.int32, (1, 128), 1)
    found = jnp.zeros((64, 128), F32)
    for q in range(3):
        bytes_here = tokens[3, 3, 1 + q].astype(F32)
        for t in range(4):
            hit = target == lane + (31232 + 512 * q + 128 * t)
            found = found + jnp.where(hit, bytes_here[t : t + 1, :], 0.0)
    column = jnp.sum(found, axis=1, keepdims=True)
    looked = jnp.dot((column == vocab[:64]).astype(BF), table_ref[...], preferred_element_type=F32)
    for t in range(4):
        s, co = start_of(4 + t)
        wave = s * cos_ref[40:56] + co * sin_ref[40:56]
        latent[16 * t : 16 * t + 16, :] = rms_rows(looked[16 * t : 16 * t + 16] + wave).astype(BF)
    weights_of = w_all.reshape(3, D, HD)
    q_own[...] = jnp.dot(latent[...], weights_of[0], preferred_element_type=F32).astype(BF)
    asked = Exchange(q_own, q_all, s_q, r_q, r, row_of, 16, whole=True)
    asked.start()
    ends.append(asked.wait_sent)

    wkv[:, :HD] = weights_of[1]
    wkv[:, HD:] = weights_of[2]
    table_w = jnp.dot(table_ref[...], wkv[...], preferred_element_type=F32)
    tw[0] = table_w.astype(BF)
    tw[1] = (table_w - table_w.astype(BF).astype(F32)).astype(BF)

    def keys_of(n):
        run = pl.ds(pl.multiple_of(n * 512, 512), 512)
        both = jnp.dot(waves[run, :], wkv[...], preferred_element_type=F32)
        both = both + jnp.dot(one_hot[run, :], tw[0], preferred_element_type=F32)
        both = both + jnp.dot(one_hot[run, :], tw[1], preferred_element_type=F32)
        both = (both * inverse[run, :]).astype(BF)
        keys[run, :] = both[:, :HD]
        values[run, :] = both[:, HD:]

    each(0, 4, keys_of)
    asked.wait_all()

    key_col = lax.broadcasted_iota(jnp.int32, (1, 2048), 1)
    key_place = 512 * (16 * x + 4 * (key_col // 512) + k) + key_col % 512
    outs = Exchange(o_msg, o_came, s_o, r_o, r, row_of, 16)
    stats = Exchange(st_msg, st_came, s_st, r_st, r, row_of, 16)
    diagonal64 = lax.broadcasted_iota(jnp.int32, (64, 128), 0) == lax.broadcasted_iota(jnp.int32, (64, 128), 1)

    def attend(step):
        t = (x + 1 + step) % 4
        query = q_all[pl.ds(4 * t, 4)].reshape(256, HD)
        scores = lax.dot_general(query, keys[...], across, preferred_element_type=F32) * SCALE
        row = lax.broadcasted_iota(jnp.int32, (256, 1), 0)
        row_place = offset + ((row // 16) % 4) * 256 + 16 * (4 * t + row // 64) + row % 16
        scores = jnp.where(key_place > row_place, MASKED, scores)
        peak = jnp.max(scores, axis=1, keepdims=True)
        weights = jnp.exp(scores - peak).astype(BF)
        total = jnp.sum(weights.astype(F32), axis=1, keepdims=True)
        out = jnp.dot(weights, values[...], preferred_element_type=F32).astype(BF)
        for g in range(4):
            some = slice(64 * g, 64 * g + 64)
            j = 4 * t + g
            o_msg[j] = out[some]
            st_msg[j, 0:1, :] = jnp.sum(jnp.where(diagonal64, peak[some], 0.0), axis=0, keepdims=True)
            st_msg[j, 1:2, :] = jnp.sum(jnp.where(diagonal64, total[some], 0.0), axis=0, keepdims=True)

            @pl.when(j != r)
            def _():
                stats.copy(j).start()
                outs.copy(j).start()

    each(0, 4, attend)
    o_came[r] = o_msg[r]
    st_came[r] = st_msg[r]
    stats.wait_all()
    outs.wait_all()
    ends += [stats.wait_sent, outs.wait_sent]

    halves = (w_in, w_out)
    others = [(x + d) % 4 for d in (1, 3, 2)]

    def along(h):
        copies = [push(halves[h].at[x], halves[h].at[x], sw2.at[h, i], rw2.at[h, x], at(i, a, b, c, y)) for i in others]
        return copies + [forward(h, x)]

    def forward(h, i):
        return push(halves[h].at[i], halves[h].at[i], sw3.at[h, i], rw3.at[h, i], partner)

    def set_out(h):
        @pl.when(source)
        def _():
            mine[h].wait()

        @pl.when(jnp.logical_and(main, jnp.logical_not(source)))
        def _():
            arrive(halves[h].at[x], rw1.at[h], partner)

        @pl.when(main)
        def _():
            for copy in along(h):
                copy.start()

    def hand_over(h):
        @pl.when(main)
        def _():
            for i in others:
                arrive(halves[h].at[i], rw2.at[h, i], partner)
                forward(h, i).start()

    def receive(h):
        @pl.when(jnp.logical_not(main))
        def _():
            for i in range(4):
                arrive(halves[h].at[i], rw3.at[h, i], partner)

    maxima, totals = st_came[:, 0, :], st_came[:, 1, :]
    factor = jnp.exp(maxima - jnp.max(maxima, axis=0, keepdims=True))
    factor = factor / jnp.sum(factor * totals, axis=0, keepdims=True)
    attended = jnp.zeros((64, HD), F32)
    for j in range(16):
        column = jnp.sum(jnp.where(diagonal64, factor[j : j + 1, :], 0.0), axis=1, keepdims=True)
        attended = attended + column * o_came[j].astype(F32)
    for copy in loads:
        copy.wait()

    def shares(rows, weight, out):
        for q in range(4):
            part = jnp.dot(rows, weight[:, 512 * q : 512 * q + 512], preferred_element_type=F32).astype(BF)
            for t in range(4):
                out[4 * t + q] = part[16 * t : 16 * t + 16]

    def rows_normed(blocks):
        for t in range(4):
            wide = jnp.concatenate([blocks[4 * t + q] for q in range(4)], axis=1).astype(F32)
            normed[16 * t : 16 * t + 16, :] = rms_rows(wide).astype(BF)

    shares(attended.astype(BF), w_co, msg)
    summed = Exchange(msg, came, s_m, r_m, p, head_of, 16)
    summed.start()
    set_out(0)
    own_block = (pl.ds(pl.multiple_of(16 * y, 16), 16), pl.ds(pl.multiple_of(512 * a, 512), 512))
    own_latent = latent[own_block].astype(F32)
    summed.wait_all()
    ends.append(summed.wait_sent)
    first = jnp.sum(came[...].astype(F32), axis=0) + own_latent
    own[...] = first.astype(BF)
    spread = Exchange(own, all_rows, s_a, r_a, p, head_of, 16, whole=True)
    spread.start()
    spread.wait_all()
    ends.append(spread.wait_sent)

    rows_normed(all_rows)
    kv[:, :HD] = jnp.dot(normed[...], w_qkv[1], preferred_element_type=F32).astype(BF)
    kv[:, HD:] = jnp.dot(normed[...], w_qkv[2], preferred_element_type=F32).astype(BF)
    both = Exchange(kv, kv_all, s_kv, r_kv, r, row_of, 16, whole=True)
    both.start()
    hand_over(0)
    query = jnp.dot(normed[...], w_qkv[0], preferred_element_type=F32).astype(BF)
    both.wait_all()
    ends.append(both.wait_sent)

    all_keys = kv_all[:, :, :HD].reshape(LATENTS, HD)
    all_values = kv_all[:, :, HD:].reshape(LATENTS, HD)
    scores = lax.dot_general(query, all_keys, across, preferred_element_type=F32) * SCALE
    row = lax.broadcasted_iota(jnp.int32, (64, 1), 0)
    col = lax.broadcasted_iota(jnp.int32, (1, LATENTS), 1)
    row_place = (row // 16) * 256 + 16 * r + row % 16
    col_place = ((col // 16) % 4) * 256 + 16 * (col // 64) + col % 16
    scores = jnp.where(col_place > row_place, MASKED, scores)
    weights = jnp.exp(scores - jnp.max(scores, axis=1, keepdims=True)).astype(BF)
    total = jnp.sum(weights.astype(F32), axis=1, keepdims=True)
    attended = jnp.dot(weights, all_values, preferred_element_type=F32) / total
    shares(attended.astype(BF), w_so, msg2)
    summed2 = Exchange(msg2, came2, s_m2, r_m2, p, head_of, 16)
    summed2.start()
    set_out(1)
    summed2.wait_all()
    ends.append(summed2.wait_sent)
    second = first + jnp.sum(came2[...].astype(F32), axis=0)
    own2[...] = second.astype(BF)
    spread2 = Exchange(own2, all_rows2, s_a2, r_a2, p, head_of, 16, whole=True)
    spread2.start()
    hand_over(1)

    spread2.wait_all()
    ends.append(spread2.wait_sent)

    rows_normed(all_rows2)
    receive(0)
    hidden = []
    for i in range(4):
        pre = jnp.dot(normed[...], w_in[i], preferred_element_type=F32)
        hidden.append(jax.nn.gelu(pre, approximate=True).astype(BF))
    hidden = jnp.concatenate(hidden, axis=1)
    receive(1)
    for q in range(4):
        columns = slice(512 * q, 512 * q + 512)
        partial[q] = jnp.dot(hidden, w_out[:, :, columns].reshape(512, 512), preferred_element_type=F32)
    here = pl.ds(pl.multiple_of(16 * y, 16), 16)
    partial[a, here, :] = partial[a, here, :] + second
    for j in range(16):
        some = slice(4 * j, 4 * j + 4)
        msg3[j] = jnp.concatenate([partial[q, some, :] for q in range(4)], axis=0).astype(BF)

    def last_copy(j):
        return push(msg3.at[j], came3.at[p], s_m3.at[j], r_m3.at[p], final_of(j))

    def last_start(i):
        j = (p + i) % 16

        @pl.when(j != final_self)
        def _():
            last_copy(j).start()

    each(0, 16, last_start)

    @pl.when(a == k)
    def _():
        came3[p] = msg3[4 * y + k]

    def last_wait(i):
        j = (p + i) % 16

        @pl.when(j != sender_self)
        def _():
            arrive(came3.at[j], r_m3.at[j], partner)

    each(0, 16, last_wait)
    ended = jnp.sum(came3[...].astype(F32), axis=0)
    for q in range(4):
        out_ref[:, 512 * q : 512 * q + 512] = ended[4 * q : 4 * q + 4]

    for end in ends:
        end()

    def last_sent(i):
        j = (p + i) % 16

        @pl.when(j != final_self)
        def _():
            last_copy(j).wait_send()

    each(0, 16, last_sent)

    @pl.when(source)
    def _():
        for copy in step1:
            copy.wait_send()

    @pl.when(main)
    def _():
        for h in range(2):
            for copy in along(h):
                copy.wait_send()
            for i in others:
                forward(h, i).wait_send()


def per_device(
    token_ids,
    latent_offset,
    embed_table,
    cross_q,
    cross_kv,
    cross_out,
    self_qkv,
    self_out,
    mlp_in,
    mlp_out,
):
    vmem = pl.BlockSpec(memory_space=pltpu.VMEM)
    hbm = pl.BlockSpec(memory_space=pl.ANY)
    dma = pltpu.SemaphoreType.DMA
    rows = pl.pallas_call(
        whole_kernel,
        out_shape=jax.ShapeDtypeStruct((4, D), F32),
        in_specs=[pl.BlockSpec(memory_space=pltpu.SMEM)] + [vmem] * 3 + [hbm] * 6,
        out_specs=vmem,
        scratch_shapes=[
            pltpu.VMEM((256, D), BF),
            pltpu.VMEM((4, 3, 32, HD), BF),
            pltpu.VMEM((3, 4, 4, 4, 32, HD), BF),
            pltpu.VMEM((4, 4, 4, 4, 128), jnp.int32),
            pltpu.VMEM((D, 2 * HD), BF),
            pltpu.VMEM((2, 256, 2 * HD), BF),
            pltpu.VMEM((56, D), F32),
            pltpu.VMEM((56, D), F32),
            pltpu.VMEM((32, D), F32),
            pltpu.VMEM((32, D), F32),
            pltpu.VMEM((2048, D), BF),
            pltpu.VMEM((2048, 256), F32),
            pltpu.VMEM((2048, 256), BF),
            pltpu.VMEM((2048, 1), F32),
            pltpu.VMEM((64, D), BF),
            pltpu.VMEM((2048, HD), BF),
            pltpu.VMEM((2048, HD), BF),
            pltpu.VMEM((64, HD), BF),
            pltpu.VMEM((16, 64, HD), BF),
            pltpu.VMEM((16, 64, HD), BF),
            pltpu.VMEM((16, 64, HD), BF),
            pltpu.VMEM((16, 8, 128), F32),
            pltpu.VMEM((16, 8, 128), F32),
            pltpu.VMEM((HD, D), BF),
            pltpu.VMEM((3, D, HD), BF),
            pltpu.VMEM((HD, D), BF),
            pltpu.VMEM((16, 16, 512), BF),
            pltpu.VMEM((16, 16, 512), BF),
            pltpu.VMEM((16, 512), BF),
            pltpu.VMEM((16, 16, 512), BF),
            pltpu.VMEM((64, D), BF),
            pltpu.VMEM((64, 2 * HD), BF),
            pltpu.VMEM((16, 64, 2 * HD), BF),
            pltpu.VMEM((16, 16, 512), BF),
            pltpu.VMEM((16, 16, 512), BF),
            pltpu.VMEM((16, 512), BF),
            pltpu.VMEM((16, 16, 512), BF),
            pltpu.VMEM((4, D, HD), BF),
            pltpu.VMEM((4, HD, D), BF),
            pltpu.VMEM((4, 64, 512), F32),
            pltpu.VMEM((16, 16, 512), BF),
            pltpu.VMEM((16, 16, 512), BF),
            dma((4,)),
            dma((2, 4)),
            dma((2, 4)),
            dma((2, 8)),
            dma((2, 8)),
            dma((2, 8)),
            dma((2, 8)),
        ]
        + [dma((16,))] * 18
        + [dma((2,)), dma((2,)), dma((2,)), dma((2, 4)), dma((2, 4)), dma((2, 4)), dma((2, 4))],
        compiler_params=pltpu.CompilerParams(
            collective_id=0, has_side_effects=True, vmem_limit_bytes=VLIMIT
        ),
    )(
        latent_offset, token_ids.reshape(4, 128), cross_q, cross_kv, embed_table, cross_out, self_qkv, self_out, mlp_in, mlp_out,
    )
    return rows.astype(BF)[None]


def solution(mesh):
    placed = (
        P("ctx"),
        P(),
        P(),
        P("ctx", "lat"),
        P(None, "ctx", "lat"),
        P("lat", None),
        P(None, None, "lat"),
        P("lat", None),
        P(None, "ctx"),
        P("ctx", None),
    )
    return jax.shard_map(
        per_device, mesh=mesh, in_specs=placed, out_specs=P("lat", "ctx", None), check_vma=False
    )
```

```python
import math

import jax
import jax.numpy as jnp
from jax import lax
from jax.experimental import pallas as pl
from jax.experimental.pallas import tpu as pltpu
from jax.sharding import PartitionSpec as P

MESH = pl.DeviceIdType.MESH
HD = 128
D = 2048
LATENTS = 1024
EPSILON = 1e-06
MASKED = -1e30
SCALE = 1.0 / math.sqrt(HD)
BF = jnp.bfloat16
F32 = jnp.float32
VLIMIT = 58 * 1024 * 1024


def place():
    g = lax.axis_index("ctx")
    y = lax.axis_index("lat")
    return g // 16, (g // 4) % 4, (g // 2) % 2, g % 2, y


def at(x, a, b, c, y):
    return (16 * x + 4 * a + 2 * b + c, y)


def push(src, dst, send_sem, recv_sem, device):
    copy = pltpu.make_async_remote_copy(
        src_ref=src,
        dst_ref=dst,
        send_sem=send_sem,
        recv_sem=recv_sem,
        device_id=device,
        device_id_type=MESH,
    )
    return copy


def arrive(dst, recv_sem, device):
    push(dst, dst, recv_sem, recv_sem, device).wait_recv()


def each(first, last, body):
    def step(k, carry):
        body(k)
        return carry

    lax.fori_loop(first, last, step, 0)


class Exchange:
    def __init__(self, src, dst, send, recv, me, device_of, n, whole=False):
        self.src, self.dst, self.send, self.recv = src, dst, send, recv
        self.me, self.device_of, self.n, self.whole = me, device_of, n, whole

    def copy(self, j):
        src = self.src if self.whole else self.src.at[j]
        return push(src, self.dst.at[self.me], self.send.at[j], self.recv.at[self.me], self.device_of(j))

    def start(self):
        def one(k):
            self.copy((self.me + k) % self.n).start()

        each(1, self.n, one)
        self.dst[self.me] = self.src[...] if self.whole else self.src[self.me]

    def wait_all(self):
        def one(k):
            j = (self.me + self.n - k) % self.n
            arrive(self.dst.at[j], self.recv.at[j], self.device_of(j))

        each(1, self.n, one)

    def wait_sent(self):
        def one(k):
            self.copy((self.me + k) % self.n).wait_send()

        each(1, self.n, one)


def rms_rows(values):
    return values * lax.rsqrt(jnp.mean(values * values, axis=-1, keepdims=True) + EPSILON)


def whole_kernel(
    offset_ref, tok_ref, q_ref, kv_ref,
    table_hbm, cout_ref, sqkv_ref, sout_ref, in_ref, mout_ref,
    out_ref,
    table_ref, stage, w_all, tokens, wkv, tw, sin_ref, cos_ref, rows_sin, rows_cos, waves, products, one_hot, inverse, latent, keys, values, q_own, q_all,
    o_msg, o_came, st_msg, st_came, w_co, w_qkv, w_so, msg, came, own, all_rows, normed, kv, kv_all, msg2, came2,
    own2, all_rows2, w_in, w_out, partial, msg3, came3,
    load, s1, r1, s2, r2, s3, r3, s_q, r_q, s_o, r_o, s_st, r_st, s_m, r_m, s_a, r_a, s_kv, r_kv, s_m2, r_m2,
    s_a2, r_a2, s_m3, r_m3, own_w, sw1, rw1, sw2, rw2, sw3, rw3,
):
    x, a, b, c, y = place()
    k = 2 * b + c
    r = 4 * x + k
    p = 4 * y + a
    j_me = 2 * x + b
    partner = at(x, a, b, 1 - c, y)

    def row_of(j):
        return at(j // 4, a, (j // 2) % 2, j % 2, y)

    def head_of(j):
        return at(x, j % 4, b, c, j // 4)

    def final_of(j):
        return at(x, k, (j // 2) % 2, j % 2, j // 4)

    def sender_of(j):
        return at(x, j % 4, a // 2, a % 2, j // 4)

    final_self = jnp.where(a == k, 4 * y + k, 16)
    sender_self = jnp.where(a == k, p, 16)

    barrier = pltpu.get_barrier_semaphore()

    def hello(device):
        pl.semaphore_signal(barrier, inc=1, device_id=device, device_id_type=MESH)

    each(1, 16, lambda i: hello(row_of((r + i) % 16)))
    each(1, 16, lambda i: hello(head_of((p + i) % 16)))

    def hello_sender(j):
        @pl.when(j != sender_self)
        def _():
            hello(sender_of(j))

    each(0, 16, hello_sender)
    row_at = pl.multiple_of(a * HD, HD)
    table_load = pltpu.make_async_copy(table_hbm, table_ref, load.at[3])
    table_load.start()
    loads = [
        pltpu.make_async_copy(cout_ref.at[pl.ds(row_at, HD), :], w_co, load.at[0]),
        pltpu.make_async_copy(sqkv_ref.at[:, :, pl.ds(row_at, HD)], w_qkv, load.at[1]),
        pltpu.make_async_copy(sout_ref.at[pl.ds(row_at, HD), :], w_so, load.at[2]),
    ]
    for copy in loads:
        copy.start()
    for h in range(4):
        stage[h, 0] = q_ref[:, 128 * h : 128 * h + 128]
        stage[h, 1] = kv_ref[0, :, 128 * h : 128 * h + 128]
        stage[h, 2] = kv_ref[1, :, 128 * h : 128 * h + 128]
    pl.semaphore_wait(barrier, jnp.where(a == k, 45, 46))
    ends = []

    heads = [(a + d) % 4 for d in range(1, 4)]
    rows = [((x + dx) % 4, (b + db) % 2) for dx in (0, 1, 3, 2) for db in (0, 1) if dx or db]
    first_copies = []
    for h in heads:
        there = at(x, h, b, c, y)
        first_copies.append(push(tok_ref, tokens.at[x, a, k], s1.at[1, h], r1.at[1, a], there))
        first_copies.append(push(stage.at[h], w_all.at[:, x, a, k], s1.at[0, h], r1.at[0, a], there))
    for copy in first_copies:
        copy.start()
        ends.append(copy.wait_send)
    main = c == y // 2
    source = jnp.logical_and(main, b == y % 2)
    beside = at(x, a, 1 - b, c, y)
    mine = [
        pltpu.make_async_copy(in_ref, w_in.at[x], own_w.at[0]),
        pltpu.make_async_copy(mout_ref, w_out.at[x], own_w.at[1]),
    ]
    step1 = [
        push(in_ref, w_in.at[x], sw1.at[0], rw1.at[0], beside),
        push(mout_ref, w_out.at[x], sw1.at[1], rw1.at[1], beside),
    ]

    @pl.when(source)
    def _():
        for copy in step1 + mine:
            copy.start()

    tokens[x, a, k] = tok_ref[...]
    for part in range(3):
        w_all[part, x, a, k] = stage[a, part]

    offset = offset_ref[0]
    index = lax.broadcasted_iota(jnp.int32, (56, 1), 0)
    places = jnp.where(index < 4, 512 * (16 * x + 4 * index + k), offset + 256 * (index - 4) + 16 * r)
    places = jnp.where(index < 8, places, jnp.where(index < 40, 16 * (index - 8), index - 40)).astype(F32)

    def table_columns(j):
        lanes = pl.ds(pl.multiple_of(j * 256, 256), 256)
        pair = ((j * 256 + lax.broadcasted_iota(jnp.int32, (1, 256), 1)) // 2).astype(F32)
        angles = places * jnp.exp(pair * (-2.0 * math.log(10000.0) / D))
        sin_ref[:, lanes] = jnp.sin(angles)
        cos_ref[:, lanes] = jnp.cos(angles)

    each(0, 8, table_columns)

    for h in heads:
        arrive(tokens.at[x, h, k], r1.at[1, h], partner)
        arrive(w_all.at[:, x, h, k], r1.at[0, h], partner)
    def pieces(rx, rb, core):
        k2 = 2 * rb + core
        return tokens.at[rx, :, k2], w_all.at[:, rx, :, k2]

    def send_on(block, there, send, recv, sent, landed):
        for n, ref in enumerate(block):
            copy = push(ref, ref, send.at[1 - n, sent], recv.at[1 - n, landed], there)
            copy.start()
            ends.append(copy.wait_send)

    def beside_on(rx):
        send_on(pieces(rx, b, c), at(x, a, 1 - b, c, y), s2, r2, 2 * rx + 1 - b, 2 * rx + b)

    def partner_on(rx, rb):
        send_on(pieces(rx, rb, c), partner, s3, r3, 2 * rx + rb, 2 * rx + rb)

    for d in (1, 3, 2):
        rx = (x + d) % 4
        send_on(pieces(x, b, c), at(rx, a, b, c, y), s2, r2, 2 * rx + b, j_me)
    beside_on(x)
    partner_on(x, b)

    def hand_on(rx, rb, further):
        for n, ref in enumerate(pieces(rx, rb, c)):
            arrive(ref, r2.at[1 - n, 2 * rx + rb], partner)
        if further:
            beside_on(rx)
        partner_on(rx, rb)


    odd = lax.broadcasted_iota(jnp.int32, (1, D), 1) % 2 == 1
    mid_sin, mid_cos = sin_ref[8:40], cos_ref[8:40]

    def start_of(n):
        s, co = sin_ref[pl.ds(n, 1)], cos_ref[pl.ds(n, 1)]
        return jnp.where(odd, co, s), jnp.where(odd, -s, co)

    def waves_of(n):
        s, co = start_of(n)
        rows_sin[...] = s * mid_cos + co * mid_sin
        rows_cos[...] = co * mid_cos - s * mid_sin

        def columns(j):
            lanes = pl.ds(pl.multiple_of(j * 128, 128), 128)
            low_sin, low_cos = sin_ref[40:56, lanes], cos_ref[40:56, lanes]
            for m in range(32):
                wave = rows_sin[m : m + 1, lanes] * low_cos + rows_cos[m : m + 1, lanes] * low_sin
                waves[pl.ds(pl.multiple_of(n * 512 + 16 * m, 16), 16), lanes] = wave.astype(BF)

        each(0, 16, columns)

    each(0, 4, waves_of)
    hand_on((x + 1) % 4, b, True)
    hand_on((x + 3) % 4, b, True)
    hand_on(x, 1 - b, False)

    table_load.wait()
    square = table_ref[...].astype(F32)
    square = square * square
    high = square.astype(BF)
    lower = (square - high.astype(F32)).astype(BF)
    ones = jnp.ones((8, D), BF)
    across = (((1,), (1,)), ((), ()))
    norms = lax.dot_general(ones, high, across, preferred_element_type=F32) + lax.dot_general(
        ones, lower, across, preferred_element_type=F32
    )
    norms = norms[0:1]

    def products_of(n):
        run = pl.ds(pl.multiple_of(n * 512, 512), 512)
        products[run, :] = lax.dot_general(waves[run, :], table_ref[...], across, preferred_element_type=F32)

    each(0, 4, products_of)
    hand_on((x + 2) % 4, b, True)
    hand_on((x + 1) % 4, 1 - b, False)
    hand_on((x + 3) % 4, 1 - b, False)

    vocab = lax.broadcasted_iota(jnp.int32, (128, 256), 1).astype(F32)
    diagonal = lax.broadcasted_iota(jnp.int32, (128, 128), 0) == lax.broadcasted_iota(jnp.int32, (128, 128), 1)

    def scales_of(n):
        here = tokens[x, n, k].astype(F32)
        for q in range(4):
            column = jnp.sum(jnp.where(diagonal, here[q : q + 1, :], 0.0), axis=1, keepdims=True)
            chosen = column == vocab
            quarter = pl.ds(pl.multiple_of(n * 512 + 128 * q, 128), 128)
            one_hot[quarter, :] = chosen.astype(BF)
            total = jnp.sum(
                jnp.where(chosen, 2.0 * products[quarter, :] + norms, 0.0), axis=1, keepdims=True
            )
            total = jnp.maximum(total + D / 2, 0.0)
            inverse[quarter, :] = lax.rsqrt(total * (1.0 / D) + EPSILON)

    each(0, 4, scales_of)

    hand_on((x + 2) % 4, 1 - b, False)
    for rx, rb in [(x, b)] + rows:
        j = 2 * rx + rb
        k3 = 2 * rb + 1 - c
        arrive(tokens.at[rx, :, k3], r3.at[1, j], partner)
        arrive(w_all.at[:, rx, :, k3], r3.at[0, j], partner)

    slot = lax.broadcasted_iota(jnp.int32, (64, 1), 0)
    target = offset + (slot // 16) * 256 + 16 * r + slot % 16
    lane = lax.broadcasted_iota(jnp.int32, (1, 128), 1)
    found = jnp.zeros((64, 128), F32)
    for q in range(3):
        bytes_here = tokens[3, 3, 1 + q].astype(F32)
        for t in range(4):
            hit = target == lane + (31232 + 512 * q + 128 * t)
            found = found + jnp.where(hit, bytes_here[t : t + 1, :], 0.0)
    column = jnp.sum(found, axis=1, keepdims=True)
    looked = jnp.dot((column == vocab[:64]).astype(BF), table_ref[...], preferred_element_type=F32)
    for t in range(4):
        s, co = start_of(4 + t)
        wave = s * cos_ref[40:56] + co * sin_ref[40:56]
        latent[16 * t : 16 * t + 16, :] = rms_rows(looked[16 * t : 16 * t + 16] + wave).astype(BF)
    weights_of = w_all.reshape(3, D, HD)
    q_own[...] = jnp.dot(latent[...], weights_of[0], preferred_element_type=F32).astype(BF)
    asked = Exchange(q_own, q_all, s_q, r_q, r, row_of, 16, whole=True)
    asked.start()
    ends.append(asked.wait_sent)

    wkv[:, :HD] = weights_of[1]
    wkv[:, HD:] = weights_of[2]
    table_w = jnp.dot(table_ref[...], wkv[...], preferred_element_type=F32)
    tw[0] = table_w.astype(BF)
    tw[1] = (table_w - table_w.astype(BF).astype(F32)).astype(BF)

    def keys_of(n):
        run = pl.ds(pl.multiple_of(n * 512, 512), 512)
        both = jnp.dot(waves[run, :], wkv[...], preferred_element_type=F32)
        both = both + jnp.dot(one_hot[run, :], tw[0], preferred_element_type=F32)
        both = both + jnp.dot(one_hot[run, :], tw[1], preferred_element_type=F32)
        both = (both * inverse[run, :]).astype(BF)
        keys[run, :] = both[:, :HD]
        values[run, :] = both[:, HD:]

    each(0, 4, keys_of)
    asked.wait_all()

    key_col = lax.broadcasted_iota(jnp.int32, (1, 2048), 1)
    key_place = 512 * (16 * x + 4 * (key_col // 512) + k) + key_col % 512
    outs = Exchange(o_msg, o_came, s_o, r_o, r, row_of, 16)
    stats = Exchange(st_msg, st_came, s_st, r_st, r, row_of, 16)
    diagonal64 = lax.broadcasted_iota(jnp.int32, (64, 128), 0) == lax.broadcasted_iota(jnp.int32, (64, 128), 1)

    def attend(step):
        t = (x + 1 + step) % 4
        query = q_all[pl.ds(4 * t, 4)].reshape(256, HD)
        scores = lax.dot_general(query, keys[...], across, preferred_element_type=F32) * SCALE
        row = lax.broadcasted_iota(jnp.int32, (256, 1), 0)
        row_place = offset + ((row // 16) % 4) * 256 + 16 * (4 * t + row // 64) + row % 16
        scores = jnp.where(key_place > row_place, MASKED, scores)
        peak = jnp.max(scores, axis=1, keepdims=True)
        weights = jnp.exp(scores - peak).astype(BF)
        total = jnp.sum(weights.astype(F32), axis=1, keepdims=True)
        out = jnp.dot(weights, values[...], preferred_element_type=F32).astype(BF)
        for g in range(4):
            some = slice(64 * g, 64 * g + 64)
            j = 4 * t + g
            o_msg[j] = out[some]
            st_msg[j, 0:1, :] = jnp.sum(jnp.where(diagonal64, peak[some], 0.0), axis=0, keepdims=True)
            st_msg[j, 1:2, :] = jnp.sum(jnp.where(diagonal64, total[some], 0.0), axis=0, keepdims=True)

            @pl.when(j != r)
            def _():
                stats.copy(j).start()
                outs.copy(j).start()

    each(0, 4, attend)
    o_came[r] = o_msg[r]
    st_came[r] = st_msg[r]
    stats.wait_all()
    outs.wait_all()
    ends += [stats.wait_sent, outs.wait_sent]

    halves = (w_in, w_out)
    others = [(x + d) % 4 for d in (1, 3, 2)]

    def along(h):
        copies = [push(halves[h].at[x], halves[h].at[x], sw2.at[h, i], rw2.at[h, x], at(i, a, b, c, y)) for i in others]
        return copies + [forward(h, x)]

    def forward(h, i):
        return push(halves[h].at[i], halves[h].at[i], sw3.at[h, i], rw3.at[h, i], partner)

    def set_out(h):
        @pl.when(source)
        def _():
            mine[h].wait()

        @pl.when(jnp.logical_and(main, jnp.logical_not(source)))
        def _():
            arrive(halves[h].at[x], rw1.at[h], partner)

        @pl.when(main)
        def _():
            for copy in along(h):
                copy.start()

    def hand_over(h):
        @pl.when(main)
        def _():
            for i in others:
                arrive(halves[h].at[i], rw2.at[h, i], partner)
                forward(h, i).start()

    def receive(h):
        @pl.when(jnp.logical_not(main))
        def _():
            for i in range(4):
                arrive(halves[h].at[i], rw3.at[h, i], partner)

    maxima, totals = st_came[:, 0, :], st_came[:, 1, :]
    factor = jnp.exp(maxima - jnp.max(maxima, axis=0, keepdims=True))
    factor = factor / jnp.sum(factor * totals, axis=0, keepdims=True)
    attended = jnp.zeros((64, HD), F32)
    for j in range(16):
        column = jnp.sum(jnp.where(diagonal64, factor[j : j + 1, :], 0.0), axis=1, keepdims=True)
        attended = attended + column * o_came[j].astype(F32)
    for copy in loads:
        copy.wait()

    def shares(rows, weight, out):
        for q in range(4):
            part = jnp.dot(rows, weight[:, 512 * q : 512 * q + 512], preferred_element_type=F32).astype(BF)
            for t in range(4):
                out[4 * t + q] = part[16 * t : 16 * t + 16]

    def rows_normed(blocks):
        for t in range(4):
            wide = jnp.concatenate([blocks[4 * t + q] for q in range(4)], axis=1).astype(F32)
            normed[16 * t : 16 * t + 16, :] = rms_rows(wide).astype(BF)

    shares(attended.astype(BF), w_co, msg)
    summed = Exchange(msg, came, s_m, r_m, p, head_of, 16)
    summed.start()
    set_out(0)
    own_block = (pl.ds(pl.multiple_of(16 * y, 16), 16), pl.ds(pl.multiple_of(512 * a, 512), 512))
    own_latent = latent[own_block].astype(F32)
    summed.wait_all()
    ends.append(summed.wait_sent)
    first = jnp.sum(came[...].astype(F32), axis=0) + own_latent
    own[...] = first.astype(BF)
    spread = Exchange(own, all_rows, s_a, r_a, p, head_of, 16, whole=True)
    spread.start()
    spread.wait_all()
    ends.append(spread.wait_sent)

    rows_normed(all_rows)
    kv[:, :HD] = jnp.dot(normed[...], w_qkv[1], preferred_element_type=F32).astype(BF)
    kv[:, HD:] = jnp.dot(normed[...], w_qkv[2], preferred_element_type=F32).astype(BF)
    both = Exchange(kv, kv_all, s_kv, r_kv, r, row_of, 16, whole=True)
    both.start()
    hand_over(0)
    query = jnp.dot(normed[...], w_qkv[0], preferred_element_type=F32).astype(BF)
    both.wait_all()
    ends.append(both.wait_sent)

    all_keys = kv_all[:, :, :HD].reshape(LATENTS, HD)
    all_values = kv_all[:, :, HD:].reshape(LATENTS, HD)
    scores = lax.dot_general(query, all_keys, across, preferred_element_type=F32) * SCALE
    row = lax.broadcasted_iota(jnp.int32, (64, 1), 0)
    col = lax.broadcasted_iota(jnp.int32, (1, LATENTS), 1)
    row_place = (row // 16) * 256 + 16 * r + row % 16
    col_place = ((col // 16) % 4) * 256 + 16 * (col // 64) + col % 16
    scores = jnp.where(col_place > row_place, MASKED, scores)
    weights = jnp.exp(scores - jnp.max(scores, axis=1, keepdims=True)).astype(BF)
    total = jnp.sum(weights.astype(F32), axis=1, keepdims=True)
    attended = jnp.dot(weights, all_values, preferred_element_type=F32) / total
    shares(attended.astype(BF), w_so, msg2)
    summed2 = Exchange(msg2, came2, s_m2, r_m2, p, head_of, 16)
    summed2.start()
    set_out(1)
    summed2.wait_all()
    ends.append(summed2.wait_sent)
    second = first + jnp.sum(came2[...].astype(F32), axis=0)
    own2[...] = second.astype(BF)
    spread2 = Exchange(own2, all_rows2, s_a2, r_a2, p, head_of, 16, whole=True)
    spread2.start()
    hand_over(1)

    spread2.wait_all()
    ends.append(spread2.wait_sent)

    rows_normed(all_rows2)
    receive(0)
    hidden = []
    for i in range(4):
        pre = jnp.dot(normed[...], w_in[i], preferred_element_type=F32)
        hidden.append(jax.nn.gelu(pre, approximate=True).astype(BF))
    hidden = jnp.concatenate(hidden, axis=1)
    receive(1)
    for q in range(4):
        columns = slice(512 * q, 512 * q + 512)
        partial[q] = jnp.dot(hidden, w_out[:, :, columns].reshape(512, 512), preferred_element_type=F32)
    here = pl.ds(pl.multiple_of(16 * y, 16), 16)
    partial[a, here, :] = partial[a, here, :] + second
    for j in range(16):
        some = slice(4 * j, 4 * j + 4)
        msg3[j] = jnp.concatenate([partial[q, some, :] for q in range(4)], axis=0).astype(BF)

    def last_copy(j):
        return push(msg3.at[j], came3.at[p], s_m3.at[j], r_m3.at[p], final_of(j))

    def last_start(i):
        j = (p + i) % 16

        @pl.when(j != final_self)
        def _():
            last_copy(j).start()

    each(0, 16, last_start)

    @pl.when(a == k)
    def _():
        came3[p] = msg3[4 * y + k]

    def last_wait(i):
        j = (p + i) % 16

        @pl.when(j != sender_self)
        def _():
            arrive(came3.at[j], r_m3.at[j], partner)

    each(0, 16, last_wait)
    ended = jnp.sum(came3[...].astype(F32), axis=0)
    for q in range(4):
        out_ref[:, 512 * q : 512 * q + 512] = ended[4 * q : 4 * q + 4]

    for end in ends:
        end()

    def last_sent(i):
        j = (p + i) % 16

        @pl.when(j != final_self)
        def _():
            last_copy(j).wait_send()

    each(0, 16, last_sent)

    @pl.when(source)
    def _():
        for copy in step1:
            copy.wait_send()

    @pl.when(main)
    def _():
        for h in range(2):
            for copy in along(h):
                copy.wait_send()
            for i in others:
                forward(h, i).wait_send()


def per_device(
    token_ids,
    latent_offset,
    embed_table,
    cross_q,
    cross_kv,
    cross_out,
    self_qkv,
    self_out,
    mlp_in,
    mlp_out,
):
    vmem = pl.BlockSpec(memory_space=pltpu.VMEM)
    hbm = pl.BlockSpec(memory_space=pl.ANY)
    dma = pltpu.SemaphoreType.DMA
    rows = pl.pallas_call(
        whole_kernel,
        out_shape=jax.ShapeDtypeStruct((4, D), F32),
        in_specs=[pl.BlockSpec(memory_space=pltpu.SMEM)] + [vmem] * 3 + [hbm] * 6,
        out_specs=vmem,
        scratch_shapes=[
            pltpu.VMEM((256, D), BF),
            pltpu.VMEM((4, 3, 32, HD), BF),
            pltpu.VMEM((3, 4, 4, 4, 32, HD), BF),
            pltpu.VMEM((4, 4, 4, 4, 128), jnp.int32),
            pltpu.VMEM((D, 2 * HD), BF),
            pltpu.VMEM((2, 256, 2 * HD), BF),
            pltpu.VMEM((56, D), F32),
            pltpu.VMEM((56, D), F32),
            pltpu.VMEM((32, D), F32),
            pltpu.VMEM((32, D), F32),
            pltpu.VMEM((2048, D), BF),
            pltpu.VMEM((2048, 256), F32),
            pltpu.VMEM((2048, 256), BF),
            pltpu.VMEM((2048, 1), F32),
            pltpu.VMEM((64, D), BF),
            pltpu.VMEM((2048, HD), BF),
            pltpu.VMEM((2048, HD), BF),
            pltpu.VMEM((64, HD), BF),
            pltpu.VMEM((16, 64, HD), BF),
            pltpu.VMEM((16, 64, HD), BF),
            pltpu.VMEM((16, 64, HD), BF),
            pltpu.VMEM((16, 8, 128), F32),
            pltpu.VMEM((16, 8, 128), F32),
            pltpu.VMEM((HD, D), BF),
            pltpu.VMEM((3, D, HD), BF),
            pltpu.VMEM((HD, D), BF),
            pltpu.VMEM((16, 16, 512), BF),
            pltpu.VMEM((16, 16, 512), BF),
            pltpu.VMEM((16, 512), BF),
            pltpu.VMEM((16, 16, 512), BF),
            pltpu.VMEM((64, D), BF),
            pltpu.VMEM((64, 2 * HD), BF),
            pltpu.VMEM((16, 64, 2 * HD), BF),
            pltpu.VMEM((16, 16, 512), BF),
            pltpu.VMEM((16, 16, 512), BF),
            pltpu.VMEM((16, 512), BF),
            pltpu.VMEM((16, 16, 512), BF),
            pltpu.VMEM((4, D, HD), BF),
            pltpu.VMEM((4, HD, D), BF),
            pltpu.VMEM((4, 64, 512), F32),
            pltpu.VMEM((16, 16, 512), BF),
            pltpu.VMEM((16, 16, 512), BF),
            dma((4,)),
            dma((2, 4)),
            dma((2, 4)),
            dma((2, 8)),
            dma((2, 8)),
            dma((2, 8)),
            dma((2, 8)),
        ]
        + [dma((16,))] * 18
        + [dma((2,)), dma((2,)), dma((2,)), dma((2, 4)), dma((2, 4)), dma((2, 4)), dma((2, 4))],
        compiler_params=pltpu.CompilerParams(
            collective_id=0, has_side_effects=True, vmem_limit_bytes=VLIMIT
        ),
    )(
        latent_offset, token_ids.reshape(4, 128), cross_q, cross_kv, embed_table, cross_out, self_qkv, self_out, mlp_in, mlp_out,
    )
    return rows.astype(BF)[None]


def solution(mesh):
    placed = (
        P("ctx"),
        P(),
        P(),
        P("ctx", "lat"),
        P(None, "ctx", "lat"),
        P("lat", None),
        P(None, None, "lat"),
        P("lat", None),
        P(None, "ctx"),
        P("ctx", None),
    )
    return jax.shard_map(
        per_device, mesh=mesh, in_specs=placed, out_specs=P("lat", "ctx", None), check_vma=False
    )
```

```python
import math

import jax
import jax.numpy as jnp
from jax import lax
from jax.experimental import pallas as pl
from jax.experimental.pallas import tpu as pltpu
from jax.sharding import PartitionSpec as P

MESH = pl.DeviceIdType.MESH
HD = 128
D = 2048
LATENTS = 1024
EPSILON = 1e-06
MASKED = -1e30
SCALE = 1.0 / math.sqrt(HD)
BF = jnp.bfloat16
F32 = jnp.float32
VLIMIT = 58 * 1024 * 1024


def place():
    g = lax.axis_index("ctx")
    y = lax.axis_index("lat")
    return g // 16, (g // 4) % 4, (g // 2) % 2, g % 2, y


def at(x, a, b, c, y):
    return (16 * x + 4 * a + 2 * b + c, y)


def push(src, dst, send_sem, recv_sem, device):
    copy = pltpu.make_async_remote_copy(
        src_ref=src,
        dst_ref=dst,
        send_sem=send_sem,
        recv_sem=recv_sem,
        device_id=device,
        device_id_type=MESH,
    )
    return copy


def arrive(dst, recv_sem, device):
    push(dst, dst, recv_sem, recv_sem, device).wait_recv()


def each(first, last, body):
    def step(k, carry):
        body(k)
        return carry

    lax.fori_loop(first, last, step, 0)


class Exchange:
    def __init__(self, src, dst, send, recv, me, device_of, n, whole=False):
        self.src, self.dst, self.send, self.recv = src, dst, send, recv
        self.me, self.device_of, self.n, self.whole = me, device_of, n, whole

    def copy(self, j):
        src = self.src if self.whole else self.src.at[j]
        return push(src, self.dst.at[self.me], self.send.at[j], self.recv.at[self.me], self.device_of(j))

    def start(self):
        def one(k):
            self.copy((self.me + k) % self.n).start()

        each(1, self.n, one)
        self.dst[self.me] = self.src[...] if self.whole else self.src[self.me]

    def wait_all(self):
        def one(k):
            j = (self.me + self.n - k) % self.n
            arrive(self.dst.at[j], self.recv.at[j], self.device_of(j))

        each(1, self.n, one)

    def wait_sent(self):
        def one(k):
            self.copy((self.me + k) % self.n).wait_send()

        each(1, self.n, one)


def rms_rows(values):
    return values * lax.rsqrt(jnp.mean(values * values, axis=-1, keepdims=True) + EPSILON)


def whole_kernel(
    offset_ref, tok_ref, q_ref, kv_ref,
    table_hbm, cout_ref, sqkv_ref, sout_ref, in_ref, mout_ref,
    out_ref,
    table_ref, stage, w_all, tokens, wkv, tw, sin_ref, cos_ref, rows_sin, rows_cos, waves, products, one_hot, inverse, latent, keys, values, q_own, q_all,
    o_msg, o_came, st_msg, st_came, w_co, w_qkv, w_so, msg, came, own, all_rows, normed, kv, kv_all, msg2, came2,
    own2, all_rows2, w_in, w_out, partial, msg3, came3,
    load, s1, r1, s2, r2, s3, r3, s_q, r_q, s_o, r_o, s_st, r_st, s_m, r_m, s_a, r_a, s_kv, r_kv, s_m2, r_m2,
    s_a2, r_a2, s_m3, r_m3, own_w, sw1, rw1, sw2, rw2, sw3, rw3,
):
    x, a, b, c, y = place()
    k = 2 * b + c
    r = 4 * x + k
    p = 4 * y + a
    j_me = 2 * x + b
    partner = at(x, a, b, 1 - c, y)

    def row_of(j):
        return at(j // 4, a, (j // 2) % 2, j % 2, y)

    def head_of(j):
        return at(x, j % 4, b, c, j // 4)

    def final_of(j):
        return at(x, k, (j // 2) % 2, j % 2, j // 4)

    def sender_of(j):
        return at(x, j % 4, a // 2, a % 2, j // 4)

    final_self = jnp.where(a == k, 4 * y + k, 16)
    sender_self = jnp.where(a == k, p, 16)

    barrier = pltpu.get_barrier_semaphore()

    def hello(device):
        pl.semaphore_signal(barrier, inc=1, device_id=device, device_id_type=MESH)

    each(1, 16, lambda i: hello(row_of((r + i) % 16)))
    each(1, 16, lambda i: hello(head_of((p + i) % 16)))

    def hello_sender(j):
        @pl.when(j != sender_self)
        def _():
            hello(sender_of(j))

    each(0, 16, hello_sender)
    row_at = pl.multiple_of(a * HD, HD)
    table_load = pltpu.make_async_copy(table_hbm, table_ref, load.at[3])
    table_load.start()
    loads = [
        pltpu.make_async_copy(cout_ref.at[pl.ds(row_at, HD), :], w_co, load.at[0]),
        pltpu.make_async_copy(sqkv_ref.at[:, :, pl.ds(row_at, HD)], w_qkv, load.at[1]),
        pltpu.make_async_copy(sout_ref.at[pl.ds(row_at, HD), :], w_so, load.at[2]),
    ]
    for copy in loads:
        copy.start()
    for h in range(4):
        stage[h, 0] = q_ref[:, 128 * h : 128 * h + 128]
        stage[h, 1] = kv_ref[0, :, 128 * h : 128 * h + 128]
        stage[h, 2] = kv_ref[1, :, 128 * h : 128 * h + 128]
    pl.semaphore_wait(barrier, jnp.where(a == k, 45, 46))
    ends = []

    heads = [(a + d) % 4 for d in range(1, 4)]
    rows = [((x + dx) % 4, (b + db) % 2) for dx in (0, 1, 3, 2) for db in (0, 1) if dx or db]
    first_copies = []
    for h in heads:
        there = at(x, h, b, c, y)
        first_copies.append(push(tok_ref, tokens.at[x, a, k], s1.at[1, h], r1.at[1, a], there))
        first_copies.append(push(stage.at[h], w_all.at[:, x, a, k], s1.at[0, h], r1.at[0, a], there))
    for copy in first_copies:
        copy.start()
        ends.append(copy.wait_send)
    main = c == y // 2
    source = jnp.logical_and(main, b == y % 2)
    beside = at(x, a, 1 - b, c, y)
    mine = [
        pltpu.make_async_copy(in_ref, w_in.at[x], own_w.at[0]),
        pltpu.make_async_copy(mout_ref, w_out.at[x], own_w.at[1]),
    ]
    step1 = [
        push(in_ref, w_in.at[x], sw1.at[0], rw1.at[0], beside),
        push(mout_ref, w_out.at[x], sw1.at[1], rw1.at[1], beside),
    ]

    @pl.when(source)
    def _():
        for copy in step1[:1] + mine:
            copy.start()

    tokens[x, a, k] = tok_ref[...]
    for part in range(3):
        w_all[part, x, a, k] = stage[a, part]

    offset = offset_ref[0]
    index = lax.broadcasted_iota(jnp.int32, (56, 1), 0)
    places = jnp.where(index < 4, 512 * (16 * x + 4 * index + k), offset + 256 * (index - 4) + 16 * r)
    places = jnp.where(index < 8, places, jnp.where(index < 40, 16 * (index - 8), index - 40)).astype(F32)

    def table_columns(j):
        lanes = pl.ds(pl.multiple_of(j * 256, 256), 256)
        pair = ((j * 256 + lax.broadcasted_iota(jnp.int32, (1, 256), 1)) // 2).astype(F32)
        angles = places * jnp.exp(pair * (-2.0 * math.log(10000.0) / D))
        sin_ref[:, lanes] = jnp.sin(angles)
        cos_ref[:, lanes] = jnp.cos(angles)

    each(0, 8, table_columns)

    for h in heads:
        arrive(tokens.at[x, h, k], r1.at[1, h], partner)
        arrive(w_all.at[:, x, h, k], r1.at[0, h], partner)
    second_copies = []
    for rx, rb in rows:
        there = at(rx, a, rb, c, y)
        j = 2 * rx + rb
        second_copies.append(push(tokens.at[x, :, k], tokens.at[x, :, k], s2.at[1, j], r2.at[1, j_me], there))
        second_copies.append(push(w_all.at[:, x, :, k], w_all.at[:, x, :, k], s2.at[0, j], r2.at[0, j_me], there))
    for copy in second_copies:
        copy.start()
        ends.append(copy.wait_send)

    def onward(rx, rb):
        j = 2 * rx + rb
        k2 = 2 * rb + c
        return [
            push(tokens.at[rx, :, k2], tokens.at[rx, :, k2], s3.at[1, j], r3.at[1, j], partner),
            push(w_all.at[:, rx, :, k2], w_all.at[:, rx, :, k2], s3.at[0, j], r3.at[0, j], partner),
        ]

    third_copies = onward(x, b)
    for copy in third_copies:
        copy.start()
        ends.append(copy.wait_send)

    odd = lax.broadcasted_iota(jnp.int32, (1, D), 1) % 2 == 1
    mid_sin, mid_cos = sin_ref[8:40], cos_ref[8:40]

    def start_of(n):
        s, co = sin_ref[pl.ds(n, 1)], cos_ref[pl.ds(n, 1)]
        return jnp.where(odd, co, s), jnp.where(odd, -s, co)

    def waves_of(n):
        s, co = start_of(n)
        rows_sin[...] = s * mid_cos + co * mid_sin
        rows_cos[...] = co * mid_cos - s * mid_sin

        def columns(j):
            lanes = pl.ds(pl.multiple_of(j * 128, 128), 128)
            low_sin, low_cos = sin_ref[40:56, lanes], cos_ref[40:56, lanes]
            for m in range(32):
                wave = rows_sin[m : m + 1, lanes] * low_cos + rows_cos[m : m + 1, lanes] * low_sin
                waves[pl.ds(pl.multiple_of(n * 512 + 16 * m, 16), 16), lanes] = wave.astype(BF)

        each(0, 16, columns)

    each(0, 4, waves_of)

    table_load.wait()
    square = table_ref[...].astype(F32)
    square = square * square
    high = square.astype(BF)
    lower = (square - high.astype(F32)).astype(BF)
    ones = jnp.ones((8, D), BF)
    across = (((1,), (1,)), ((), ()))
    norms = lax.dot_general(ones, high, across, preferred_element_type=F32) + lax.dot_general(
        ones, lower, across, preferred_element_type=F32
    )
    norms = norms[0:1]

    def products_of(n):
        run = pl.ds(pl.multiple_of(n * 512, 512), 512)
        products[run, :] = lax.dot_general(waves[run, :], table_ref[...], across, preferred_element_type=F32)

    each(0, 4, products_of)

    vocab = lax.broadcasted_iota(jnp.int32, (128, 256), 1).astype(F32)
    diagonal = lax.broadcasted_iota(jnp.int32, (128, 128), 0) == lax.broadcasted_iota(jnp.int32, (128, 128), 1)

    def scales_of(n):
        here = tokens[x, n, k].astype(F32)
        for q in range(4):
            column = jnp.sum(jnp.where(diagonal, here[q : q + 1, :], 0.0), axis=1, keepdims=True)
            chosen = column == vocab
            quarter = pl.ds(pl.multiple_of(n * 512 + 128 * q, 128), 128)
            one_hot[quarter, :] = chosen.astype(BF)
            total = jnp.sum(
                jnp.where(chosen, 2.0 * products[quarter, :] + norms, 0.0), axis=1, keepdims=True
            )
            total = jnp.maximum(total + D / 2, 0.0)
            inverse[quarter, :] = lax.rsqrt(total * (1.0 / D) + EPSILON)

    each(0, 4, scales_of)

    for rx, rb in rows:
        sx, sb = (2 * x + 4 - rx) % 4, rb
        j = 2 * sx + sb
        k2 = 2 * sb + c
        arrive(tokens.at[sx, :, k2], r2.at[1, j], partner)
        arrive(w_all.at[:, sx, :, k2], r2.at[0, j], partner)
        more = onward(sx, sb)
        for copy in more:
            copy.start()
            ends.append(copy.wait_send)
    for rx, rb in [(x, b)] + rows:
        j = 2 * rx + rb
        k3 = 2 * rb + 1 - c
        arrive(tokens.at[rx, :, k3], r3.at[1, j], partner)
        arrive(w_all.at[:, rx, :, k3], r3.at[0, j], partner)

    slot = lax.broadcasted_iota(jnp.int32, (64, 1), 0)
    target = offset + (slot // 16) * 256 + 16 * r + slot % 16
    lane = lax.broadcasted_iota(jnp.int32, (1, 128), 1)
    found = jnp.zeros((64, 128), F32)
    for q in range(3):
        bytes_here = tokens[3, 3, 1 + q].astype(F32)
        for t in range(4):
            hit = target == lane + (31232 + 512 * q + 128 * t)
            found = found + jnp.where(hit, bytes_here[t : t + 1, :], 0.0)
    column = jnp.sum(found, axis=1, keepdims=True)
    looked = jnp.dot((column == vocab[:64]).astype(BF), table_ref[...], preferred_element_type=F32)
    for t in range(4):
        s, co = start_of(4 + t)
        wave = s * cos_ref[40:56] + co * sin_ref[40:56]
        latent[16 * t : 16 * t + 16, :] = rms_rows(looked[16 * t : 16 * t + 16] + wave).astype(BF)
    weights_of = w_all.reshape(3, D, HD)
    q_own[...] = jnp.dot(latent[...], weights_of[0], preferred_element_type=F32).astype(BF)
    asked = Exchange(q_own, q_all, s_q, r_q, r, row_of, 16, whole=True)
    asked.start()
    ends.append(asked.wait_sent)

    wkv[:, :HD] = weights_of[1]
    wkv[:, HD:] = weights_of[2]
    table_w = jnp.dot(table_ref[...], wkv[...], preferred_element_type=F32)
    tw[0] = table_w.astype(BF)
    tw[1] = (table_w - table_w.astype(BF).astype(F32)).astype(BF)

    def keys_of(n):
        run = pl.ds(pl.multiple_of(n * 512, 512), 512)
        both = jnp.dot(waves[run, :], wkv[...], preferred_element_type=F32)
        both = both + jnp.dot(one_hot[run, :], tw[0], preferred_element_type=F32)
        both = both + jnp.dot(one_hot[run, :], tw[1], preferred_element_type=F32)
        both = (both * inverse[run, :]).astype(BF)
        keys[run, :] = both[:, :HD]
        values[run, :] = both[:, HD:]

    each(0, 4, keys_of)
    asked.wait_all()

    key_col = lax.broadcasted_iota(jnp.int32, (1, 2048), 1)
    key_place = 512 * (16 * x + 4 * (key_col // 512) + k) + key_col % 512
    outs = Exchange(o_msg, o_came, s_o, r_o, r, row_of, 16)
    stats = Exchange(st_msg, st_came, s_st, r_st, r, row_of, 16)
    diagonal64 = lax.broadcasted_iota(jnp.int32, (64, 128), 0) == lax.broadcasted_iota(jnp.int32, (64, 128), 1)

    def attend(step):
        t = (x + 1 + step) % 4
        query = q_all[pl.ds(4 * t, 4)].reshape(256, HD)
        scores = lax.dot_general(query, keys[...], across, preferred_element_type=F32) * SCALE
        row = lax.broadcasted_iota(jnp.int32, (256, 1), 0)
        row_place = offset + ((row // 16) % 4) * 256 + 16 * (4 * t + row // 64) + row % 16
        scores = jnp.where(key_place > row_place, MASKED, scores)
        peak = jnp.max(scores, axis=1, keepdims=True)
        weights = jnp.exp(scores - peak).astype(BF)
        total = jnp.sum(weights.astype(F32), axis=1, keepdims=True)
        out = jnp.dot(weights, values[...], preferred_element_type=F32).astype(BF)
        for g in range(4):
            some = slice(64 * g, 64 * g + 64)
            j = 4 * t + g
            o_msg[j] = out[some]
            st_msg[j, 0:1, :] = jnp.sum(jnp.where(diagonal64, peak[some], 0.0), axis=0, keepdims=True)
            st_msg[j, 1:2, :] = jnp.sum(jnp.where(diagonal64, total[some], 0.0), axis=0, keepdims=True)

            @pl.when(j != r)
            def _():
                stats.copy(j).start()
                outs.copy(j).start()

    each(0, 4, attend)
    o_came[r] = o_msg[r]
    st_came[r] = st_msg[r]
    stats.wait_all()
    outs.wait_all()
    ends += [stats.wait_sent, outs.wait_sent]

    halves = (w_in, w_out)
    others = [(x + d) % 4 for d in (1, 3, 2)]

    def along(h):
        copies = [push(halves[h].at[x], halves[h].at[x], sw2.at[h, i], rw2.at[h, x], at(i, a, b, c, y)) for i in others]
        return copies + [forward(h, x)]

    def forward(h, i):
        return push(halves[h].at[i], halves[h].at[i], sw3.at[h, i], rw3.at[h, i], partner)

    def set_out(h):
        @pl.when(source)
        def _():
            mine[h].wait()

        @pl.when(jnp.logical_and(main, jnp.logical_not(source)))
        def _():
            arrive(halves[h].at[x], rw1.at[h], partner)

        @pl.when(main)
        def _():
            for copy in along(h):
                copy.start()

    def hand_over(h):
        @pl.when(main)
        def _():
            for i in others:
                arrive(halves[h].at[i], rw2.at[h, i], partner)
                forward(h, i).start()

    def receive(h):
        @pl.when(jnp.logical_not(main))
        def _():
            for i in range(4):
                arrive(halves[h].at[i], rw3.at[h, i], partner)

    maxima, totals = st_came[:, 0, :], st_came[:, 1, :]
    factor = jnp.exp(maxima - jnp.max(maxima, axis=0, keepdims=True))
    factor = factor / jnp.sum(factor * totals, axis=0, keepdims=True)
    attended = jnp.zeros((64, HD), F32)
    for j in range(16):
        column = jnp.sum(jnp.where(diagonal64, factor[j : j + 1, :], 0.0), axis=1, keepdims=True)
        attended = attended + column * o_came[j].astype(F32)
    for copy in loads:
        copy.wait()

    def shares(rows, weight, out):
        for q in range(4):
            part = jnp.dot(rows, weight[:, 512 * q : 512 * q + 512], preferred_element_type=F32).astype(BF)
            for t in range(4):
                out[4 * t + q] = part[16 * t : 16 * t + 16]

    def rows_normed(blocks):
        for t in range(4):
            wide = jnp.concatenate([blocks[4 * t + q] for q in range(4)], axis=1).astype(F32)
            normed[16 * t : 16 * t + 16, :] = rms_rows(wide).astype(BF)

    shares(attended.astype(BF), w_co, msg)
    summed = Exchange(msg, came, s_m, r_m, p, head_of, 16)
    summed.start()
    set_out(0)
    own_block = (pl.ds(pl.multiple_of(16 * y, 16), 16), pl.ds(pl.multiple_of(512 * a, 512), 512))
    own_latent = latent[own_block].astype(F32)
    summed.wait_all()
    ends.append(summed.wait_sent)
    first = jnp.sum(came[...].astype(F32), axis=0) + own_latent
    own[...] = first.astype(BF)
    spread = Exchange(own, all_rows, s_a, r_a, p, head_of, 16, whole=True)
    spread.start()

    @pl.when(source)
    def _():
        step1[1].start()

    spread.wait_all()
    ends.append(spread.wait_sent)

    rows_normed(all_rows)
    kv[:, :HD] = jnp.dot(normed[...], w_qkv[1], preferred_element_type=F32).astype(BF)
    kv[:, HD:] = jnp.dot(normed[...], w_qkv[2], preferred_element_type=F32).astype(BF)
    both = Exchange(kv, kv_all, s_kv, r_kv, r, row_of, 16, whole=True)
    both.start()
    hand_over(0)
    query = jnp.dot(normed[...], w_qkv[0], preferred_element_type=F32).astype(BF)
    both.wait_all()
    ends.append(both.wait_sent)

    all_keys = kv_all[:, :, :HD].reshape(LATENTS, HD)
    all_values = kv_all[:, :, HD:].reshape(LATENTS, HD)
    scores = lax.dot_general(query, all_keys, across, preferred_element_type=F32) * SCALE
    row = lax.broadcasted_iota(jnp.int32, (64, 1), 0)
    col = lax.broadcasted_iota(jnp.int32, (1, LATENTS), 1)
    row_place = (row // 16) * 256 + 16 * r + row % 16
    col_place = ((col // 16) % 4) * 256 + 16 * (col // 64) + col % 16
    scores = jnp.where(col_place > row_place, MASKED, scores)
    weights = jnp.exp(scores - jnp.max(scores, axis=1, keepdims=True)).astype(BF)
    total = jnp.sum(weights.astype(F32), axis=1, keepdims=True)
    attended = jnp.dot(weights, all_values, preferred_element_type=F32) / total
    shares(attended.astype(BF), w_so, msg2)
    summed2 = Exchange(msg2, came2, s_m2, r_m2, p, head_of, 16)
    summed2.start()
    set_out(1)
    summed2.wait_all()
    ends.append(summed2.wait_sent)
    second = first + jnp.sum(came2[...].astype(F32), axis=0)
    own2[...] = second.astype(BF)
    spread2 = Exchange(own2, all_rows2, s_a2, r_a2, p, head_of, 16, whole=True)
    spread2.start()
    hand_over(1)

    spread2.wait_all()
    ends.append(spread2.wait_sent)

    rows_normed(all_rows2)
    receive(0)
    hidden = []
    for i in range(4):
        pre = jnp.dot(normed[...], w_in[i], preferred_element_type=F32)
        hidden.append(jax.nn.gelu(pre, approximate=True).astype(BF))
    hidden = jnp.concatenate(hidden, axis=1)
    receive(1)
    for q in range(4):
        columns = slice(512 * q, 512 * q + 512)
        partial[q] = jnp.dot(hidden, w_out[:, :, columns].reshape(512, 512), preferred_element_type=F32)
    here = pl.ds(pl.multiple_of(16 * y, 16), 16)
    partial[a, here, :] = partial[a, here, :] + second
    for j in range(16):
        some = slice(4 * j, 4 * j + 4)
        msg3[j] = jnp.concatenate([partial[q, some, :] for q in range(4)], axis=0).astype(BF)

    def last_copy(j):
        return push(msg3.at[j], came3.at[p], s_m3.at[j], r_m3.at[p], final_of(j))

    def last_start(i):
        j = (p + i) % 16

        @pl.when(j != final_self)
        def _():
            last_copy(j).start()

    each(0, 16, last_start)

    @pl.when(a == k)
    def _():
        came3[p] = msg3[4 * y + k]

    def last_wait(i):
        j = (p + i) % 16

        @pl.when(j != sender_self)
        def _():
            arrive(came3.at[j], r_m3.at[j], partner)

    each(0, 16, last_wait)
    ended = jnp.sum(came3[...].astype(F32), axis=0)
    for q in range(4):
        out_ref[:, 512 * q : 512 * q + 512] = ended[4 * q : 4 * q + 4]

    for end in ends:
        end()

    def last_sent(i):
        j = (p + i) % 16

        @pl.when(j != final_self)
        def _():
            last_copy(j).wait_send()

    each(0, 16, last_sent)

    @pl.when(source)
    def _():
        for copy in step1:
            copy.wait_send()

    @pl.when(main)
    def _():
        for h in range(2):
            for copy in along(h):
                copy.wait_send()
            for i in others:
                forward(h, i).wait_send()


def per_device(
    token_ids,
    latent_offset,
    embed_table,
    cross_q,
    cross_kv,
    cross_out,
    self_qkv,
    self_out,
    mlp_in,
    mlp_out,
):
    vmem = pl.BlockSpec(memory_space=pltpu.VMEM)
    hbm = pl.BlockSpec(memory_space=pl.ANY)
    dma = pltpu.SemaphoreType.DMA
    rows = pl.pallas_call(
        whole_kernel,
        out_shape=jax.ShapeDtypeStruct((4, D), F32),
        in_specs=[pl.BlockSpec(memory_space=pltpu.SMEM)] + [vmem] * 3 + [hbm] * 6,
        out_specs=vmem,
        scratch_shapes=[
            pltpu.VMEM((256, D), BF),
            pltpu.VMEM((4, 3, 32, HD), BF),
            pltpu.VMEM((3, 4, 4, 4, 32, HD), BF),
            pltpu.VMEM((4, 4, 4, 4, 128), jnp.int32),
            pltpu.VMEM((D, 2 * HD), BF),
            pltpu.VMEM((2, 256, 2 * HD), BF),
            pltpu.VMEM((56, D), F32),
            pltpu.VMEM((56, D), F32),
            pltpu.VMEM((32, D), F32),
            pltpu.VMEM((32, D), F32),
            pltpu.VMEM((2048, D), BF),
            pltpu.VMEM((2048, 256), F32),
            pltpu.VMEM((2048, 256), BF),
            pltpu.VMEM((2048, 1), F32),
            pltpu.VMEM((64, D), BF),
            pltpu.VMEM((2048, HD), BF),
            pltpu.VMEM((2048, HD), BF),
            pltpu.VMEM((64, HD), BF),
            pltpu.VMEM((16, 64, HD), BF),
            pltpu.VMEM((16, 64, HD), BF),
            pltpu.VMEM((16, 64, HD), BF),
            pltpu.VMEM((16, 8, 128), F32),
            pltpu.VMEM((16, 8, 128), F32),
            pltpu.VMEM((HD, D), BF),
            pltpu.VMEM((3, D, HD), BF),
            pltpu.VMEM((HD, D), BF),
            pltpu.VMEM((16, 16, 512), BF),
            pltpu.VMEM((16, 16, 512), BF),
            pltpu.VMEM((16, 512), BF),
            pltpu.VMEM((16, 16, 512), BF),
            pltpu.VMEM((64, D), BF),
            pltpu.VMEM((64, 2 * HD), BF),
            pltpu.VMEM((16, 64, 2 * HD), BF),
            pltpu.VMEM((16, 16, 512), BF),
            pltpu.VMEM((16, 16, 512), BF),
            pltpu.VMEM((16, 512), BF),
            pltpu.VMEM((16, 16, 512), BF),
            pltpu.VMEM((4, D, HD), BF),
            pltpu.VMEM((4, HD, D), BF),
            pltpu.VMEM((4, 64, 512), F32),
            pltpu.VMEM((16, 16, 512), BF),
            pltpu.VMEM((16, 16, 512), BF),
            dma((4,)),
            dma((2, 4)),
            dma((2, 4)),
            dma((2, 8)),
            dma((2, 8)),
            dma((2, 8)),
            dma((2, 8)),
        ]
        + [dma((16,))] * 18
        + [dma((2,)), dma((2,)), dma((2,)), dma((2, 4)), dma((2, 4)), dma((2, 4)), dma((2, 4))],
        compiler_params=pltpu.CompilerParams(
            collective_id=0, has_side_effects=True, vmem_limit_bytes=VLIMIT
        ),
    )(
        latent_offset, token_ids.reshape(4, 128), cross_q, cross_kv, embed_table, cross_out, self_qkv, self_out, mlp_in, mlp_out,
    )
    return rows.astype(BF)[None]


def solution(mesh):
    placed = (
        P("ctx"),
        P(),
        P(),
        P("ctx", "lat"),
        P(None, "ctx", "lat"),
        P("lat", None),
        P(None, None, "lat"),
        P("lat", None),
        P(None, "ctx"),
        P("ctx", None),
    )
    return jax.shard_map(
        per_device, mesh=mesh, in_specs=placed, out_specs=P("lat", "ctx", None), check_vma=False
    )
```

```python
import math

import jax
import jax.numpy as jnp
from jax import lax
from jax.experimental import pallas as pl
from jax.experimental.pallas import tpu as pltpu
from jax.sharding import PartitionSpec as P

MESH = pl.DeviceIdType.MESH
HD = 128
D = 2048
LATENTS = 1024
EPSILON = 1e-06
MASKED = -1e30
SCALE = 1.0 / math.sqrt(HD)
BF = jnp.bfloat16
F32 = jnp.float32
VLIMIT = 58 * 1024 * 1024


def place():
    g = lax.axis_index("ctx")
    y = lax.axis_index("lat")
    return g // 16, (g // 4) % 4, (g // 2) % 2, g % 2, y


def at(x, a, b, c, y):
    return (16 * x + 4 * a + 2 * b + c, y)


def push(src, dst, send_sem, recv_sem, device):
    copy = pltpu.make_async_remote_copy(
        src_ref=src,
        dst_ref=dst,
        send_sem=send_sem,
        recv_sem=recv_sem,
        device_id=device,
        device_id_type=MESH,
    )
    return copy


def arrive(dst, recv_sem, device):
    push(dst, dst, recv_sem, recv_sem, device).wait_recv()


def each(first, last, body):
    def step(k, carry):
        body(k)
        return carry

    lax.fori_loop(first, last, step, 0)


class Exchange:
    def __init__(self, src, dst, send, recv, me, device_of, n, whole=False):
        self.src, self.dst, self.send, self.recv = src, dst, send, recv
        self.me, self.device_of, self.n, self.whole = me, device_of, n, whole

    def copy(self, j):
        src = self.src if self.whole else self.src.at[j]
        return push(src, self.dst.at[self.me], self.send.at[j], self.recv.at[self.me], self.device_of(j))

    def start(self):
        def one(k):
            self.copy((self.me + k) % self.n).start()

        each(1, self.n, one)
        self.dst[self.me] = self.src[...] if self.whole else self.src[self.me]

    def wait_all(self):
        def one(k):
            j = (self.me + self.n - k) % self.n
            arrive(self.dst.at[j], self.recv.at[j], self.device_of(j))

        each(1, self.n, one)

    def wait_sent(self):
        def one(k):
            self.copy((self.me + k) % self.n).wait_send()

        each(1, self.n, one)


def rms_rows(values):
    return values * lax.rsqrt(jnp.mean(values * values, axis=-1, keepdims=True) + EPSILON)


def whole_kernel(
    offset_ref, tok_ref, q_ref, kv_ref,
    table_hbm, cout_ref, sqkv_ref, sout_ref, in_ref, mout_ref,
    out_ref,
    table_ref, stage, w_all, tokens, wkv, tw, sin_ref, cos_ref, rows_sin, rows_cos, waves, products, one_hot, inverse, latent, keys, values, q_own, q_all,
    o_msg, o_came, st_msg, st_came, w_co, w_qkv, w_so, msg, came, own, all_rows, normed, kv, kv_all, msg2, came2,
    own2, all_rows2, w_in, w_out, partial, msg3, came3,
    load, s1, r1, s2, r2, s3, r3, s_q, r_q, s_o, r_o, s_st, r_st, s_m, r_m, s_a, r_a, s_kv, r_kv, s_m2, r_m2,
    s_a2, r_a2, s_m3, r_m3, own_w, sw1, rw1, sw2, rw2, sw3, rw3,
):
    x, a, b, c, y = place()
    k = 2 * b + c
    r = 4 * x + k
    p = 4 * y + a
    j_me = 2 * x + b
    partner = at(x, a, b, 1 - c, y)

    def row_of(j):
        return at(j // 4, a, (j // 2) % 2, j % 2, y)

    def head_of(j):
        return at(x, j % 4, b, c, j // 4)

    def final_of(j):
        return at(x, k, (j // 2) % 2, j % 2, j // 4)

    def sender_of(j):
        return at(x, j % 4, a // 2, a % 2, j // 4)

    final_self = jnp.where(a == k, 4 * y + k, 16)
    sender_self = jnp.where(a == k, p, 16)

    barrier = pltpu.get_barrier_semaphore()

    def hello(device):
        pl.semaphore_signal(barrier, inc=1, device_id=device, device_id_type=MESH)

    each(1, 16, lambda i: hello(row_of((r + i) % 16)))
    each(1, 16, lambda i: hello(head_of((p + i) % 16)))

    def hello_sender(j):
        @pl.when(j != sender_self)
        def _():
            hello(sender_of(j))

    each(0, 16, hello_sender)
    row_at = pl.multiple_of(a * HD, HD)
    table_load = pltpu.make_async_copy(table_hbm, table_ref, load.at[3])
    table_load.start()
    loads = [
        pltpu.make_async_copy(cout_ref.at[pl.ds(row_at, HD), :], w_co, load.at[0]),
        pltpu.make_async_copy(sqkv_ref.at[:, :, pl.ds(row_at, HD)], w_qkv, load.at[1]),
        pltpu.make_async_copy(sout_ref.at[pl.ds(row_at, HD), :], w_so, load.at[2]),
    ]
    for copy in loads:
        copy.start()
    for h in range(4):
        stage[h, 0] = q_ref[:, 128 * h : 128 * h + 128]
        stage[h, 1] = kv_ref[0, :, 128 * h : 128 * h + 128]
        stage[h, 2] = kv_ref[1, :, 128 * h : 128 * h + 128]
    pl.semaphore_wait(barrier, jnp.where(a == k, 45, 46))
    ends = []

    heads = [(a + d) % 4 for d in range(1, 4)]
    rows = [((x + dx) % 4, (b + db) % 2) for dx in (0, 1, 3, 2) for db in (0, 1) if dx or db]
    first_copies = []
    for h in heads:
        there = at(x, h, b, c, y)
        first_copies.append(push(tok_ref, tokens.at[x, a, k], s1.at[1, h], r1.at[1, a], there))
        first_copies.append(push(stage.at[h], w_all.at[:, x, a, k], s1.at[0, h], r1.at[0, a], there))
    for copy in first_copies:
        copy.start()
        ends.append(copy.wait_send)
    main = c == y // 2
    source = jnp.logical_and(main, b == y % 2)
    beside = at(x, a, 1 - b, c, y)
    mine = [
        pltpu.make_async_copy(in_ref, w_in.at[x], own_w.at[0]),
        pltpu.make_async_copy(mout_ref, w_out.at[x], own_w.at[1]),
    ]
    step1 = [
        push(in_ref, w_in.at[x], sw1.at[0], rw1.at[0], beside),
        push(mout_ref, w_out.at[x], sw1.at[1], rw1.at[1], beside),
    ]

    @pl.when(source)
    def _():
        for copy in mine:
            copy.start()

    tokens[x, a, k] = tok_ref[...]
    for part in range(3):
        w_all[part, x, a, k] = stage[a, part]

    offset = offset_ref[0]
    index = lax.broadcasted_iota(jnp.int32, (56, 1), 0)
    places = jnp.where(index < 4, 512 * (16 * x + 4 * index + k), offset + 256 * (index - 4) + 16 * r)
    places = jnp.where(index < 8, places, jnp.where(index < 40, 16 * (index - 8), index - 40)).astype(F32)

    def table_columns(j):
        lanes = pl.ds(pl.multiple_of(j * 256, 256), 256)
        pair = ((j * 256 + lax.broadcasted_iota(jnp.int32, (1, 256), 1)) // 2).astype(F32)
        angles = places * jnp.exp(pair * (-2.0 * math.log(10000.0) / D))
        sin_ref[:, lanes] = jnp.sin(angles)
        cos_ref[:, lanes] = jnp.cos(angles)

    each(0, 8, table_columns)

    for h in heads:
        arrive(tokens.at[x, h, k], r1.at[1, h], partner)
        arrive(w_all.at[:, x, h, k], r1.at[0, h], partner)
    second_copies = []
    for rx, rb in rows:
        there = at(rx, a, rb, c, y)
        j = 2 * rx + rb
        second_copies.append(push(tokens.at[x, :, k], tokens.at[x, :, k], s2.at[1, j], r2.at[1, j_me], there))
        second_copies.append(push(w_all.at[:, x, :, k], w_all.at[:, x, :, k], s2.at[0, j], r2.at[0, j_me], there))
    for copy in second_copies:
        copy.start()
        ends.append(copy.wait_send)

    def onward(rx, rb):
        j = 2 * rx + rb
        k2 = 2 * rb + c
        return [
            push(tokens.at[rx, :, k2], tokens.at[rx, :, k2], s3.at[1, j], r3.at[1, j], partner),
            push(w_all.at[:, rx, :, k2], w_all.at[:, rx, :, k2], s3.at[0, j], r3.at[0, j], partner),
        ]

    third_copies = onward(x, b)
    for copy in third_copies:
        copy.start()
        ends.append(copy.wait_send)

    odd = lax.broadcasted_iota(jnp.int32, (1, D), 1) % 2 == 1
    mid_sin, mid_cos = sin_ref[8:40], cos_ref[8:40]

    def start_of(n):
        s, co = sin_ref[pl.ds(n, 1)], cos_ref[pl.ds(n, 1)]
        return jnp.where(odd, co, s), jnp.where(odd, -s, co)

    def waves_of(n):
        s, co = start_of(n)
        rows_sin[...] = s * mid_cos + co * mid_sin
        rows_cos[...] = co * mid_cos - s * mid_sin

        def columns(j):
            lanes = pl.ds(pl.multiple_of(j * 128, 128), 128)
            low_sin, low_cos = sin_ref[40:56, lanes], cos_ref[40:56, lanes]
            for m in range(32):
                wave = rows_sin[m : m + 1, lanes] * low_cos + rows_cos[m : m + 1, lanes] * low_sin
                waves[pl.ds(pl.multiple_of(n * 512 + 16 * m, 16), 16), lanes] = wave.astype(BF)

        each(0, 16, columns)

    each(0, 4, waves_of)

    table_load.wait()
    square = table_ref[...].astype(F32)
    square = square * square
    high = square.astype(BF)
    lower = (square - high.astype(F32)).astype(BF)
    ones = jnp.ones((8, D), BF)
    across = (((1,), (1,)), ((), ()))
    norms = lax.dot_general(ones, high, across, preferred_element_type=F32) + lax.dot_general(
        ones, lower, across, preferred_element_type=F32
    )
    norms = norms[0:1]

    def products_of(n):
        run = pl.ds(pl.multiple_of(n * 512, 512), 512)
        products[run, :] = lax.dot_general(waves[run, :], table_ref[...], across, preferred_element_type=F32)

    each(0, 4, products_of)

    vocab = lax.broadcasted_iota(jnp.int32, (128, 256), 1).astype(F32)
    diagonal = lax.broadcasted_iota(jnp.int32, (128, 128), 0) == lax.broadcasted_iota(jnp.int32, (128, 128), 1)

    def scales_of(n):
        here = tokens[x, n, k].astype(F32)
        for q in range(4):
            column = jnp.sum(jnp.where(diagonal, here[q : q + 1, :], 0.0), axis=1, keepdims=True)
            chosen = column == vocab
            quarter = pl.ds(pl.multiple_of(n * 512 + 128 * q, 128), 128)
            one_hot[quarter, :] = chosen.astype(BF)
            total = jnp.sum(
                jnp.where(chosen, 2.0 * products[quarter, :] + norms, 0.0), axis=1, keepdims=True
            )
            total = jnp.maximum(total + D / 2, 0.0)
            inverse[quarter, :] = lax.rsqrt(total * (1.0 / D) + EPSILON)

    each(0, 4, scales_of)

    for rx, rb in rows:
        sx, sb = (2 * x + 4 - rx) % 4, rb
        j = 2 * sx + sb
        k2 = 2 * sb + c
        arrive(tokens.at[sx, :, k2], r2.at[1, j], partner)
        arrive(w_all.at[:, sx, :, k2], r2.at[0, j], partner)
        more = onward(sx, sb)
        for copy in more:
            copy.start()
            ends.append(copy.wait_send)
    for rx, rb in [(x, b)] + rows:
        j = 2 * rx + rb
        k3 = 2 * rb + 1 - c
        arrive(tokens.at[rx, :, k3], r3.at[1, j], partner)
        arrive(w_all.at[:, rx, :, k3], r3.at[0, j], partner)

    slot = lax.broadcasted_iota(jnp.int32, (64, 1), 0)
    target = offset + (slot // 16) * 256 + 16 * r + slot % 16
    lane = lax.broadcasted_iota(jnp.int32, (1, 128), 1)
    found = jnp.zeros((64, 128), F32)
    for q in range(3):
        bytes_here = tokens[3, 3, 1 + q].astype(F32)
        for t in range(4):
            hit = target == lane + (31232 + 512 * q + 128 * t)
            found = found + jnp.where(hit, bytes_here[t : t + 1, :], 0.0)
    column = jnp.sum(found, axis=1, keepdims=True)
    looked = jnp.dot((column == vocab[:64]).astype(BF), table_ref[...], preferred_element_type=F32)
    for t in range(4):
        s, co = start_of(4 + t)
        wave = s * cos_ref[40:56] + co * sin_ref[40:56]
        latent[16 * t : 16 * t + 16, :] = rms_rows(looked[16 * t : 16 * t + 16] + wave).astype(BF)
    weights_of = w_all.reshape(3, D, HD)
    q_own[...] = jnp.dot(latent[...], weights_of[0], preferred_element_type=F32).astype(BF)
    asked = Exchange(q_own, q_all, s_q, r_q, r, row_of, 16, whole=True)
    asked.start()
    ends.append(asked.wait_sent)

    wkv[:, :HD] = weights_of[1]
    wkv[:, HD:] = weights_of[2]
    table_w = jnp.dot(table_ref[...], wkv[...], preferred_element_type=F32)
    tw[0] = table_w.astype(BF)
    tw[1] = (table_w - table_w.astype(BF).astype(F32)).astype(BF)

    def keys_of(n):
        run = pl.ds(pl.multiple_of(n * 512, 512), 512)
        both = jnp.dot(waves[run, :], wkv[...], preferred_element_type=F32)
        both = both + jnp.dot(one_hot[run, :], tw[0], preferred_element_type=F32)
        both = both + jnp.dot(one_hot[run, :], tw[1], preferred_element_type=F32)
        both = (both * inverse[run, :]).astype(BF)
        keys[run, :] = both[:, :HD]
        values[run, :] = both[:, HD:]

    each(0, 4, keys_of)
    asked.wait_all()

    key_col = lax.broadcasted_iota(jnp.int32, (1, 2048), 1)
    key_place = 512 * (16 * x + 4 * (key_col // 512) + k) + key_col % 512
    outs = Exchange(o_msg, o_came, s_o, r_o, r, row_of, 16)
    stats = Exchange(st_msg, st_came, s_st, r_st, r, row_of, 16)
    diagonal64 = lax.broadcasted_iota(jnp.int32, (64, 128), 0) == lax.broadcasted_iota(jnp.int32, (64, 128), 1)

    def attend(step):
        t = (x + 1 + step) % 4
        query = q_all[pl.ds(4 * t, 4)].reshape(256, HD)
        scores = lax.dot_general(query, keys[...], across, preferred_element_type=F32) * SCALE
        row = lax.broadcasted_iota(jnp.int32, (256, 1), 0)
        row_place = offset + ((row // 16) % 4) * 256 + 16 * (4 * t + row // 64) + row % 16
        scores = jnp.where(key_place > row_place, MASKED, scores)
        peak = jnp.max(scores, axis=1, keepdims=True)
        weights = jnp.exp(scores - peak).astype(BF)
        total = jnp.sum(weights.astype(F32), axis=1, keepdims=True)
        out = jnp.dot(weights, values[...], preferred_element_type=F32).astype(BF)
        for g in range(4):
            some = slice(64 * g, 64 * g + 64)
            j = 4 * t + g
            o_msg[j] = out[some]
            st_msg[j, 0:1, :] = jnp.sum(jnp.where(diagonal64, peak[some], 0.0), axis=0, keepdims=True)
            st_msg[j, 1:2, :] = jnp.sum(jnp.where(diagonal64, total[some], 0.0), axis=0, keepdims=True)

            @pl.when(j != r)
            def _():
                stats.copy(j).start()
                outs.copy(j).start()

    each(0, 4, attend)
    o_came[r] = o_msg[r]
    st_came[r] = st_msg[r]
    stats.wait_all()
    outs.wait_all()
    ends += [stats.wait_sent, outs.wait_sent]

    halves = (w_in, w_out)
    others = [(x + d) % 4 for d in (1, 3, 2)]

    def along(h):
        copies = [push(halves[h].at[x], halves[h].at[x], sw2.at[h, i], rw2.at[h, x], at(i, a, b, c, y)) for i in others]
        return copies + [forward(h, x)]

    def forward(h, i):
        return push(halves[h].at[i], halves[h].at[i], sw3.at[h, i], rw3.at[h, i], partner)

    def set_out(h):
        @pl.when(source)
        def _():
            mine[h].wait()

        @pl.when(jnp.logical_and(main, jnp.logical_not(source)))
        def _():
            arrive(halves[h].at[x], rw1.at[h], partner)

        @pl.when(main)
        def _():
            for copy in along(h):
                copy.start()

    def hand_over(h):
        @pl.when(main)
        def _():
            for i in others:
                arrive(halves[h].at[i], rw2.at[h, i], partner)
                forward(h, i).start()

    def receive(h):
        @pl.when(jnp.logical_not(main))
        def _():
            for i in range(4):
                arrive(halves[h].at[i], rw3.at[h, i], partner)

    maxima, totals = st_came[:, 0, :], st_came[:, 1, :]
    factor = jnp.exp(maxima - jnp.max(maxima, axis=0, keepdims=True))
    factor = factor / jnp.sum(factor * totals, axis=0, keepdims=True)
    attended = jnp.zeros((64, HD), F32)
    for j in range(16):
        column = jnp.sum(jnp.where(diagonal64, factor[j : j + 1, :], 0.0), axis=1, keepdims=True)
        attended = attended + column * o_came[j].astype(F32)
    for copy in loads:
        copy.wait()

    def shares(rows, weight, out):
        for q in range(4):
            part = jnp.dot(rows, weight[:, 512 * q : 512 * q + 512], preferred_element_type=F32).astype(BF)
            for t in range(4):
                out[4 * t + q] = part[16 * t : 16 * t + 16]

    def rows_normed(blocks):
        for t in range(4):
            wide = jnp.concatenate([blocks[4 * t + q] for q in range(4)], axis=1).astype(F32)
            normed[16 * t : 16 * t + 16, :] = rms_rows(wide).astype(BF)

    shares(attended.astype(BF), w_co, msg)
    summed = Exchange(msg, came, s_m, r_m, p, head_of, 16)
    summed.start()

    @pl.when(source)
    def _():
        step1[0].start()

    own_block = (pl.ds(pl.multiple_of(16 * y, 16), 16), pl.ds(pl.multiple_of(512 * a, 512), 512))
    own_latent = latent[own_block].astype(F32)
    summed.wait_all()
    ends.append(summed.wait_sent)
    first = jnp.sum(came[...].astype(F32), axis=0) + own_latent
    own[...] = first.astype(BF)
    spread = Exchange(own, all_rows, s_a, r_a, p, head_of, 16, whole=True)
    spread.start()
    set_out(0)

    @pl.when(source)
    def _():
        step1[1].start()

    spread.wait_all()
    ends.append(spread.wait_sent)

    rows_normed(all_rows)
    kv[:, :HD] = jnp.dot(normed[...], w_qkv[1], preferred_element_type=F32).astype(BF)
    kv[:, HD:] = jnp.dot(normed[...], w_qkv[2], preferred_element_type=F32).astype(BF)
    both = Exchange(kv, kv_all, s_kv, r_kv, r, row_of, 16, whole=True)
    both.start()
    query = jnp.dot(normed[...], w_qkv[0], preferred_element_type=F32).astype(BF)
    both.wait_all()
    ends.append(both.wait_sent)

    all_keys = kv_all[:, :, :HD].reshape(LATENTS, HD)
    all_values = kv_all[:, :, HD:].reshape(LATENTS, HD)
    scores = lax.dot_general(query, all_keys, across, preferred_element_type=F32) * SCALE
    row = lax.broadcasted_iota(jnp.int32, (64, 1), 0)
    col = lax.broadcasted_iota(jnp.int32, (1, LATENTS), 1)
    row_place = (row // 16) * 256 + 16 * r + row % 16
    col_place = ((col // 16) % 4) * 256 + 16 * (col // 64) + col % 16
    scores = jnp.where(col_place > row_place, MASKED, scores)
    weights = jnp.exp(scores - jnp.max(scores, axis=1, keepdims=True)).astype(BF)
    total = jnp.sum(weights.astype(F32), axis=1, keepdims=True)
    attended = jnp.dot(weights, all_values, preferred_element_type=F32) / total
    shares(attended.astype(BF), w_so, msg2)
    summed2 = Exchange(msg2, came2, s_m2, r_m2, p, head_of, 16)
    summed2.start()
    hand_over(0)
    set_out(1)
    summed2.wait_all()
    ends.append(summed2.wait_sent)
    second = first + jnp.sum(came2[...].astype(F32), axis=0)
    own2[...] = second.astype(BF)
    spread2 = Exchange(own2, all_rows2, s_a2, r_a2, p, head_of, 16, whole=True)
    spread2.start()
    hand_over(1)

    spread2.wait_all()
    ends.append(spread2.wait_sent)

    rows_normed(all_rows2)
    receive(0)
    hidden = []
    for i in range(4):
        pre = jnp.dot(normed[...], w_in[i], preferred_element_type=F32)
        hidden.append(jax.nn.gelu(pre, approximate=True).astype(BF))
    hidden = jnp.concatenate(hidden, axis=1)
    receive(1)
    for q in range(4):
        columns = slice(512 * q, 512 * q + 512)
        partial[q] = jnp.dot(hidden, w_out[:, :, columns].reshape(512, 512), preferred_element_type=F32)
    here = pl.ds(pl.multiple_of(16 * y, 16), 16)
    partial[a, here, :] = partial[a, here, :] + second
    for j in range(16):
        some = slice(4 * j, 4 * j + 4)
        msg3[j] = jnp.concatenate([partial[q, some, :] for q in range(4)], axis=0).astype(BF)

    def last_copy(j):
        return push(msg3.at[j], came3.at[p], s_m3.at[j], r_m3.at[p], final_of(j))

    def last_start(i):
        j = (p + i) % 16

        @pl.when(j != final_self)
        def _():
            last_copy(j).start()

    each(0, 16, last_start)

    @pl.when(a == k)
    def _():
        came3[p] = msg3[4 * y + k]

    def last_wait(i):
        j = (p + i) % 16

        @pl.when(j != sender_self)
        def _():
            arrive(came3.at[j], r_m3.at[j], partner)

    each(0, 16, last_wait)
    ended = jnp.sum(came3[...].astype(F32), axis=0)
    for q in range(4):
        out_ref[:, 512 * q : 512 * q + 512] = ended[4 * q : 4 * q + 4]

    for end in ends:
        end()

    def last_sent(i):
        j = (p + i) % 16

        @pl.when(j != final_self)
        def _():
            last_copy(j).wait_send()

    each(0, 16, last_sent)

    @pl.when(source)
    def _():
        for copy in step1:
            copy.wait_send()

    @pl.when(main)
    def _():
        for h in range(2):
            for copy in along(h):
                copy.wait_send()
            for i in others:
                forward(h, i).wait_send()


def per_device(
    token_ids,
    latent_offset,
    embed_table,
    cross_q,
    cross_kv,
    cross_out,
    self_qkv,
    self_out,
    mlp_in,
    mlp_out,
):
    vmem = pl.BlockSpec(memory_space=pltpu.VMEM)
    hbm = pl.BlockSpec(memory_space=pl.ANY)
    dma = pltpu.SemaphoreType.DMA
    rows = pl.pallas_call(
        whole_kernel,
        out_shape=jax.ShapeDtypeStruct((4, D), F32),
        in_specs=[pl.BlockSpec(memory_space=pltpu.SMEM)] + [vmem] * 3 + [hbm] * 6,
        out_specs=vmem,
        scratch_shapes=[
            pltpu.VMEM((256, D), BF),
            pltpu.VMEM((4, 3, 32, HD), BF),
            pltpu.VMEM((3, 4, 4, 4, 32, HD), BF),
            pltpu.VMEM((4, 4, 4, 4, 128), jnp.int32),
            pltpu.VMEM((D, 2 * HD), BF),
            pltpu.VMEM((2, 256, 2 * HD), BF),
            pltpu.VMEM((56, D), F32),
            pltpu.VMEM((56, D), F32),
            pltpu.VMEM((32, D), F32),
            pltpu.VMEM((32, D), F32),
            pltpu.VMEM((2048, D), BF),
            pltpu.VMEM((2048, 256), F32),
            pltpu.VMEM((2048, 256), BF),
            pltpu.VMEM((2048, 1), F32),
            pltpu.VMEM((64, D), BF),
            pltpu.VMEM((2048, HD), BF),
            pltpu.VMEM((2048, HD), BF),
            pltpu.VMEM((64, HD), BF),
            pltpu.VMEM((16, 64, HD), BF),
            pltpu.VMEM((16, 64, HD), BF),
            pltpu.VMEM((16, 64, HD), BF),
            pltpu.VMEM((16, 8, 128), F32),
            pltpu.VMEM((16, 8, 128), F32),
            pltpu.VMEM((HD, D), BF),
            pltpu.VMEM((3, D, HD), BF),
            pltpu.VMEM((HD, D), BF),
            pltpu.VMEM((16, 16, 512), BF),
            pltpu.VMEM((16, 16, 512), BF),
            pltpu.VMEM((16, 512), BF),
            pltpu.VMEM((16, 16, 512), BF),
            pltpu.VMEM((64, D), BF),
            pltpu.VMEM((64, 2 * HD), BF),
            pltpu.VMEM((16, 64, 2 * HD), BF),
            pltpu.VMEM((16, 16, 512), BF),
            pltpu.VMEM((16, 16, 512), BF),
            pltpu.VMEM((16, 512), BF),
            pltpu.VMEM((16, 16, 512), BF),
            pltpu.VMEM((4, D, HD), BF),
            pltpu.VMEM((4, HD, D), BF),
            pltpu.VMEM((4, 64, 512), F32),
            pltpu.VMEM((16, 16, 512), BF),
            pltpu.VMEM((16, 16, 512), BF),
            dma((4,)),
            dma((2, 4)),
            dma((2, 4)),
            dma((2, 8)),
            dma((2, 8)),
            dma((2, 8)),
            dma((2, 8)),
        ]
        + [dma((16,))] * 18
        + [dma((2,)), dma((2,)), dma((2,)), dma((2, 4)), dma((2, 4)), dma((2, 4)), dma((2, 4))],
        compiler_params=pltpu.CompilerParams(
            collective_id=0, has_side_effects=True, vmem_limit_bytes=VLIMIT
        ),
    )(
        latent_offset, token_ids.reshape(4, 128), cross_q, cross_kv, embed_table, cross_out, self_qkv, self_out, mlp_in, mlp_out,
    )
    return rows.astype(BF)[None]


def solution(mesh):
    placed = (
        P("ctx"),
        P(),
        P(),
        P("ctx", "lat"),
        P(None, "ctx", "lat"),
        P("lat", None),
        P(None, None, "lat"),
        P("lat", None),
        P(None, "ctx"),
        P("ctx", None),
    )
    return jax.shard_map(
        per_device, mesh=mesh, in_specs=placed, out_specs=P("lat", "ctx", None), check_vma=False
    )
```
